256 devices in a mesh: face: 128 (over x, y_hi, z, core), sub: 2 (over y_lo).
Axes of the slice: x: 4, y: 4 (y_hi: 2, y_lo: 2; y = y_hi * 2 + y_lo), z: 8, core: 2. Of those that a mesh axis runs over, the one named last changes fastest.
Arguments:
- inputs: bfloat16 [128, 2, 64, 64, 128], P('face', 'sub'), may hold values from -6 to 6
- kernel_one: bfloat16 [3, 3, 128, 128], replicated, may hold values from -0.1875 to 0.1875
- kernel_two: bfloat16 [3, 3, 128, 128], replicated, may hold values from -0.1875 to 0.1875
- cotangent: bfloat16 [128, 2, 64, 64, 128], P('face', 'sub'), may hold values from -6 to 6
- edge_codes: int32 [128, 2, 4], replicated, may hold values from 0 to 7
- corner_codes: int32 [128, 2, 4], replicated, may hold values from 0 to 3
Outputs:
- outputs: bfloat16 [128, 2, 64, 64, 128], P('face', 'sub')
- grad_inputs: bfloat16 [128, 2, 64, 64, 128], P('face', 'sub')
- grad_kernel_one: float32 [3, 3, 128, 128], replicated
- grad_kernel_two: float32 [3, 3, 128, 128], replicated
The draws below stay inside these ranges and needn't reach their ends.
All inputs are finite; a program needn't handle non-finite values.
Results may differ from the reference program's by a relative error of at most 0.005.
Values may be sent and summed in bfloat16 or wider, within the bound.
No kernel may reach another device: no remote copies, remote signals or barrier semaphores. Data moves between devices by JAX's collectives and lax.ppermute only.
A program may use at most 128 MiB of HBM per device.

```python
import math
from functools import partial
import jax
import jax.numpy as jnp
from jax import lax

CHANNELS = 128
EDGE_CELLS = 64
PATCHES = 128
HALVES = 2
ROW_PATCHES = 16
TOTAL_CELLS = 1048576


def touch_ends(drawn, rng, least, largest):
    index_at = [jax.random.randint(jax.random.fold_in(rng, axis), (), 0, length) for axis, length in enumerate(drawn.shape)]
    widest = drawn.shape.index(max(drawn.shape))
    beside = index_at[:widest] + [(index_at[widest] + 1) % drawn.shape[widest]] + index_at[widest + 1:]
    return drawn.at[tuple(index_at)].set(least).at[tuple(beside)].set(largest)


def block_scale(key, dims, shards, smallest, high):
    level = 1.0
    for dim, blocks in shards:
        steps = jax.random.uniform(jax.random.fold_in(jax.random.fold_in(key, 6), dim), (blocks,), jnp.float32, smallest / len(shards), high / len(shards))
        level = level * jnp.repeat(jnp.exp(steps), dims[dim] // blocks).reshape((-1,) + (1,) * (len(dims) - 1 - dim))
    return level


def normal_values(key, dims, spread, limit, split=(), held_as=jnp.bfloat16):
    values = jax.random.normal(key, dims, jnp.float32) * spread
    if len(split) > 0:
        values = block_scale(key, dims, split, -0.22, 0.18) * values
    return jnp.clip(values, min=-limit, max=limit).astype(held_as)


def setup_inputs(seed: int = 0) -> dict:
    streams_of = jax.random.split(jax.random.key(seed), 7)
    inputs = normal_values(streams_of[0], (PATCHES, HALVES, EDGE_CELLS, EDGE_CELLS, CHANNELS), 1.0, 6.0, ((0, 128), (1, 2)))
    kernel_one = normal_values(streams_of[1], (3, 3, CHANNELS, CHANNELS), (9 * CHANNELS) ** -0.5, 0.1875)
    kernel_two = normal_values(streams_of[2], (3, 3, CHANNELS, CHANNELS), (9 * CHANNELS) ** -0.5, 0.1875)
    cotangent = normal_values(streams_of[3], (PATCHES, HALVES, EDGE_CELLS, EDGE_CELLS, CHANNELS), 1.0, 6.0, ((0, 128), (1, 2)))
    edge_codes = touch_ends(jax.random.randint(streams_of[4], (PATCHES, HALVES, 4), 0, 8), jax.random.fold_in(streams_of[4], 1), 0, 7).astype(jnp.int32)
    corner_codes = touch_ends(jax.random.randint(streams_of[5], (PATCHES, HALVES, 4), 0, 4), jax.random.fold_in(streams_of[5], 1), 0, 3).astype(jnp.int32)
    return dict(inputs=inputs, kernel_one=kernel_one, kernel_two=kernel_two, cotangent=cotangent, edge_codes=edge_codes, corner_codes=corner_codes)


def fill_halo(fields, edge_codes, corner_codes):
    device_count = fields.shape[0]
    side_len = fields.shape[1]
    row_width = HALVES * ROW_PATCHES
    own_index = jnp.arange(device_count, dtype=jnp.int32)
    edge_sets = jnp.stack([fields[:, 0], fields[:, :, -1], fields[:, -1], fields[:, :, 0]])
    corner_sets = jnp.stack([fields[:, 0, 0], fields[:, 0, -1], fields[:, -1, -1], fields[:, -1, 0]])
    edge_table = edge_codes.reshape(device_count, 4)
    corner_table = corner_codes.reshape(device_count, 4)
    edge_steps = [-row_width, 1, row_width, -1]
    corner_steps = [-row_width - 1, -row_width + 1, row_width + 1, row_width - 1]
    strips = []
    for direction in range(4):
        neighbour = (own_index + edge_steps[direction]) % device_count
        edge_code = edge_table[:, direction]
        picked = edge_sets[edge_code % 4, neighbour]
        picked = jnp.where((edge_code >= 4)[:, None, None], picked[:, ::-1], picked)
        strips.append(picked)
    corner_vals = []
    for corner in range(4):
        neighbour = (own_index + corner_steps[corner]) % device_count
        corner_vals.append(corner_sets[corner_table[:, corner], neighbour])
    padded = jnp.pad(fields, ((0, 0), (1, 1), (1, 1), (0, 0)))
    last = side_len + 1
    padded = padded.at[:, 0, 1:last].set(strips[0]).at[:, 1:last, last].set(strips[1])
    padded = padded.at[:, last, 1:last].set(strips[2]).at[:, 1:last, 0].set(strips[3])
    padded = padded.at[:, 0, 0].set(corner_vals[0]).at[:, 0, last].set(corner_vals[1])
    padded = padded.at[:, last, last].set(corner_vals[2]).at[:, last, 0].set(corner_vals[3])
    return padded

def conv_forward(padded, kernel):
    return lax.conv_general_dilated(padded, kernel, (1, 1), 'VALID', dimension_numbers=('NHWC', 'HWIO', 'NHWC'), preferred_element_type=jnp.float32)

def conv_inputs(upstream, kernel):
    widened = jnp.pad(upstream, ((0, 0), (2, 2), (2, 2), (0, 0)))
    turned = jnp.transpose(jnp.flip(kernel, (0, 1)), (0, 1, 3, 2))
    return lax.conv_general_dilated(widened, turned, (1, 1), 'VALID', dimension_numbers=('NHWC', 'HWIO', 'NHWC'), preferred_element_type=jnp.float32)

def conv_kernel(padded, upstream):
    side_len = upstream.shape[1]
    chans = upstream.shape[-1]
    flat_up = upstream.reshape(-1, chans)
    rows_out = []
    for row_off in range(3):
        cols_out = []
        for col_off in range(3):
            window = padded[:, row_off:row_off + side_len, col_off:col_off + side_len, :].reshape(-1, chans)
            cols_out.append(lax.dot_general(window, flat_up, (((0,), (0,)), ((), ())), preferred_element_type=jnp.float32))
        rows_out.append(jnp.stack(cols_out))
    return jnp.stack(rows_out)

def return_halo(grad_pad, edge_codes, corner_codes):
    zero_fields = jnp.zeros(grad_pad[:, 1:-1, 1:-1].shape, grad_pad.dtype)
    halo_only = partial(fill_halo, edge_codes=edge_codes, corner_codes=corner_codes)
    unused, pullback = jax.vjp(halo_only, zero_fields)
    return pullback(grad_pad)[0]

def reference(inputs, kernel_one, kernel_two, cotangent, edge_codes, corner_codes):
    device_count = PATCHES * HALVES
    fields = inputs.reshape(device_count, EDGE_CELLS, EDGE_CELLS, CHANNELS)
    upstream = cotangent.reshape(device_count, EDGE_CELLS, EDGE_CELLS, CHANNELS)
    padded_one = fill_halo(fields, edge_codes, corner_codes)
    preact = conv_forward(padded_one, kernel_one)
    hidden = jax.nn.silu(preact).astype(jnp.bfloat16)
    padded_two = fill_halo(hidden, edge_codes, corner_codes)
    outputs = conv_forward(padded_two, kernel_two).astype(jnp.bfloat16)
    grad_two = conv_kernel(padded_two, upstream)
    grad_hidden = return_halo(conv_inputs(upstream, kernel_two), edge_codes, corner_codes)
    sigmoid_vals = jax.nn.sigmoid(preact)
    grad_pre = (grad_hidden * sigmoid_vals * (1.0 + preact * (1.0 - sigmoid_vals))).astype(jnp.bfloat16)
    grad_one = conv_kernel(padded_one, grad_pre)
    grad_fields = return_halo(conv_inputs(grad_pre, kernel_one), edge_codes, corner_codes).astype(jnp.bfloat16)
    norm_factor = 1.0 / math.sqrt(TOTAL_CELLS)
    whole_shape = (PATCHES, HALVES, EDGE_CELLS, EDGE_CELLS, CHANNELS)
    return (outputs.reshape(whole_shape), grad_fields.reshape(whole_shape), grad_one * norm_factor, grad_two * norm_factor)
```

```python
import math

import jax
import jax.numpy as jnp
from jax import lax
from jax.experimental import pallas as pl
from jax.experimental.pallas import tpu as pltpu
from jax.sharding import PartitionSpec as P

AXES = ("face", "sub")
GRID_ROWS = 8
SIDE = 64
CH = 128
HALF = SIDE // 2
STRIPS = 2 * SIDE
VROWS = STRIPS + 32
BF16 = jnp.bfloat16
F32 = jnp.float32
N, E, S, W = 0, 1, 2, 3
NW, NE, SE, SW = 0, 1, 2, 3
VMEM = pl.BlockSpec(memory_space=pltpu.VMEM)
SMEM = pl.BlockSpec(memory_space=pltpu.SMEM)
PARAMS = pltpu.CompilerParams(vmem_limit_bytes=50 * 1024 * 1024)


def iota(shape, dim):
    return lax.broadcasted_iota(jnp.int32, shape, dim)


def side_strips(block, dst):
    dst[N] = block[0, 0].astype(F32)
    dst[S] = block[HALF - 1, 1].astype(F32)
    low = block[:, :, 0:16, :].reshape(SIDE, 16, CH).astype(F32)
    dst[W] = jnp.sum(jnp.where(iota(low.shape, 1) == 0, low, 0.0), axis=1)
    high = block[:, :, SIDE - 16 : SIDE, :].reshape(SIDE, 16, CH).astype(F32)
    dst[E] = jnp.sum(jnp.where(iota(high.shape, 1) == 15, high, 0.0), axis=1)


def corner_rows(strips):
    north = strips[N]
    south = strips[S]
    last = SIDE - 1
    return [north[0:1], north[last : last + 1], south[last : last + 1], south[0:1]]


def turned(strip, flip):
    row = iota((SIDE, SIDE), 0)
    col = iota((SIDE, SIDE), 1)
    target = jnp.where(flip, SIDE - 1 - row, row)
    matrix = jnp.where(col == target, 1.0, 0.0).astype(BF16)
    return jnp.dot(matrix, strip.astype(BF16), preferred_element_type=F32).astype(BF16)


def corner_block(code, own, other):
    picked = jnp.where(code == 0, own[0], jnp.where(code == 1, own[1], jnp.where(code == 2, own[2], own[3])))
    row = iota((16, CH), 0)
    return (jnp.where(row == 0, picked, 0.0) + jnp.where(row == 1, other, 0.0)).astype(BF16)


def pack(me, edge, corner, count, width, fore, back, vp, vm, hp, hm):
    fore_corners = corner_rows(fore)
    back_corners = corner_rows(back)

    def block(offset):
        return lax.rem(me + offset + 2 * count, count)

    def strips(dst, offset, read_side, own_side):
        code = edge[block(offset) * 4 + read_side]
        dst[0:SIDE] = turned(fore[lax.rem(code, 4)], code >= 4)
        dst[SIDE:STRIPS] = turned(back[own_side], edge[me * 4 + own_side] >= 4)

    def relayed(offset, read_corner, own_corner):
        return corner_block(
            corner[block(offset) * 4 + read_corner], fore_corners, back_corners[own_corner]
        )

    strips(vp, width, N, S)
    vp[STRIPS : STRIPS + 16] = relayed(width + 1, NW, SE)
    vp[STRIPS + 16 : VROWS] = relayed(width - 1, NE, SW)
    strips(vm, -width, S, N)
    vm[STRIPS : STRIPS + 16] = relayed(-width + 1, SW, NE)
    vm[STRIPS + 16 : VROWS] = relayed(-width - 1, SE, NW)
    strips(hp, 1, W, E)
    strips(hm, -1, E, W)


def put_row(dst, pair, part, row, west, east):
    col = iota((SIDE, CH), 0)
    wide = row.astype(F32)
    dst[1, pair, part] = row.astype(BF16)
    dst[0, pair, part] = jnp.where(col == 0, west, pltpu.roll(wide, 1, 0)).astype(BF16)
    dst[2, pair, part] = jnp.where(col == SIDE - 1, east, pltpu.roll(wide, SIDE - 1, 0)).astype(BF16)


def shift_copies(dst, src, west=None, east=None):
    def step(k, _):
        for part in range(2):
            i = 2 * k + part
            w = 0.0 if west is None else west[pl.ds(i, 1), :]
            e = 0.0 if east is None else east[pl.ds(i, 1), :]
            put_row(dst, k + part, 1 - part, src[k, part], w, e)
        return 0

    lax.fori_loop(0, HALF, step, 0, unroll=4)


def halo_copies(dst, src, west, east, vp, vm, hp, hm):
    west[...] = hp[0:SIDE].astype(F32)
    east[...] = hm[0:SIDE].astype(F32)
    shift_copies(dst, src, west, east)
    hp1 = hp[STRIPS : STRIPS + 16].astype(F32)
    hp2 = hp[STRIPS + 16 : VROWS].astype(F32)
    hm1 = hm[STRIPS : STRIPS + 16].astype(F32)
    hm2 = hm[STRIPS + 16 : VROWS].astype(F32)
    put_row(dst, 0, 0, vp[0:SIDE], hp1[0:1], hm1[0:1])
    put_row(dst, HALF, 1, vm[0:SIDE], hp2[0:1], hm2[0:1])


def zero_copies(dst, src):
    zero = jnp.zeros((SIDE, CH), BF16)
    for b in range(3):
        dst[b, 0, 0] = zero
        dst[b, HALF, 1] = zero
    shift_copies(dst, src)


def window(copies, m, mb):
    parts = [
        copies[b, pl.ds(m + a // 2, mb), a % 2].reshape(mb * SIDE, CH)
        for a in range(4)
        for b in range(3)
    ]
    return jnp.concatenate(parts, axis=1)


def conv_pairs(copies, weights, m, mb):
    return jnp.dot(window(copies, m, mb), weights[...], preferred_element_type=F32)


def edge_tap(side, k):
    return {N: (0, k), S: (2, k), W: (k, 0), E: (k, 2)}[side]


CORNER_TAP = {NW: (0, 0), NE: (0, 2), SE: (2, 2), SW: (2, 0)}


def tap_transposed(turned_weights, a, b):
    at = ((2 - a) * 3 + 2 - b) * CH
    return turned_weights[at : at + CH, 0:CH]


def returned(me, edge, corner, count, width, turned_weights, vp, vm, hp, hm, adds, pieces=None, corners=None):
    def block(offset):
        return lax.rem(me + offset + 2 * count, count)

    adds[...] = jnp.zeros_like(adds)
    row = iota((SIDE, CH), 0)
    for side, offset, message in ((N, width, vm), (E, -1, hp), (S, -width, vp), (W, 1, hm)):
        code = edge[block(offset) * 4 + side]
        flip = code >= 4
        strip = message[SIDE:STRIPS].astype(F32)
        up = jnp.where(row == SIDE - 1, 0.0, pltpu.roll(strip, SIDE - 1, 0))
        down = jnp.where(row == 0, 0.0, pltpu.roll(strip, 1, 0))
        joined = jnp.concatenate(
            [jnp.where(flip, down, up), strip, jnp.where(flip, up, down)], axis=1
        ).astype(BF16)
        if pieces is not None:
            pieces[side] = joined
        taps = jnp.concatenate(
            [tap_transposed(turned_weights, *edge_tap(side, k)) for k in range(3)], axis=0
        )
        at = lax.rem(code, 4)
        adds[at] = adds[at] + jnp.dot(joined, taps, preferred_element_type=F32)
    for q, offset, message, start in (
        (NW, width + 1, hm, STRIPS + 16),
        (NE, width - 1, hp, STRIPS + 16),
        (SE, -width - 1, hp, STRIPS),
        (SW, -width + 1, hm, STRIPS),
    ):
        code = corner[block(offset) * 4 + q]
        cells = message[start : start + 16]
        if corners is not None:
            corners[q] = cells
        given = jnp.dot(
            cells, tap_transposed(turned_weights, *CORNER_TAP[q]), preferred_element_type=F32
        )[1:2]
        first = jnp.where(row == 0, given, 0.0)
        last = jnp.where(row == SIDE - 1, given, 0.0)
        adds[N] = adds[N] + jnp.where(code == NW, first, 0.0) + jnp.where(code == NE, last, 0.0)
        adds[S] = adds[S] + jnp.where(code == SW, first, 0.0) + jnp.where(code == SE, last, 0.0)


def with_adds(rows, i, adds, at_first, at_last):
    col = iota((SIDE, CH), 0)
    rows = rows + jnp.where(col == SIDE - 1, adds[E, pl.ds(i, 1), :], 0.0)
    rows = rows + jnp.where(col == 0, adds[W, pl.ds(i, 1), :], 0.0)
    if at_first is not None:
        rows = rows + jnp.where(at_first, adds[N], 0.0)
    if at_last is not None:
        rows = rows + jnp.where(at_last, adds[S], 0.0)
    return rows


def pack_kernel(count, width, me, edge, corner, fields, upstream, vp, vm, hp, hm, fore, back):
    side_strips(fields, fore)
    side_strips(upstream, back)
    pack(me[0], edge, corner, count, width, fore, back, vp, vm, hp, hm)


def prepare_kernel(kernel_one, kernel_two, upstream, fwd_one, fwd_two, in_one, in_two, up_copies):
    zero = jnp.zeros((CH, CH), BF16)
    for source, plain, back in ((kernel_one, fwd_one, in_one), (kernel_two, fwd_two, in_two)):
        for b in range(3):
            for a in range(4):
                at = (a * 3 + b) * CH
                if a < 3:
                    block = source[a, b]
                    plain[at : at + CH, 0:CH] = block
                    plain[at + 3 * CH : at + 4 * CH, CH : 2 * CH] = block
                    swapped = source[2 - a, 2 - b].astype(F32).T.astype(BF16)
                    back[at : at + CH, 0:CH] = swapped
                    back[at + 3 * CH : at + 4 * CH, CH : 2 * CH] = swapped
                else:
                    plain[at : at + CH, 0:CH] = zero
                    back[at : at + CH, 0:CH] = zero
            plain[b * CH : (b + 1) * CH, CH : 2 * CH] = zero
            back[b * CH : (b + 1) * CH, CH : 2 * CH] = zero
    zero_copies(up_copies, upstream)


def middle_kernel(
    count, width, scale, me, edge, corner, fields, vp, vm, hp, hm, fwd_one, in_two, up_copies,
    hidden, grad_pre, vp2, vm2, hp2, hm2, sums,
    copies, west, east, adds, pieces, corners, fore, back, acc,
):
    where_am_i = me[0]
    returned(where_am_i, edge, corner, count, width, in_two, vp, vm, hp, hm, adds, pieces, corners)
    halo_copies(copies, fields, west, east, vp, vm, hp, hm)
    mb = 4
    steps = HALF // mb

    def step(n, _):
        m = n * mb
        pre = conv_pairs(copies, fwd_one, m, mb)
        grad = conv_pairs(up_copies, in_two, m, mb)
        for k in range(mb):
            for part in range(2):
                rows = slice(k * SIDE, (k + 1) * SIDE)
                lanes = slice(part * CH, (part + 1) * CH)
                p = pre[rows, lanes]
                g = with_adds(
                    grad[rows, lanes], 2 * (m + k) + part, adds,
                    n == 0 if k == 0 and part == 0 else None,
                    n == steps - 1 if k == mb - 1 and part == 1 else None,
                )
                s = 1.0 / (1.0 + jnp.exp(-p))
                hidden[m + k, part] = (p * s).astype(BF16)
                grad_pre[m + k, part] = (g * s * (1.0 + p * (1.0 - s))).astype(BF16)
        return 0

    lax.fori_loop(0, steps, step, 0)
    side_strips(hidden, fore)
    side_strips(grad_pre, back)
    pack(where_am_i, edge, corner, count, width, fore, back, vp2, vm2, hp2, hm2)

    gb = 8
    first = (((0,), (0,)), ((), ()))

    def gather(values, shifted):
        def grad_step(n, _):
            m = n * gb
            left = jnp.concatenate(
                [values[pl.ds(m, gb), part].reshape(gb * SIDE, CH) for part in range(2)], axis=1
            )
            acc[...] += lax.dot_general(left, window(shifted, m, gb), first, preferred_element_type=F32)
            return 0

        acc[...] = jnp.zeros_like(acc)
        lax.fori_loop(0, HALF // gb, grad_step, 0)

    def from_acc(a, b):
        low = (a * 3 + b) * CH
        high = low + 3 * CH
        return acc[0:CH, low : low + CH] + acc[CH : 2 * CH, high : high + CH]

    gather(grad_pre, copies)
    for a in range(3):
        for b in range(3):
            at = (a * 3 + b) * CH
            sums[at : at + CH] = from_acc(a, b).T * scale
    gather(hidden, up_copies)
    for a in range(3):
        for b in range(3):
            at = (9 + a * 3 + b) * CH
            sums[at : at + CH] = from_acc(2 - a, 2 - b) * scale

    def block(offset):
        return lax.rem(where_am_i + offset + 2 * count, count)

    for side, offset in ((N, width), (E, -1), (S, -width), (W, 1)):
        code = lax.rem(edge[block(offset) * 4 + side], 4)
        term = lax.dot_general(fore[code].astype(BF16), pieces[side], first, preferred_element_type=F32)
        for k in range(3):
            a, b = edge_tap(side, k)
            at = (9 + a * 3 + b) * CH
            sums[at : at + CH] = sums[at : at + CH] + term[:, k * CH : (k + 1) * CH] * scale
    own = corner_rows(fore)
    row = iota((16, CH), 0)
    for q, offset in ((NW, width + 1), (NE, width - 1), (SE, -width - 1), (SW, -width + 1)):
        code = corner[block(offset) * 4 + q]
        cell = jnp.where(code == 0, own[0], jnp.where(code == 1, own[1], jnp.where(code == 2, own[2], own[3])))
        left = jnp.where(row == 1, cell, 0.0).astype(BF16)
        a, b = CORNER_TAP[q]
        at = (9 + a * 3 + b) * CH
        term = lax.dot_general(left, corners[q], first, preferred_element_type=F32)
        sums[at : at + CH] = sums[at : at + CH] + term * scale


def last_kernel(
    count, width, me, edge, corner, hidden, grad_pre, vp, vm, hp, hm, fwd_two, in_one,
    outputs, grad_fields, copies, west, east, adds,
):
    mb = 4
    steps = HALF // mb
    halo_copies(copies, hidden, west, east, vp, vm, hp, hm)

    def out_step(n, _):
        m = n * mb
        got = conv_pairs(copies, fwd_two, m, mb)
        for part in range(2):
            lanes = slice(part * CH, (part + 1) * CH)
            outputs[pl.ds(m, mb), part] = got[:, lanes].reshape(mb, SIDE, CH).astype(BF16)
        return 0

    lax.fori_loop(0, steps, out_step, 0)
    returned(me[0], edge, corner, count, width, in_one, vp, vm, hp, hm, adds)
    zero_copies(copies, grad_pre)

    def grad_step(n, _):
        m = n * mb
        got = conv_pairs(copies, in_one, m, mb)
        for k in range(mb):
            for part in range(2):
                g = with_adds(
                    got[k * SIDE : (k + 1) * SIDE, part * CH : (part + 1) * CH],
                    2 * (m + k) + part, adds,
                    n == 0 if k == 0 and part == 0 else None,
                    n == steps - 1 if k == mb - 1 and part == 1 else None,
                )
                grad_fields[m + k, part] = g.astype(BF16)
        return 0

    lax.fori_loop(0, steps, grad_step, 0)


def struct(shape, dtype=BF16):
    return jax.ShapeDtypeStruct(shape, dtype)


BLOCK = (HALF, 2, SIDE, CH)
COPIES = (3, HALF + 1, 2, SIDE, CH)
WEIGHTS = (12 * CH, 2 * CH)


def call(body, tables, arrays, outs, scratch, flops=0, moved=4 << 20):
    return pl.pallas_call(
        body,
        out_shape=outs,
        in_specs=[SMEM] * tables + [VMEM] * arrays,
        out_specs=tuple(VMEM for _ in outs),
        scratch_shapes=scratch,
        compiler_params=PARAMS,
        cost_estimate=pl.CostEstimate(flops=flops, bytes_accessed=moved, transcendentals=0),
    )


def shifted(x, by):
    size = lax.axis_size(AXES)
    return lax.ppermute(x, AXES, [(i, (i + by) % size) for i in range(size)])


def swap(x, bit):
    size = lax.axis_size(AXES)
    return lax.ppermute(x, AXES, [(i, i ^ bit) for i in range(size)])


def exchange(vp, vm, hp, hm, width):
    vp = shifted(vp, width)
    vm = shifted(vm, -width)
    hp = jnp.concatenate([hp, vp[STRIPS : STRIPS + 16], vm[STRIPS : STRIPS + 16]])
    hm = jnp.concatenate([hm, vp[STRIPS + 16 : VROWS], vm[STRIPS + 16 : VROWS]])
    return vp, vm, shifted(hp, 1), shifted(hm, -1)


HALVED = (2, 1, 4, 64)
WHOLE = (32, 128, 8, 16)


def total(x):
    me = lax.axis_index(AXES)
    rows = x.shape[0]
    for bit in HALVED:
        rows //= 2
        high = (me // bit) % 2
        send = lax.dynamic_slice_in_dim(x, (1 - high) * rows, rows, 0)
        keep = lax.dynamic_slice_in_dim(x, high * rows, rows, 0)
        x = keep + swap(send, bit)
    for bit in WHOLE:
        x = x + swap(x, bit)
    for bit in reversed(HALVED):
        high = (me // bit) % 2
        other = swap(x, bit)
        x = jnp.where(high == 1, jnp.concatenate([other, x]), jnp.concatenate([x, other]))
    return x


def local(inputs, kernel_one, kernel_two, cotangent, edge_codes, corner_codes):
    count = lax.axis_size(AXES)
    width = lax.axis_size("face") // GRID_ROWS * lax.axis_size("sub")
    scale = 1.0 / math.sqrt(count * SIDE * SIDE)
    me = lax.axis_index(AXES).astype(jnp.int32).reshape(1)
    edge = edge_codes.reshape(-1)
    corner = corner_codes.reshape(-1)
    tables = (me, edge, corner)
    fields = inputs.reshape(BLOCK)
    upstream = cotangent.reshape(BLOCK)
    message = struct((VROWS, CH))
    own = struct((STRIPS, CH))
    strips = pltpu.VMEM((4, SIDE, CH), F32)
    column = pltpu.VMEM((SIDE, CH), F32)
    conv_flops = 2 * SIDE * SIDE * 9 * CH * CH

    sent = call(
        lambda *refs: pack_kernel(count, width, *refs), 3, 2, (message, message, own, own), [strips, strips],
    )(*tables, fields, upstream)
    weights = struct(WEIGHTS)
    fwd_one, fwd_two, in_one, in_two, up_copies = call(
        prepare_kernel, 0, 3, (weights, weights, weights, weights, struct(COPIES)), [], conv_flops,
    )(kernel_one, kernel_two, upstream)
    arrived = exchange(*sent, width)
    hidden, grad_pre, vp2, vm2, hp2, hm2, sums = call(
        lambda *refs: middle_kernel(count, width, scale, *refs), 3, 8,
        (struct(BLOCK), struct(BLOCK), message, message, own, own, struct((18 * CH, CH), F32)),
        [
            pltpu.VMEM(COPIES, BF16), column, column, strips,
            pltpu.VMEM((4, SIDE, 3 * CH), BF16), pltpu.VMEM((4, 16, CH), BF16), strips, strips,
            pltpu.VMEM((2 * CH, 12 * CH), F32),
        ],
        4 * conv_flops,
    )(*tables, fields, *arrived, fwd_one, in_two, up_copies)
    arrived = exchange(vp2, vm2, hp2, hm2, width)
    outputs, grad_fields = call(
        lambda *refs: last_kernel(count, width, *refs), 3, 8, (struct(BLOCK), struct(BLOCK)),
        [pltpu.VMEM(COPIES, BF16), column, column, strips],
        2 * conv_flops,
    )(*tables, hidden, grad_pre, *arrived, fwd_two, in_one)
    sums = total(sums)
    shape = (1, 1, SIDE, SIDE, CH)
    grads = sums.reshape(2, 3, 3, CH, CH)
    return outputs.reshape(shape), grad_fields.reshape(shape), grads[0], grads[1]


def solution(mesh):
    block = P("face", "sub", None, None, None)
    return jax.shard_map(
        local,
        mesh=mesh,
        in_specs=(block, P(), P(), block, P(), P()),
        out_specs=(block, block, P(), P()),
        check_vma=False,
    )
```

```python
import math

import jax
import jax.numpy as jnp
from jax import lax
from jax.experimental import pallas as pl
from jax.experimental.pallas import tpu as pltpu
from jax.sharding import PartitionSpec as P

AXES = ("face", "sub")
GRID_ROWS = 8
SIDE = 64
CH = 128
HALF = SIDE // 2
STRIPS = 2 * SIDE
VROWS = STRIPS + 32
BF16 = jnp.bfloat16
F32 = jnp.float32
N, E, S, W = 0, 1, 2, 3
NW, NE, SE, SW = 0, 1, 2, 3
VMEM = pl.BlockSpec(memory_space=pltpu.VMEM)
SMEM = pl.BlockSpec(memory_space=pltpu.SMEM)
HBM = pl.BlockSpec(memory_space=pltpu.HBM)
PARAMS = pltpu.CompilerParams(vmem_limit_bytes=24 * 1024 * 1024)


def code_at(table, block, which):
    return table[block // 2, block % 2, which]


def iota(shape, dim):
    return lax.broadcasted_iota(jnp.int32, shape, dim)


def strips_from(north, south, low, high, dst):
    dst[N] = north.astype(F32)
    dst[S] = south.astype(F32)
    low = low.reshape(SIDE, 16, CH).astype(F32)
    dst[W] = jnp.sum(jnp.where(iota(low.shape, 1) == 0, low, 0.0), axis=1)
    high = high.reshape(SIDE, 16, CH).astype(F32)
    dst[E] = jnp.sum(jnp.where(iota(high.shape, 1) == 15, high, 0.0), axis=1)


def side_strips(block, dst):
    strips_from(
        block[0, 0], block[HALF - 1, 1], block[:, :, 0:16, :], block[:, :, SIDE - 16 : SIDE, :], dst
    )


def corner_rows(strips):
    north = strips[N]
    south = strips[S]
    last = SIDE - 1
    return [north[0:1], north[last : last + 1], south[last : last + 1], south[0:1]]


def turned(strip, flip):
    row = iota((SIDE, SIDE), 0)
    col = iota((SIDE, SIDE), 1)
    target = jnp.where(flip, SIDE - 1 - row, row)
    matrix = jnp.where(col == target, 1.0, 0.0).astype(BF16)
    return jnp.dot(matrix, strip.astype(BF16), preferred_element_type=F32).astype(BF16)


def corner_block(code, own, other):
    picked = jnp.where(code == 0, own[0], jnp.where(code == 1, own[1], jnp.where(code == 2, own[2], own[3])))
    row = iota((16, CH), 0)
    return (jnp.where(row == 0, picked, 0.0) + jnp.where(row == 1, other, 0.0)).astype(BF16)


def pack(me, edge, corner, count, width, fore, back, vp, vm, hp, hm):
    fore_corners = corner_rows(fore)
    back_corners = corner_rows(back)

    def block(offset):
        return lax.rem(me + offset + 2 * count, count)

    def strips(dst, offset, read_side, own_side):
        code = code_at(edge, block(offset), read_side)
        dst[0:SIDE] = turned(fore[lax.rem(code, 4)], code >= 4)
        dst[SIDE:STRIPS] = turned(back[own_side], code_at(edge, me, own_side) >= 4)

    def relayed(offset, read_corner, own_corner):
        return corner_block(
            code_at(corner, block(offset), read_corner), fore_corners, back_corners[own_corner]
        )

    strips(vp, width, N, S)
    vp[STRIPS : STRIPS + 16] = relayed(width + 1, NW, SE)
    vp[STRIPS + 16 : VROWS] = relayed(width - 1, NE, SW)
    strips(vm, -width, S, N)
    vm[STRIPS : STRIPS + 16] = relayed(-width + 1, SW, NE)
    vm[STRIPS + 16 : VROWS] = relayed(-width - 1, SE, NW)
    strips(hp, 1, W, E)
    strips(hm, -1, E, W)


def put_row(dst, pair, part, row, west, east):
    col = iota((SIDE, CH), 0)
    wide = row.astype(F32)
    dst[1, pair, part] = row.astype(BF16)
    dst[0, pair, part] = jnp.where(col == 0, west, pltpu.roll(wide, 1, 0)).astype(BF16)
    dst[2, pair, part] = jnp.where(col == SIDE - 1, east, pltpu.roll(wide, SIDE - 1, 0)).astype(BF16)


def shift_copies(dst, src, west=None, east=None):
    def step(k, _):
        for part in range(2):
            i = 2 * k + part
            w = 0.0 if west is None else west[pl.ds(i, 1), :]
            e = 0.0 if east is None else east[pl.ds(i, 1), :]
            put_row(dst, k + part, 1 - part, src[k, part], w, e)
        return 0

    lax.fori_loop(0, HALF, step, 0, unroll=4)


def halo_copies(dst, src, west, east, vp, vm, hp, hm):
    west[...] = hp[0:SIDE].astype(F32)
    east[...] = hm[0:SIDE].astype(F32)
    shift_copies(dst, src, west, east)
    hp1 = hp[STRIPS : STRIPS + 16].astype(F32)
    hp2 = hp[STRIPS + 16 : VROWS].astype(F32)
    hm1 = hm[STRIPS : STRIPS + 16].astype(F32)
    hm2 = hm[STRIPS + 16 : VROWS].astype(F32)
    put_row(dst, 0, 0, vp[0:SIDE], hp1[0:1], hm1[0:1])
    put_row(dst, HALF, 1, vm[0:SIDE], hp2[0:1], hm2[0:1])


def zero_copies(dst, src):
    zero = jnp.zeros((SIDE, CH), BF16)
    for b in range(3):
        dst[b, 0, 0] = zero
        dst[b, HALF, 1] = zero
    shift_copies(dst, src)


def window(copies, m, mb):
    parts = [
        copies[b, pl.ds(m + a // 2, mb), a % 2].reshape(mb * SIDE, CH)
        for a in range(4)
        for b in range(3)
    ]
    return jnp.concatenate(parts, axis=1)


def conv_pairs(copies, weights, m, mb):
    return jnp.dot(window(copies, m, mb), weights[...], preferred_element_type=F32)


def edge_tap(side, k):
    return {N: (0, k), S: (2, k), W: (k, 0), E: (k, 2)}[side]


CORNER_TAP = {NW: (0, 0), NE: (0, 2), SE: (2, 2), SW: (2, 0)}


def neighbours(strip):
    row = iota((SIDE, CH), 0)
    up = jnp.where(row == SIDE - 1, 0.0, pltpu.roll(strip, SIDE - 1, 0))
    down = jnp.where(row == 0, 0.0, pltpu.roll(strip, 1, 0))
    return up, down


def tap_plain(weights, a, b):
    at = (a * 3 + b) * CH
    return weights[at : at + CH, 0:CH]


def tap_transposed(turned_weights, a, b):
    at = ((2 - a) * 3 + 2 - b) * CH
    return turned_weights[at : at + CH, 0:CH]


def returned(me, edge, corner, count, width, turned_weights, vp, vm, hp, hm, adds, pieces=None, corners=None):
    def block(offset):
        return lax.rem(me + offset + 2 * count, count)

    adds[...] = jnp.zeros_like(adds)
    row = iota((SIDE, CH), 0)
    for side, offset, message in ((N, width, vm), (E, -1, hp), (S, -width, vp), (W, 1, hm)):
        code = code_at(edge, block(offset), side)
        flip = code >= 4
        strip = message[SIDE:STRIPS].astype(F32)
        up, down = neighbours(strip)
        joined = jnp.concatenate(
            [jnp.where(flip, down, up), strip, jnp.where(flip, up, down)], axis=1
        ).astype(BF16)
        if pieces is not None:
            pieces[side] = joined
        taps = jnp.concatenate(
            [tap_transposed(turned_weights, *edge_tap(side, k)) for k in range(3)], axis=0
        )
        at = lax.rem(code, 4)
        adds[at] = adds[at] + jnp.dot(joined, taps, preferred_element_type=F32)
    for q, offset, message, start in (
        (NW, width + 1, hm, STRIPS + 16),
        (NE, width - 1, hp, STRIPS + 16),
        (SE, -width - 1, hp, STRIPS),
        (SW, -width + 1, hm, STRIPS),
    ):
        code = code_at(corner, block(offset), q)
        cells = message[start : start + 16]
        if corners is not None:
            corners[q] = cells
        given = jnp.dot(
            cells, tap_transposed(turned_weights, *CORNER_TAP[q]), preferred_element_type=F32
        )[1:2]
        first = jnp.where(row == 0, given, 0.0)
        last = jnp.where(row == SIDE - 1, given, 0.0)
        adds[N] = adds[N] + jnp.where(code == NW, first, 0.0) + jnp.where(code == NE, last, 0.0)
        adds[S] = adds[S] + jnp.where(code == SW, first, 0.0) + jnp.where(code == SE, last, 0.0)


def with_adds(rows, i, adds, first=False, last=False):
    col = iota((8, CH), 0)
    rows = jnp.concatenate(
        [
            rows[0:8] + jnp.where(col == 0, adds[W, pl.ds(i, 1), :], 0.0),
            rows[8 : SIDE - 8],
            rows[SIDE - 8 :] + jnp.where(col == 7, adds[E, pl.ds(i, 1), :], 0.0),
        ],
        axis=0,
    )
    if first:
        rows = rows + adds[N]
    if last:
        rows = rows + adds[S]
    return rows


def pad_sides(vp, vm, hp, hm):
    return ((N, vp), (S, vm), (W, hp), (E, hm))


def pad_corners(hp, hm):
    return ((NW, hp, STRIPS), (NE, hm, STRIPS), (SE, hm, STRIPS + 16), (SW, hp, STRIPS + 16))


def received(weights, vp, vm, hp, hm, adds):
    row = iota((SIDE, CH), 0)
    for side, message in pad_sides(vp, vm, hp, hm):
        strip = message[0:SIDE].astype(F32)
        up, down = neighbours(strip)
        joined = jnp.concatenate([down, strip, up], axis=1).astype(BF16)
        taps = jnp.concatenate([tap_plain(weights, *edge_tap(side, k)) for k in range(3)], axis=0)
        adds[side] = jnp.dot(joined, taps, preferred_element_type=F32)
    for q, message, start in pad_corners(hp, hm):
        cells = message[start : start + 16]
        given = jnp.dot(cells, tap_plain(weights, *CORNER_TAP[q]), preferred_element_type=F32)[0:1]
        side = N if q in (NW, NE) else S
        place = 0 if q in (NW, SW) else SIDE - 1
        adds[side] = adds[side] + jnp.where(row == place, given, 0.0)


def pack_kernel(
    count, width, me, edge, corner, fields, upstream, vp, vm, hp, hm, fore, back, rows, columns, sems
):
    copies = []
    for k, source in enumerate((fields, upstream)):
        for j, (part, dst) in enumerate((
            (source.at[0, 0], rows.at[k, 0]),
            (source.at[HALF - 1, 1], rows.at[k, 1]),
            (source.at[:, :, pl.ds(0, 16), :], columns.at[k, 0]),
            (source.at[:, :, pl.ds(SIDE - 16, 16), :], columns.at[k, 1]),
        )):
            copies.append(pltpu.make_async_copy(part, dst, sems.at[k, j]))
    for copy in copies:
        copy.start()
    for copy in copies:
        copy.wait()
    for k, dst in enumerate((fore, back)):
        strips_from(rows[k, 0], rows[k, 1], columns[k, 0], columns[k, 1], dst)
    pack(me[0], edge, corner, count, width, fore, back, vp, vm, hp, hm)


def plain_weights(source, dst):
    zero = jnp.zeros((CH, CH), BF16)
    for b in range(3):
        for a in range(3):
            at = (a * 3 + b) * CH
            dst[at : at + CH, 0:CH] = source[a, b]
            dst[at + 3 * CH : at + 4 * CH, CH : 2 * CH] = source[a, b]
        dst[(9 + b) * CH : (10 + b) * CH, 0:CH] = zero
        dst[b * CH : (b + 1) * CH, CH : 2 * CH] = zero


def turned_weights(source, dst):
    zero = jnp.zeros((CH, CH), BF16)
    for b in range(3):
        for a in range(3):
            at = (a * 3 + b) * CH
            swapped = source[2 - a, 2 - b].astype(F32).T.astype(BF16)
            dst[at : at + CH, 0:CH] = swapped
            dst[at + 3 * CH : at + 4 * CH, CH : 2 * CH] = swapped
        dst[(9 + b) * CH : (10 + b) * CH, 0:CH] = zero
        dst[b * CH : (b + 1) * CH, CH : 2 * CH] = zero


def conv_all(copies, weights, dst):
    mb = 4

    def step(n, _):
        m = n * mb
        got = conv_pairs(copies, weights, m, mb)
        for part in range(2):
            lanes = slice(part * CH, (part + 1) * CH)
            dst[pl.ds(m, mb), part] = got[:, lanes].reshape(mb, SIDE, CH).astype(dst.dtype)
        return 0

    lax.fori_loop(0, HALF // mb, step, 0)


def back_kernel(kernel_two, upstream, in_two, up_copies, grad):
    turned_weights(kernel_two, in_two)
    zero_copies(up_copies, upstream)
    conv_all(up_copies, in_two, grad)


def fore_kernel(kernel_one, fields, fwd_one, copies, pre):
    plain_weights(kernel_one, fwd_one)
    zero_copies(copies, fields)
    conv_all(copies, fwd_one, pre)


def middle_kernel(
    count, width, me, edge, corner, vp, vm, hp, hm, fwd_one, in_two, pre, grad,
    hidden, grad_pre, vp2, vm2, hp2, hm2, fore, back, pieces, corners, grad_adds, pre_adds,
):
    returned(me[0], edge, corner, count, width, in_two, vp, vm, hp, hm, grad_adds, pieces, corners)
    received(fwd_one, vp, vm, hp, hm, pre_adds)

    def one(m, part, first=False, last=False):
        i = 2 * m + part
        p = with_adds(pre[m, part], i, pre_adds, first, last)
        g = with_adds(grad[m, part], i, grad_adds, first, last)
        s = 1.0 / (1.0 + jnp.exp(-p))
        hidden[m, part] = (p * s).astype(BF16)
        grad_pre[m, part] = (g * s * (1.0 + p * (1.0 - s))).astype(BF16)

    def step(m, _):
        one(m, 0)
        one(m, 1)
        return 0

    one(0, 0, first=True)
    one(0, 1)
    lax.fori_loop(1, HALF - 1, step, 0, unroll=2)
    one(HALF - 1, 0)
    one(HALF - 1, 1, last=True)
    side_strips(hidden, fore)
    side_strips(grad_pre, back)
    pack(me[0], edge, corner, count, width, fore, back, vp2, vm2, hp2, hm2)


def sums_kernel(
    count, width, scale, me, edge, corner, vp, vm, hp, hm, hidden, grad_pre, field_copies, up_copies,
    fore, back, pieces, corners, keep, send, acc, sums,
):
    gb = 8
    first = (((0,), (0,)), ((), ()))

    def gather(values, shifted):
        def grad_step(n, _):
            m = n * gb
            left = jnp.concatenate(
                [values[pl.ds(m, gb), part].reshape(gb * SIDE, CH) for part in range(2)], axis=1
            )
            acc[...] += lax.dot_general(left, window(shifted, m, gb), first, preferred_element_type=F32)
            return 0

        acc[...] = jnp.zeros_like(acc)
        lax.fori_loop(0, HALF // gb, grad_step, 0)

    def from_acc(a, b):
        low = (a * 3 + b) * CH
        high = low + 3 * CH
        return acc[0:CH, low : low + CH] + acc[CH : 2 * CH, high : high + CH]

    def add(half, tap, term):
        at = (tap[0] * 3 + tap[1]) * CH
        sums[half, at : at + CH] = sums[half, at : at + CH] + term * scale

    def block(offset):
        return lax.rem(me[0] + offset + 2 * count, count)

    row = iota((16, CH), 0)
    gather(grad_pre, field_copies)
    for a in range(3):
        for b in range(3):
            at = (a * 3 + b) * CH
            sums[0, at : at + CH] = from_acc(a, b).T * scale
    for side, message in pad_sides(vp, vm, hp, hm):
        strip = back[side]
        up, down = neighbours(strip)
        joined = jnp.concatenate([up, strip, down], axis=1).astype(BF16)
        term = lax.dot_general(message[0:SIDE], joined, first, preferred_element_type=F32)
        for k in range(3):
            add(0, edge_tap(side, k), term[:, k * CH : (k + 1) * CH])
    own = corner_rows(back)
    for q, message, start in pad_corners(hp, hm):
        right = jnp.where(row == 0, own[q], 0.0).astype(BF16)
        add(0, CORNER_TAP[q], lax.dot_general(message[start : start + 16], right, first, preferred_element_type=F32))

    gather(hidden, up_copies)
    for a in range(3):
        for b in range(3):
            at = (a * 3 + b) * CH
            sums[1, at : at + CH] = from_acc(2 - a, 2 - b) * scale
    for side, offset in ((N, width), (E, -1), (S, -width), (W, 1)):
        code = lax.rem(code_at(edge, block(offset), side), 4)
        term = lax.dot_general(fore[code].astype(BF16), pieces[side], first, preferred_element_type=F32)
        for k in range(3):
            add(1, edge_tap(side, k), term[:, k * CH : (k + 1) * CH])
    own = corner_rows(fore)
    for q, offset in ((NW, width + 1), (NE, width - 1), (SE, -width - 1), (SW, -width + 1)):
        code = code_at(corner, block(offset), q)
        cell = jnp.where(code == 0, own[0], jnp.where(code == 1, own[1], jnp.where(code == 2, own[2], own[3])))
        left = jnp.where(row == 1, cell, 0.0).astype(BF16)
        add(1, CORNER_TAP[q], lax.dot_general(left, corners[q], first, preferred_element_type=F32))

    high = (me[0] // 2) % 2
    keep[...] = sums[high]
    send[...] = sums[1 - high]


def weights_kernel(kernel_one, kernel_two, in_one, fwd_two):
    turned_weights(kernel_one, in_one)
    plain_weights(kernel_two, fwd_two)


def outputs_kernel(hidden, vp, vm, hp, hm, fwd_two, outputs, copies, west, east):
    halo_copies(copies, hidden, west, east, vp, vm, hp, hm)
    conv_all(copies, fwd_two, outputs)


def grads_kernel(
    count, width, me, edge, corner, vp, vm, hp, hm, grad_pre, in_one, grad_fields, copies, adds
):
    mb = 4
    returned(me[0], edge, corner, count, width, in_one, vp, vm, hp, hm, adds)
    zero_copies(copies, grad_pre)

    def rows(n, first=False, last=False):
        m = n * mb
        got = conv_pairs(copies, in_one, m, mb)
        for k in range(mb):
            for part in range(2):
                g = with_adds(
                    got[k * SIDE : (k + 1) * SIDE, part * CH : (part + 1) * CH],
                    2 * (m + k) + part, adds,
                    first and k == 0 and part == 0, last and k == mb - 1 and part == 1,
                )
                grad_fields[m + k, part] = g.astype(BF16)

    def step(n, _):
        rows(n)
        return 0

    rows(0, first=True)
    lax.fori_loop(1, HALF // mb - 1, step, 0)
    rows(HALF // mb - 1, last=True)


def struct(shape, dtype=BF16):
    return jax.ShapeDtypeStruct(shape, dtype)


BLOCK = (HALF, 2, SIDE, CH)
COPIES = (3, HALF + 1, 2, SIDE, CH)
WEIGHTS = (12 * CH, 2 * CH)


def call(body, tables, arrays, outs, scratch=(), flops=0, moved=4 << 20, space=VMEM):
    return pl.pallas_call(
        body,
        out_shape=outs,
        in_specs=[SMEM] * tables + [space] * arrays,
        out_specs=tuple(VMEM for _ in outs),
        scratch_shapes=list(scratch),
        compiler_params=PARAMS,
        cost_estimate=pl.CostEstimate(flops=flops, bytes_accessed=moved, transcendentals=0),
    )


def shifted(x, by):
    size = lax.axis_size(AXES)
    return lax.ppermute(x, AXES, [(i, (i + by) % size) for i in range(size)])


def swap(x, bit):
    size = lax.axis_size(AXES)
    return lax.ppermute(x, AXES, [(i, i ^ bit) for i in range(size)])


def vertical(vp, vm, width):
    return shifted(vp, width), shifted(vm, -width)


def horizontal(vp, vm, hp, hm):
    hp = jnp.concatenate([hp, vp[STRIPS : STRIPS + 16], vm[STRIPS : STRIPS + 16]])
    hm = jnp.concatenate([hm, vp[STRIPS + 16 : VROWS], vm[STRIPS + 16 : VROWS]])
    return shifted(hp, 1), shifted(hm, -1)


FIRST = 2
HALVED = (1, 4, 64)
NARROW = (1, 4)
WHOLE = (32, 128, 8, 16)


def total(keep, send, works):
    me = lax.axis_index(AXES)
    done = {}
    steps = [0]

    def beside(sent, bit):
        work = works.get(steps[0])
        steps[0] += 1
        if work is None:
            return swap(sent, bit)
        sent, held = lax.optimization_barrier((sent, done.copy()))
        done.update(held)
        got = swap(sent, bit)
        gave = work(done)
        got, gave = lax.optimization_barrier((got, gave))
        done.update(gave)
        return got

    x = keep + beside(send, FIRST)
    rows = x.shape[0]
    for bit in HALVED:
        rows //= 2
        high = (me // bit) % 2
        send = lax.dynamic_slice_in_dim(x, (1 - high) * rows, rows, 0)
        keep = lax.dynamic_slice_in_dim(x, high * rows, rows, 0)
        if bit in NARROW:
            x = keep + beside(send.astype(BF16), bit).astype(F32)
        else:
            x = keep + beside(send, bit)
    for bit in WHOLE:
        x = x + beside(x, bit)
    x = x.astype(BF16)
    for bit in reversed(HALVED):
        high = (me // bit) % 2
        other = beside(x, bit)
        x = jnp.where(high == 1, jnp.concatenate([other, x]), jnp.concatenate([x, other]))
    other = beside(x, FIRST)
    high = (me // FIRST) % 2
    grads = jnp.where(high == 0, x, other), jnp.where(high == 0, other, x)
    return [grad.astype(F32) for grad in grads], done


def local(inputs, kernel_one, kernel_two, cotangent, edge_codes, corner_codes):
    count = lax.axis_size(AXES)
    width = lax.axis_size("face") // GRID_ROWS * lax.axis_size("sub")
    scale = 1.0 / math.sqrt(count * SIDE * SIDE)
    me = lax.axis_index(AXES).astype(jnp.int32).reshape(1)
    tables = (me, edge_codes, corner_codes)
    fields = inputs.reshape(BLOCK)
    upstream = cotangent.reshape(BLOCK)
    message = struct((VROWS, CH))
    own = struct((STRIPS, CH))
    weights = struct(WEIGHTS)
    block = struct(BLOCK)
    copies = struct(COPIES)
    wide = struct(BLOCK, F32)
    sides = (4, SIDE, CH)
    strips = pltpu.VMEM(sides, F32)
    column = pltpu.VMEM((SIDE, CH), F32)
    conv_flops = 2 * SIDE * SIDE * 9 * CH * CH

    vp, vm, hp, hm = call(
        lambda *refs: pack_kernel(count, width, *refs), 3, 2, (message, message, own, own),
        [
            strips, strips, pltpu.VMEM((2, 2, SIDE, CH), BF16),
            pltpu.VMEM((2, 2, HALF, 2, 16, CH), BF16), pltpu.SemaphoreType.DMA((2, 4)),
        ],
        space=HBM,
    )(*tables, fields, upstream)
    vp, vm, kernel_two, upstream = lax.optimization_barrier((vp, vm, kernel_two, upstream))
    vp, vm = vertical(vp, vm, width)
    in_two, up_copies, grad = call(back_kernel, 0, 2, (weights, copies, wide), (), conv_flops)(
        kernel_two, upstream
    )
    vp, vm, in_two, up_copies, grad, kernel_one, fields = lax.optimization_barrier(
        (vp, vm, in_two, up_copies, grad, kernel_one, fields)
    )
    hp, hm = horizontal(vp, vm, hp, hm)
    fwd_one, field_copies, pre = call(fore_kernel, 0, 2, (weights, copies, wide), (), conv_flops)(
        kernel_one, fields
    )
    hidden, grad_pre, vp2, vm2, hp2, hm2, fore, back, pieces, corners = call(
        lambda *refs: middle_kernel(count, width, *refs), 3, 8,
        (
            block, block, message, message, own, own, struct(sides, F32), struct(sides, F32),
            struct((4, SIDE, 3 * CH)), struct((4, 16, CH)),
        ),
        [strips, strips], conv_flops,
    )(*tables, vp, vm, hp, hm, fwd_one, in_two, pre, grad)
    keep, send = call(
        lambda *refs: sums_kernel(count, width, scale, *refs), 3, 12,
        (struct((9 * CH, CH), F32), struct((9 * CH, CH), F32)),
        [pltpu.VMEM((2 * CH, 12 * CH), F32), pltpu.VMEM((2, 9 * CH, CH), F32)],
        2 * conv_flops,
    )(*tables, vp, vm, hp, hm, hidden, grad_pre, field_copies, up_copies, fore, back, pieces, corners)

    def first_permutes(done):
        vp, vm = vertical(vp2, vm2, width)
        return dict(vp=vp, vm=vm)

    def second_permutes(done):
        hp, hm = horizontal(done["vp"], done["vm"], hp2, hm2)
        return dict(hp=hp, hm=hm)

    def make_weights(done):
        in_one, fwd_two = call(weights_kernel, 0, 2, (weights, weights))(
            done["kernel_one"], done["kernel_two"]
        )
        return dict(in_one=in_one, fwd_two=fwd_two)

    def messages(done):
        return done["vp"], done["vm"], done["hp"], done["hm"]

    def make_outputs(done):
        outputs, = call(
            outputs_kernel, 0, 6, (block,), [pltpu.VMEM(COPIES, BF16), column, column], conv_flops
        )(hidden, *messages(done), done["fwd_two"])
        return dict(outputs=outputs)

    def make_grads(done):
        grad_fields, = call(
            lambda *refs: grads_kernel(count, width, *refs), 3, 6, (block,),
            [pltpu.VMEM(COPIES, BF16), strips], conv_flops,
        )(*tables, *messages(done), grad_pre, done["in_one"])
        return dict(grad_fields=grad_fields)

    def given(work, **arrays):
        return lambda done: work({**arrays, **done})

    grads, done = total(
        keep, send,
        {
            1: first_permutes,
            2: second_permutes,
            4: given(make_weights, kernel_one=kernel_one, kernel_two=kernel_two),
            5: make_outputs,
            6: make_grads,
        },
    )
    shape = (1, 1, SIDE, SIDE, CH)
    taps = (3, 3, CH, CH)
    return (
        done["outputs"].reshape(shape), done["grad_fields"].reshape(shape),
        grads[0].reshape(taps), grads[1].reshape(taps),
    )


def solution(mesh):
    block = P("face", "sub", None, None, None)
    return jax.shard_map(
        local,
        mesh=mesh,
        in_specs=(block, P(), P(), block, P(), P()),
        out_specs=(block, block, P(), P()),
        check_vma=False,
    )
```

```python
import math

import jax
import jax.numpy as jnp
from jax import lax
from jax.experimental import pallas as pl
from jax.experimental.pallas import tpu as pltpu
from jax.sharding import PartitionSpec as P

AXES = ("face", "sub")
GRID_ROWS = 8
SIDE = 64
CH = 128
HALF = SIDE // 2
STRIPS = 2 * SIDE
VROWS = STRIPS + 32
BF16 = jnp.bfloat16
F32 = jnp.float32
N, E, S, W = 0, 1, 2, 3
NW, NE, SE, SW = 0, 1, 2, 3
VMEM = pl.BlockSpec(memory_space=pltpu.VMEM)
SMEM = pl.BlockSpec(memory_space=pltpu.SMEM)
ANY = pl.BlockSpec(memory_space=pl.ANY)
ROOM = 20 << 20


def code_at(table, block, which):
    return table[block % 2, which, block // 2]


def iota(shape, dim):
    return lax.broadcasted_iota(jnp.int32, shape, dim)


def strips_from(north, south, low, high, dst):
    dst[N] = north.astype(F32)
    dst[S] = south.astype(F32)
    low = low.reshape(SIDE, 16, CH).astype(F32)
    dst[W] = jnp.sum(jnp.where(iota(low.shape, 1) == 0, low, 0.0), axis=1)
    high = high.reshape(SIDE, 16, CH).astype(F32)
    dst[E] = jnp.sum(jnp.where(iota(high.shape, 1) == 15, high, 0.0), axis=1)


def side_strips(block, dst):
    strips_from(
        block[0, 0], block[HALF - 1, 1], block[:, :, 0:16, :], block[:, :, SIDE - 16 : SIDE, :], dst
    )


def corner_rows(strips):
    north = strips[N]
    south = strips[S]
    last = SIDE - 1
    return [north[0:1], north[last : last + 1], south[last : last + 1], south[0:1]]


def turned(strip, flip):
    row = iota((SIDE, SIDE), 0)
    col = iota((SIDE, SIDE), 1)
    target = jnp.where(flip, SIDE - 1 - row, row)
    matrix = jnp.where(col == target, 1.0, 0.0).astype(BF16)
    return jnp.dot(matrix, strip.astype(BF16), preferred_element_type=F32).astype(BF16)


def corner_block(code, own, other):
    picked = jnp.where(code == 0, own[0], jnp.where(code == 1, own[1], jnp.where(code == 2, own[2], own[3])))
    row = iota((16, CH), 0)
    return (jnp.where(row == 0, picked, 0.0) + jnp.where(row == 1, other, 0.0)).astype(BF16)


def pack(me, edge, corner, count, width, fore, back, vp, vm, hp, hm):
    fore_corners = corner_rows(fore)
    back_corners = corner_rows(back)

    def block(offset):
        return lax.rem(me + offset + 2 * count, count)

    def strips(dst, offset, read_side, own_side):
        code = code_at(edge, block(offset), read_side)
        dst[0:SIDE] = turned(fore[lax.rem(code, 4)], code >= 4)
        dst[SIDE:STRIPS] = turned(back[own_side], code_at(edge, me, own_side) >= 4)

    def relayed(offset, read_corner, own_corner):
        return corner_block(
            code_at(corner, block(offset), read_corner), fore_corners, back_corners[own_corner]
        )

    strips(vp, width, N, S)
    vp[STRIPS : STRIPS + 16] = relayed(width + 1, NW, SE)
    vp[STRIPS + 16 : VROWS] = relayed(width - 1, NE, SW)
    strips(vm, -width, S, N)
    vm[STRIPS : STRIPS + 16] = relayed(-width + 1, SW, NE)
    vm[STRIPS + 16 : VROWS] = relayed(-width - 1, SE, NW)
    strips(hp, 1, W, E)
    strips(hm, -1, E, W)


def put_row(dst, pair, part, row, west, east):
    col = iota((SIDE, CH), 0)
    wide = row.astype(F32)
    dst[1, pair, part] = row.astype(BF16)
    dst[0, pair, part] = jnp.where(col == 0, west, pltpu.roll(wide, 1, 0)).astype(BF16)
    dst[2, pair, part] = jnp.where(col == SIDE - 1, east, pltpu.roll(wide, SIDE - 1, 0)).astype(BF16)


def shift_copies(dst, src, west=None, east=None):
    def step(k, _):
        for part in range(2):
            i = 2 * k + part
            w = 0.0 if west is None else west[pl.ds(i, 1), :]
            e = 0.0 if east is None else east[pl.ds(i, 1), :]
            put_row(dst, k + part, 1 - part, src[k, part], w, e)
        return 0

    lax.fori_loop(0, HALF, step, 0, unroll=4)


def halo_copies(dst, src, west, east, vp, vm, hp, hm):
    west[...] = hp[0:SIDE].astype(F32)
    east[...] = hm[0:SIDE].astype(F32)
    shift_copies(dst, src, west, east)
    hp1 = hp[STRIPS : STRIPS + 16].astype(F32)
    hp2 = hp[STRIPS + 16 : VROWS].astype(F32)
    hm1 = hm[STRIPS : STRIPS + 16].astype(F32)
    hm2 = hm[STRIPS + 16 : VROWS].astype(F32)
    put_row(dst, 0, 0, vp[0:SIDE], hp1[0:1], hm1[0:1])
    put_row(dst, HALF, 1, vm[0:SIDE], hp2[0:1], hm2[0:1])


def zero_copies(dst, src):
    zero = jnp.zeros((SIDE, CH), BF16)
    for b in range(3):
        dst[b, 0, 0] = zero
        dst[b, HALF, 1] = zero
    shift_copies(dst, src)


def window(copies, m, mb):
    parts = [
        copies[b, pl.ds(m + a // 2, mb), a % 2].reshape(mb * SIDE, CH)
        for a in range(4)
        for b in range(3)
    ]
    return jnp.concatenate(parts, axis=1)


def conv_pairs(copies, weights, m, mb):
    return jnp.dot(window(copies, m, mb), weights[...], preferred_element_type=F32)


def edge_tap(side, k):
    return {N: (0, k), S: (2, k), W: (k, 0), E: (k, 2)}[side]


CORNER_TAP = {NW: (0, 0), NE: (0, 2), SE: (2, 2), SW: (2, 0)}


def neighbours(strip):
    row = iota((SIDE, CH), 0)
    up = jnp.where(row == SIDE - 1, 0.0, pltpu.roll(strip, SIDE - 1, 0))
    down = jnp.where(row == 0, 0.0, pltpu.roll(strip, 1, 0))
    return up, down


def tap_plain(weights, a, b):
    at = (a * 3 + b) * CH
    return weights[at : at + CH, 0:CH]


def tap_transposed(turned_weights, a, b):
    at = ((2 - a) * 3 + 2 - b) * CH
    return turned_weights[at : at + CH, 0:CH]


def returned(me, edge, corner, count, width, turned_weights, vp, vm, hp, hm, adds, pieces=None, corners=None):
    def block(offset):
        return lax.rem(me + offset + 2 * count, count)

    adds[...] = jnp.zeros_like(adds)
    row = iota((SIDE, CH), 0)
    for side, offset, message in ((N, width, vm), (E, -1, hp), (S, -width, vp), (W, 1, hm)):
        code = code_at(edge, block(offset), side)
        flip = code >= 4
        strip = message[SIDE:STRIPS].astype(F32)
        up, down = neighbours(strip)
        joined = jnp.concatenate(
            [jnp.where(flip, down, up), strip, jnp.where(flip, up, down)], axis=1
        ).astype(BF16)
        if pieces is not None:
            pieces[side] = joined
        taps = jnp.concatenate(
            [tap_transposed(turned_weights, *edge_tap(side, k)) for k in range(3)], axis=0
        )
        at = lax.rem(code, 4)
        adds[at] = adds[at] + jnp.dot(joined, taps, preferred_element_type=F32)
    for q, offset, message, start in (
        (NW, width + 1, hm, STRIPS + 16),
        (NE, width - 1, hp, STRIPS + 16),
        (SE, -width - 1, hp, STRIPS),
        (SW, -width + 1, hm, STRIPS),
    ):
        code = code_at(corner, block(offset), q)
        cells = message[start : start + 16]
        if corners is not None:
            corners[q] = cells
        given = jnp.dot(
            cells, tap_transposed(turned_weights, *CORNER_TAP[q]), preferred_element_type=F32
        )[1:2]
        first = jnp.where(row == 0, given, 0.0)
        last = jnp.where(row == SIDE - 1, given, 0.0)
        adds[N] = adds[N] + jnp.where(code == NW, first, 0.0) + jnp.where(code == NE, last, 0.0)
        adds[S] = adds[S] + jnp.where(code == SW, first, 0.0) + jnp.where(code == SE, last, 0.0)


def with_adds(rows, i, adds, first=False, last=False):
    col = iota((8, CH), 0)
    rows = jnp.concatenate(
        [
            rows[0:8] + jnp.where(col == 0, adds[W, pl.ds(i, 1), :], 0.0),
            rows[8 : SIDE - 8],
            rows[SIDE - 8 :] + jnp.where(col == 7, adds[E, pl.ds(i, 1), :], 0.0),
        ],
        axis=0,
    )
    if first:
        rows = rows + adds[N]
    if last:
        rows = rows + adds[S]
    return rows


def pad_sides(vp, vm, hp, hm):
    return ((N, vp), (S, vm), (W, hp), (E, hm))


def pad_corners(hp, hm):
    return ((NW, hp, STRIPS), (NE, hm, STRIPS), (SE, hm, STRIPS + 16), (SW, hp, STRIPS + 16))


def received(weights, vp, vm, hp, hm, adds):
    row = iota((SIDE, CH), 0)
    for side, message in pad_sides(vp, vm, hp, hm):
        strip = message[0:SIDE].astype(F32)
        up, down = neighbours(strip)
        joined = jnp.concatenate([down, strip, up], axis=1).astype(BF16)
        taps = jnp.concatenate([tap_plain(weights, *edge_tap(side, k)) for k in range(3)], axis=0)
        adds[side] = jnp.dot(joined, taps, preferred_element_type=F32)
    for q, message, start in pad_corners(hp, hm):
        cells = message[start : start + 16]
        given = jnp.dot(cells, tap_plain(weights, *CORNER_TAP[q]), preferred_element_type=F32)[0:1]
        side = N if q in (NW, NE) else S
        place = 0 if q in (NW, SW) else SIDE - 1
        adds[side] = adds[side] + jnp.where(row == place, given, 0.0)


def pack_kernel(
    count, width, me, edge, corner, fields, upstream, vp, vm, hp, hm, fore, back, rows, columns, sems
):
    copies = []
    for k, source in enumerate((fields, upstream)):
        for j, (part, dst) in enumerate((
            (source.at[0, 0], rows.at[k, 0]),
            (source.at[HALF - 1, 1], rows.at[k, 1]),
            (source.at[:, :, pl.ds(0, 16), :], columns.at[k, 0]),
            (source.at[:, :, pl.ds(SIDE - 16, 16), :], columns.at[k, 1]),
        )):
            copies.append(pltpu.make_async_copy(part, dst, sems.at[k, j]))
    for copy in copies:
        copy.start()
    for copy in copies:
        copy.wait()
    for k, dst in enumerate((fore, back)):
        strips_from(rows[k, 0], rows[k, 1], columns[k, 0], columns[k, 1], dst)
    pack(me[0], edge, corner, count, width, fore, back, vp, vm, hp, hm)


def plain_weights(source, dst):
    zero = jnp.zeros((CH, CH), BF16)
    for b in range(3):
        for a in range(3):
            at = (a * 3 + b) * CH
            dst[at : at + CH, 0:CH] = source[a, b]
            dst[at + 3 * CH : at + 4 * CH, CH : 2 * CH] = source[a, b]
        dst[(9 + b) * CH : (10 + b) * CH, 0:CH] = zero
        dst[b * CH : (b + 1) * CH, CH : 2 * CH] = zero


def turned_weights(source, dst):
    zero = jnp.zeros((CH, CH), BF16)
    for b in range(3):
        for a in range(3):
            at = (a * 3 + b) * CH
            swapped = source[2 - a, 2 - b].astype(F32).T.astype(BF16)
            dst[at : at + CH, 0:CH] = swapped
            dst[at + 3 * CH : at + 4 * CH, CH : 2 * CH] = swapped
        dst[(9 + b) * CH : (10 + b) * CH, 0:CH] = zero
        dst[b * CH : (b + 1) * CH, CH : 2 * CH] = zero


def conv_all(copies, weights, dst):
    mb = 16

    def step(n, _):
        m = n * mb
        got = conv_pairs(copies, weights, m, mb)
        for part in range(2):
            lanes = slice(part * CH, (part + 1) * CH)
            dst[pl.ds(m, mb), part] = got[:, lanes].reshape(mb, SIDE, CH).astype(dst.dtype)
        return 0

    lax.fori_loop(0, HALF // mb, step, 0)


def back_kernel(token, kernel_two, upstream, in_two, up_copies, grad):
    turned_weights(kernel_two, in_two)
    zero_copies(up_copies, upstream)
    conv_all(up_copies, in_two, grad)


def fore_kernel(token, kernel_one, fields, fwd_one, copies, pre):
    plain_weights(kernel_one, fwd_one)
    zero_copies(copies, fields)
    conv_all(copies, fwd_one, pre)


def middle_kernel(
    count, width, me, edge, corner, vp, vm, hp, hm, fwd_one, in_two, pre, grad,
    hidden, grad_pre, vp2, vm2, hp2, hm2, fore, back, pieces, corners, grad_adds, pre_adds,
):
    returned(me[0], edge, corner, count, width, in_two, vp, vm, hp, hm, grad_adds, pieces, corners)
    received(fwd_one, vp, vm, hp, hm, pre_adds)

    def one(m, part, first=False, last=False):
        i = 2 * m + part
        p = with_adds(pre[m, part], i, pre_adds, first, last)
        g = with_adds(grad[m, part], i, grad_adds, first, last)
        s = 1.0 / (1.0 + jnp.exp(-p))
        hidden[m, part] = (p * s).astype(BF16)
        grad_pre[m, part] = (g * s * (1.0 + p * (1.0 - s))).astype(BF16)

    def step(m, _):
        one(m, 0)
        one(m, 1)
        return 0

    one(0, 0, first=True)
    one(0, 1)
    lax.fori_loop(1, HALF - 1, step, 0, unroll=2)
    one(HALF - 1, 0)
    one(HALF - 1, 1, last=True)
    side_strips(hidden, fore)
    side_strips(grad_pre, back)
    pack(me[0], edge, corner, count, width, fore, back, vp2, vm2, hp2, hm2)


def sums_kernel(
    count, width, scale, me, edge, corner, vp, vm, hp, hm, hidden, grad_pre, field_copies, up_copies,
    fore, back, pieces, corners, keep, send, acc, sums,
):
    gb = 8
    first = (((0,), (0,)), ((), ()))

    def gather(values, shifted):
        def grad_step(n, _):
            m = n * gb
            left = jnp.concatenate(
                [values[pl.ds(m, gb), part].reshape(gb * SIDE, CH) for part in range(2)], axis=1
            )
            acc[...] += lax.dot_general(left, window(shifted, m, gb), first, preferred_element_type=F32)
            return 0

        acc[...] = jnp.zeros_like(acc)
        lax.fori_loop(0, HALF // gb, grad_step, 0)

    def from_acc(a, b):
        low = (a * 3 + b) * CH
        high = low + 3 * CH
        return acc[0:CH, low : low + CH] + acc[CH : 2 * CH, high : high + CH]

    def add(half, tap, term):
        at = (tap[0] * 3 + tap[1]) * CH
        sums[half, at : at + CH] = sums[half, at : at + CH] + term * scale

    def block(offset):
        return lax.rem(me[0] + offset + 2 * count, count)

    row = iota((16, CH), 0)
    gather(grad_pre, field_copies)
    for a in range(3):
        for b in range(3):
            at = (a * 3 + b) * CH
            sums[0, at : at + CH] = from_acc(a, b).T * scale
    for side, message in pad_sides(vp, vm, hp, hm):
        strip = back[side]
        up, down = neighbours(strip)
        joined = jnp.concatenate([up, strip, down], axis=1).astype(BF16)
        term = lax.dot_general(message[0:SIDE], joined, first, preferred_element_type=F32)
        for k in range(3):
            add(0, edge_tap(side, k), term[:, k * CH : (k + 1) * CH])
    own = corner_rows(back)
    for q, message, start in pad_corners(hp, hm):
        right = jnp.where(row == 0, own[q], 0.0).astype(BF16)
        add(0, CORNER_TAP[q], lax.dot_general(message[start : start + 16], right, first, preferred_element_type=F32))

    gather(hidden, up_copies)
    for a in range(3):
        for b in range(3):
            at = (a * 3 + b) * CH
            sums[1, at : at + CH] = from_acc(2 - a, 2 - b) * scale
    for side, offset in ((N, width), (E, -1), (S, -width), (W, 1)):
        code = lax.rem(code_at(edge, block(offset), side), 4)
        term = lax.dot_general(fore[code].astype(BF16), pieces[side], first, preferred_element_type=F32)
        for k in range(3):
            add(1, edge_tap(side, k), term[:, k * CH : (k + 1) * CH])
    own = corner_rows(fore)
    for q, offset in ((NW, width + 1), (NE, width - 1), (SE, -width - 1), (SW, -width + 1)):
        code = code_at(corner, block(offset), q)
        cell = jnp.where(code == 0, own[0], jnp.where(code == 1, own[1], jnp.where(code == 2, own[2], own[3])))
        left = jnp.where(row == 1, cell, 0.0).astype(BF16)
        add(1, CORNER_TAP[q], lax.dot_general(left, corners[q], first, preferred_element_type=F32))

    high = (me[0] // 2) % 2
    keep[...] = sums[high]
    send[...] = sums[1 - high]


def weights_kernel(token, kernel_one, kernel_two, in_one, fwd_two):
    turned_weights(kernel_one, in_one)
    plain_weights(kernel_two, fwd_two)


def outputs_kernel(hidden, vp, vm, hp, hm, fwd_two, outputs, copies, west, east):
    halo_copies(copies, hidden, west, east, vp, vm, hp, hm)
    conv_all(copies, fwd_two, outputs)


def grads_kernel(
    count, width, me, edge, corner, vp, vm, hp, hm, grad_pre, in_one, grad_fields, copies, adds
):
    mb = 8
    returned(me[0], edge, corner, count, width, in_one, vp, vm, hp, hm, adds)
    zero_copies(copies, grad_pre)

    def rows(n, first=False, last=False):
        m = n * mb
        got = conv_pairs(copies, in_one, m, mb)
        for k in range(mb):
            for part in range(2):
                g = with_adds(
                    got[k * SIDE : (k + 1) * SIDE, part * CH : (part + 1) * CH],
                    2 * (m + k) + part, adds,
                    first and k == 0 and part == 0, last and k == mb - 1 and part == 1,
                )
                grad_fields[m + k, part] = g.astype(BF16)

    def step(n, _):
        rows(n)
        return 0

    rows(0, first=True)
    lax.fori_loop(1, HALF // mb - 1, step, 0)
    rows(HALF // mb - 1, last=True)


def finish_kernel(me, mine, other, first, second):
    high = (me[0] // FIRST) % 2

    @pl.when(high == 0)
    def _():
        first[...] = mine[...].astype(F32)
        second[...] = other[...].astype(F32)

    @pl.when(high == 1)
    def _():
        first[...] = other[...].astype(F32)
        second[...] = mine[...].astype(F32)


def struct(shape, dtype=BF16):
    return jax.ShapeDtypeStruct(shape, dtype)


BLOCK = (HALF, 2, SIDE, CH)
COPIES = (3, HALF + 1, 2, SIDE, CH)
WEIGHTS = (12 * CH, 2 * CH)


def call(body, tables, arrays, outs, scratch=(), flops=0, moved=4 << 20, space=VMEM, room=ROOM):
    return pl.pallas_call(
        body,
        out_shape=outs,
        in_specs=[SMEM] * tables + [space] * arrays,
        out_specs=tuple(VMEM for _ in outs),
        scratch_shapes=list(scratch),
        compiler_params=pltpu.CompilerParams(vmem_limit_bytes=room),
        cost_estimate=pl.CostEstimate(flops=flops, bytes_accessed=moved, transcendentals=0),
    )


def shifted(x, by):
    size = lax.axis_size(AXES)
    return lax.ppermute(x, AXES, [(i, (i + by) % size) for i in range(size)])


def swap(x, bit):
    size = lax.axis_size(AXES)
    return lax.ppermute(x, AXES, [(i, i ^ bit) for i in range(size)])


def vertical(vp, vm, width):
    return shifted(vp, width), shifted(vm, -width)


def horizontal(vp, vm, hp, hm):
    hp = jnp.concatenate([hp, vp[STRIPS : STRIPS + 16], vm[STRIPS : STRIPS + 16]])
    hm = jnp.concatenate([hm, vp[STRIPS + 16 : VROWS], vm[STRIPS + 16 : VROWS]])
    return shifted(hp, 1), shifted(hm, -1)


FIRST = 2
HALVED = (1, 4, 64)
NARROW = (1, 4)
WHOLE = (32, 128, 8, 16)


def total(keep, send, done, works):
    me = lax.axis_index(AXES).astype(jnp.int32)
    steps = [0]

    def beside(sent, bit):
        work = works.get(steps[0])
        steps[0] += 1
        if work is None:
            return swap(sent, bit)
        sent, held = lax.optimization_barrier((sent, done.copy()))
        done.update(held)
        got = swap(sent, bit)
        gave = work(done)
        got, gave = lax.optimization_barrier((got, gave))
        done.update(gave)
        return got

    x = keep + beside(send, FIRST)
    rows = x.shape[0]
    for bit in HALVED:
        rows //= 2
        high = (me // bit) % 2
        send = lax.dynamic_slice_in_dim(x, (1 - high) * rows, rows, 0)
        keep = lax.dynamic_slice_in_dim(x, high * rows, rows, 0)
        if bit in NARROW:
            x = keep + beside(send.astype(BF16), bit).astype(F32)
        else:
            x = keep + beside(send, bit)
    for bit in WHOLE:
        x = x + beside(x, bit)
    x = x.astype(BF16)
    for bit in reversed(HALVED):
        high = (me // bit) % 2
        other = beside(x, bit)
        x = jnp.where(high == 1, jnp.concatenate([other, x]), jnp.concatenate([x, other]))
    out = struct(x.shape, F32)
    grads = call(finish_kernel, 1, 2, (out, out))(me.reshape(1), x, beside(x, FIRST))
    return grads, done


def local(inputs, kernel_one, kernel_two, cotangent, edge_codes, corner_codes):
    count = lax.axis_size(AXES)
    width = lax.axis_size("face") // GRID_ROWS * lax.axis_size("sub")
    scale = 1.0 / math.sqrt(count * SIDE * SIDE)
    me = lax.axis_index(AXES).astype(jnp.int32).reshape(1)
    tables = (me, jnp.transpose(edge_codes, (1, 2, 0)), jnp.transpose(corner_codes, (1, 2, 0)))
    fields = inputs.reshape(BLOCK)
    upstream = cotangent.reshape(BLOCK)
    message = struct((VROWS, CH))
    own = struct((STRIPS, CH))
    weights = struct(WEIGHTS)
    block = struct(BLOCK)
    copies = struct(COPIES)
    wide = struct(BLOCK, F32)
    sides = (4, SIDE, CH)
    strips = pltpu.VMEM(sides, F32)
    column = pltpu.VMEM((SIDE, CH), F32)
    conv_flops = 2 * SIDE * SIDE * 9 * CH * CH

    vp, vm, hp, hm = call(
        lambda *refs: pack_kernel(count, width, *refs), 3, 2, (message, message, own, own),
        [
            strips, strips, pltpu.VMEM((2, 2, SIDE, CH), BF16),
            pltpu.VMEM((2, 2, HALF, 2, 16, CH), BF16), pltpu.SemaphoreType.DMA((2, 4)),
        ],
        space=ANY, room=56 << 20,
    )(*tables, fields, upstream)
    vp, vm, token = lax.optimization_barrier((vp, vm, me))
    vp, vm = vertical(vp, vm, width)
    in_two, up_copies, grad = call(back_kernel, 1, 2, (weights, copies, wide), (), conv_flops)(
        token, kernel_two, upstream
    )
    vp, vm, in_two, up_copies, grad, token = lax.optimization_barrier(
        (vp, vm, in_two, up_copies, grad, token)
    )
    hp, hm = horizontal(vp, vm, hp, hm)
    fwd_one, field_copies, pre = call(fore_kernel, 1, 2, (weights, copies, wide), (), conv_flops)(
        token, kernel_one, fields
    )
    hidden, grad_pre, vp2, vm2, hp2, hm2, fore, back, pieces, corners = call(
        lambda *refs: middle_kernel(count, width, *refs), 3, 8,
        (
            block, block, message, message, own, own, struct(sides, F32), struct(sides, F32),
            struct((4, SIDE, 3 * CH)), struct((4, 16, CH)),
        ),
        [strips, strips], conv_flops,
    )(*tables, vp, vm, hp, hm, fwd_one, in_two, pre, grad)
    hidden, grad_pre, vp2, vm2 = lax.optimization_barrier((hidden, grad_pre, vp2, vm2))
    vp2, vm2 = vertical(vp2, vm2, width)
    keep, send = call(
        lambda *refs: sums_kernel(count, width, scale, *refs), 3, 12,
        (struct((9 * CH, CH), F32), struct((9 * CH, CH), F32)),
        [pltpu.VMEM((2 * CH, 12 * CH), F32), pltpu.VMEM((2, 9 * CH, CH), F32)],
        2 * conv_flops,
    )(*tables, vp, vm, hp, hm, hidden, grad_pre, field_copies, up_copies, fore, back, pieces, corners)

    keep, send, vp2, vm2 = lax.optimization_barrier((keep, send, vp2, vm2))

    def second_permutes(done):
        hp, hm = horizontal(done["vp"], done["vm"], hp2, hm2)
        return dict(hp=hp, hm=hm)

    def make_weights(done):
        in_one, fwd_two = call(weights_kernel, 1, 2, (weights, weights))(
            done["token"], kernel_one, kernel_two
        )
        return dict(in_one=in_one, fwd_two=fwd_two)

    def messages(done):
        return done["vp"], done["vm"], done["hp"], done["hm"]

    def make_outputs(done):
        outputs, = call(
            outputs_kernel, 0, 6, (block,), [pltpu.VMEM(COPIES, BF16), column, column], conv_flops
        )(hidden, *messages(done), done["fwd_two"])
        return dict(outputs=outputs)

    def make_grads(done):
        grad_fields, = call(
            lambda *refs: grads_kernel(count, width, *refs), 3, 6, (block,),
            [pltpu.VMEM(COPIES, BF16), strips], conv_flops,
        )(*tables, *messages(done), grad_pre, done["in_one"])
        return dict(grad_fields=grad_fields)

    grads, done = total(
        keep, send, dict(token=token, vp=vp2, vm=vm2),
        {1: second_permutes, 3: make_weights, 4: make_outputs, 6: make_grads},
    )
    shape = (1, 1, SIDE, SIDE, CH)
    taps = (3, 3, CH, CH)
    return (
        done["outputs"].reshape(shape), done["grad_fields"].reshape(shape),
        grads[0].reshape(taps), grads[1].reshape(taps),
    )


def solution(mesh):
    block = P("face", "sub", None, None, None)
    return jax.shard_map(
        local,
        mesh=mesh,
        in_specs=(block, P(), P(), block, P(), P()),
        out_specs=(block, block, P(), P()),
        check_vma=False,
    )
```

```python
import math

import jax
import jax.numpy as jnp
from jax import lax
from jax.experimental import pallas as pl
from jax.experimental.pallas import tpu as pltpu
from jax.sharding import PartitionSpec as P

AXES = ("face", "sub")
GRID_ROWS = 8
SIDE = 64
CH = 128
HALF = SIDE // 2
STRIPS = 2 * SIDE
VROWS = STRIPS + 32
BF16 = jnp.bfloat16
F32 = jnp.float32
N, E, S, W = 0, 1, 2, 3
NW, NE, SE, SW = 0, 1, 2, 3
VMEM = pl.BlockSpec(memory_space=pltpu.VMEM)
SMEM = pl.BlockSpec(memory_space=pltpu.SMEM)
ANY = pl.BlockSpec(memory_space=pl.ANY)
ROOM = 20 << 20


def code_at(table, block, which):
    return table[block % 2, which, block // 2]


def iota(shape, dim):
    return lax.broadcasted_iota(jnp.int32, shape, dim)


def strips_from(north, south, low, high, dst):
    dst[N] = north.astype(F32)
    dst[S] = south.astype(F32)
    low = low.reshape(SIDE, 16, CH).astype(F32)
    dst[W] = jnp.sum(jnp.where(iota(low.shape, 1) == 0, low, 0.0), axis=1)
    high = high.reshape(SIDE, 16, CH).astype(F32)
    dst[E] = jnp.sum(jnp.where(iota(high.shape, 1) == 15, high, 0.0), axis=1)


def side_strips(block, dst):
    strips_from(
        block[0, 0], block[HALF - 1, 1], block[:, :, 0:16, :], block[:, :, SIDE - 16 : SIDE, :], dst
    )


def corner_rows(strips):
    north = strips[N]
    south = strips[S]
    last = SIDE - 1
    return [north[0:1], north[last : last + 1], south[last : last + 1], south[0:1]]


def turned(strip, flip):
    row = iota((SIDE, SIDE), 0)
    col = iota((SIDE, SIDE), 1)
    target = jnp.where(flip, SIDE - 1 - row, row)
    matrix = jnp.where(col == target, 1.0, 0.0).astype(BF16)
    return jnp.dot(matrix, strip.astype(BF16), preferred_element_type=F32).astype(BF16)


def corner_block(code, own, other):
    picked = jnp.where(code == 0, own[0], jnp.where(code == 1, own[1], jnp.where(code == 2, own[2], own[3])))
    row = iota((16, CH), 0)
    return (jnp.where(row == 0, picked, 0.0) + jnp.where(row == 1, other, 0.0)).astype(BF16)


def pack(me, edge, corner, count, width, fore, back, vp, vm, hp, hm):
    fore_corners = corner_rows(fore)
    back_corners = corner_rows(back)

    def block(offset):
        return lax.rem(me + offset + 2 * count, count)

    def strips(dst, offset, read_side, own_side):
        code = code_at(edge, block(offset), read_side)
        dst[0:SIDE] = turned(fore[lax.rem(code, 4)], code >= 4)
        dst[SIDE:STRIPS] = turned(back[own_side], code_at(edge, me, own_side) >= 4)

    def relayed(offset, read_corner, own_corner):
        return corner_block(
            code_at(corner, block(offset), read_corner), fore_corners, back_corners[own_corner]
        )

    strips(vp, width, N, S)
    vp[STRIPS : STRIPS + 16] = relayed(width + 1, NW, SE)
    vp[STRIPS + 16 : VROWS] = relayed(width - 1, NE, SW)
    strips(vm, -width, S, N)
    vm[STRIPS : STRIPS + 16] = relayed(-width + 1, SW, NE)
    vm[STRIPS + 16 : VROWS] = relayed(-width - 1, SE, NW)
    strips(hp, 1, W, E)
    strips(hm, -1, E, W)


def put_row(dst, pair, part, row, west, east):
    col = iota((SIDE, CH), 0)
    wide = row.astype(F32)
    dst[1, pair, part] = row.astype(BF16)
    dst[0, pair, part] = jnp.where(col == 0, west, pltpu.roll(wide, 1, 0)).astype(BF16)
    dst[2, pair, part] = jnp.where(col == SIDE - 1, east, pltpu.roll(wide, SIDE - 1, 0)).astype(BF16)


def shift_copies(dst, src, west=None, east=None):
    def step(k, _):
        for part in range(2):
            i = 2 * k + part
            w = 0.0 if west is None else west[pl.ds(i, 1), :]
            e = 0.0 if east is None else east[pl.ds(i, 1), :]
            put_row(dst, k + part, 1 - part, src[k, part], w, e)
        return 0

    lax.fori_loop(0, HALF, step, 0, unroll=4)


def halo_copies(dst, src, west, east, vp, vm, hp, hm):
    west[...] = hp[0:SIDE].astype(F32)
    east[...] = hm[0:SIDE].astype(F32)
    shift_copies(dst, src, west, east)
    hp1 = hp[STRIPS : STRIPS + 16].astype(F32)
    hp2 = hp[STRIPS + 16 : VROWS].astype(F32)
    hm1 = hm[STRIPS : STRIPS + 16].astype(F32)
    hm2 = hm[STRIPS + 16 : VROWS].astype(F32)
    put_row(dst, 0, 0, vp[0:SIDE], hp1[0:1], hm1[0:1])
    put_row(dst, HALF, 1, vm[0:SIDE], hp2[0:1], hm2[0:1])


def zero_copies(dst, src):
    zero = jnp.zeros((SIDE, CH), BF16)
    for b in range(3):
        dst[b, 0, 0] = zero
        dst[b, HALF, 1] = zero
    shift_copies(dst, src)


def window(copies, m, mb):
    parts = [
        copies[b, pl.ds(m + a // 2, mb), a % 2].reshape(mb * SIDE, CH)
        for a in range(4)
        for b in range(3)
    ]
    return jnp.concatenate(parts, axis=1)


def conv_pairs(copies, weights, m, mb):
    return jnp.dot(window(copies, m, mb), weights[...], preferred_element_type=F32)


def edge_tap(side, k):
    return {N: (0, k), S: (2, k), W: (k, 0), E: (k, 2)}[side]


CORNER_TAP = {NW: (0, 0), NE: (0, 2), SE: (2, 2), SW: (2, 0)}


def neighbours(strip):
    row = iota((SIDE, CH), 0)
    up = jnp.where(row == SIDE - 1, 0.0, pltpu.roll(strip, SIDE - 1, 0))
    down = jnp.where(row == 0, 0.0, pltpu.roll(strip, 1, 0))
    return up, down


def tap_plain(weights, a, b):
    at = (a * 3 + b) * CH
    return weights[at : at + CH, 0:CH]


def tap_transposed(turned_weights, a, b):
    at = ((2 - a) * 3 + 2 - b) * CH
    return turned_weights[at : at + CH, 0:CH]


def returned(me, edge, corner, count, width, turned_weights, vp, vm, hp, hm, adds, pieces=None, corners=None):
    def block(offset):
        return lax.rem(me + offset + 2 * count, count)

    adds[...] = jnp.zeros_like(adds)
    row = iota((SIDE, CH), 0)
    for side, offset, message in ((N, width, vm), (E, -1, hp), (S, -width, vp), (W, 1, hm)):
        code = code_at(edge, block(offset), side)
        flip = code >= 4
        strip = message[SIDE:STRIPS].astype(F32)
        up, down = neighbours(strip)
        joined = jnp.concatenate(
            [jnp.where(flip, down, up), strip, jnp.where(flip, up, down)], axis=1
        ).astype(BF16)
        if pieces is not None:
            pieces[side] = joined
        taps = jnp.concatenate(
            [tap_transposed(turned_weights, *edge_tap(side, k)) for k in range(3)], axis=0
        )
        at = lax.rem(code, 4)
        adds[at] = adds[at] + jnp.dot(joined, taps, preferred_element_type=F32)
    for q, offset, message, start in (
        (NW, width + 1, hm, STRIPS + 16),
        (NE, width - 1, hp, STRIPS + 16),
        (SE, -width - 1, hp, STRIPS),
        (SW, -width + 1, hm, STRIPS),
    ):
        code = code_at(corner, block(offset), q)
        cells = message[start : start + 16]
        if corners is not None:
            corners[q] = cells
        given = jnp.dot(
            cells, tap_transposed(turned_weights, *CORNER_TAP[q]), preferred_element_type=F32
        )[1:2]
        first = jnp.where(row == 0, given, 0.0)
        last = jnp.where(row == SIDE - 1, given, 0.0)
        adds[N] = adds[N] + jnp.where(code == NW, first, 0.0) + jnp.where(code == NE, last, 0.0)
        adds[S] = adds[S] + jnp.where(code == SW, first, 0.0) + jnp.where(code == SE, last, 0.0)


def with_adds(rows, i, adds, first=False, last=False):
    col = iota((8, CH), 0)
    rows = jnp.concatenate(
        [
            rows[0:8] + jnp.where(col == 0, adds[W, pl.ds(i, 1), :], 0.0),
            rows[8 : SIDE - 8],
            rows[SIDE - 8 :] + jnp.where(col == 7, adds[E, pl.ds(i, 1), :], 0.0),
        ],
        axis=0,
    )
    if first:
        rows = rows + adds[N]
    if last:
        rows = rows + adds[S]
    return rows


def pad_sides(vp, vm, hp, hm):
    return ((N, vp), (S, vm), (W, hp), (E, hm))


def pad_corners(hp, hm):
    return ((NW, hp, STRIPS), (NE, hm, STRIPS), (SE, hm, STRIPS + 16), (SW, hp, STRIPS + 16))


def received(weights, vp, vm, hp, hm, adds):
    row = iota((SIDE, CH), 0)
    for side, message in pad_sides(vp, vm, hp, hm):
        strip = message[0:SIDE].astype(F32)
        up, down = neighbours(strip)
        joined = jnp.concatenate([down, strip, up], axis=1).astype(BF16)
        taps = jnp.concatenate([tap_plain(weights, *edge_tap(side, k)) for k in range(3)], axis=0)
        adds[side] = jnp.dot(joined, taps, preferred_element_type=F32)
    for q, message, start in pad_corners(hp, hm):
        cells = message[start : start + 16]
        given = jnp.dot(cells, tap_plain(weights, *CORNER_TAP[q]), preferred_element_type=F32)[0:1]
        side = N if q in (NW, NE) else S
        place = 0 if q in (NW, SW) else SIDE - 1
        adds[side] = adds[side] + jnp.where(row == place, given, 0.0)


def pack_kernel(
    count, width, me, edge, corner, fields, upstream, vp, vm, hp, hm, fore, back, rows, columns, sems
):
    copies = []
    for k, source in enumerate((fields, upstream)):
        for j, (part, dst) in enumerate((
            (source.at[0, 0], rows.at[k, 0]),
            (source.at[HALF - 1, 1], rows.at[k, 1]),
            (source.at[:, :, pl.ds(0, 16), :], columns.at[k, 0]),
            (source.at[:, :, pl.ds(SIDE - 16, 16), :], columns.at[k, 1]),
        )):
            copies.append(pltpu.make_async_copy(part, dst, sems.at[k, j]))
    for copy in copies:
        copy.start()
    for copy in copies:
        copy.wait()
    for k, dst in enumerate((fore, back)):
        strips_from(rows[k, 0], rows[k, 1], columns[k, 0], columns[k, 1], dst)
    pack(me[0], edge, corner, count, width, fore, back, vp, vm, hp, hm)


def plain_weights(source, dst):
    zero = jnp.zeros((CH, CH), BF16)
    for b in range(3):
        for a in range(3):
            at = (a * 3 + b) * CH
            dst[at : at + CH, 0:CH] = source[a, b]
            dst[at + 3 * CH : at + 4 * CH, CH : 2 * CH] = source[a, b]
        dst[(9 + b) * CH : (10 + b) * CH, 0:CH] = zero
        dst[b * CH : (b + 1) * CH, CH : 2 * CH] = zero


def turned_weights(source, dst):
    zero = jnp.zeros((CH, CH), BF16)
    for b in range(3):
        for a in range(3):
            at = (a * 3 + b) * CH
            swapped = source[2 - a, 2 - b].astype(F32).T.astype(BF16)
            dst[at : at + CH, 0:CH] = swapped
            dst[at + 3 * CH : at + 4 * CH, CH : 2 * CH] = swapped
        dst[(9 + b) * CH : (10 + b) * CH, 0:CH] = zero
        dst[b * CH : (b + 1) * CH, CH : 2 * CH] = zero


def conv_all(copies, weights, dst):
    mb = 16

    def step(n, _):
        m = n * mb
        got = conv_pairs(copies, weights, m, mb)
        for part in range(2):
            lanes = slice(part * CH, (part + 1) * CH)
            dst[pl.ds(m, mb), part] = got[:, lanes].reshape(mb, SIDE, CH).astype(dst.dtype)
        return 0

    lax.fori_loop(0, HALF // mb, step, 0)


def back_kernel(token, kernel_two, upstream, in_two, up_copies, grad):
    turned_weights(kernel_two, in_two)
    zero_copies(up_copies, upstream)
    conv_all(up_copies, in_two, grad)


def fore_kernel(token, kernel_one, fields, fwd_one, copies, pre):
    plain_weights(kernel_one, fwd_one)
    zero_copies(copies, fields)
    conv_all(copies, fwd_one, pre)


def middle_kernel(
    count, width, me, edge, corner, vp, vm, hp, hm, fwd_one, in_two, pre, grad,
    hidden, grad_pre, vp2, vm2, hp2, hm2, fore, back, pieces, corners, grad_adds, pre_adds,
):
    returned(me[0], edge, corner, count, width, in_two, vp, vm, hp, hm, grad_adds, pieces, corners)
    received(fwd_one, vp, vm, hp, hm, pre_adds)

    def one(m, part, first=False, last=False):
        i = 2 * m + part
        p = with_adds(pre[m, part], i, pre_adds, first, last)
        g = with_adds(grad[m, part], i, grad_adds, first, last)
        s = 1.0 / (1.0 + jnp.exp(-p))
        hidden[m, part] = (p * s).astype(BF16)
        grad_pre[m, part] = (g * s * (1.0 + p * (1.0 - s))).astype(BF16)

    def step(m, _):
        one(m, 0)
        one(m, 1)
        return 0

    one(0, 0, first=True)
    one(0, 1)
    lax.fori_loop(1, HALF - 1, step, 0, unroll=2)
    one(HALF - 1, 0)
    one(HALF - 1, 1, last=True)
    side_strips(hidden, fore)
    side_strips(grad_pre, back)
    pack(me[0], edge, corner, count, width, fore, back, vp2, vm2, hp2, hm2)


def sums_kernel(
    count, width, scale, me, edge, corner, vp, vm, hp, hm, hidden, grad_pre, field_copies, up_copies,
    fore, back, pieces, corners, keep, send, acc, sums,
):
    gb = 8
    first = (((0,), (0,)), ((), ()))

    def gather(values, shifted):
        def grad_step(n, _):
            m = n * gb
            left = jnp.concatenate(
                [values[pl.ds(m, gb), part].reshape(gb * SIDE, CH) for part in range(2)], axis=1
            )
            acc[...] += lax.dot_general(left, window(shifted, m, gb), first, preferred_element_type=F32)
            return 0

        acc[...] = jnp.zeros_like(acc)
        lax.fori_loop(0, HALF // gb, grad_step, 0)

    def from_acc(a, b):
        low = (a * 3 + b) * CH
        high = low + 3 * CH
        return acc[0:CH, low : low + CH] + acc[CH : 2 * CH, high : high + CH]

    def add(half, tap, term):
        at = (tap[0] * 3 + tap[1]) * CH
        sums[half, at : at + CH] = sums[half, at : at + CH] + term * scale

    def block(offset):
        return lax.rem(me[0] + offset + 2 * count, count)

    row = iota((16, CH), 0)
    gather(grad_pre, field_copies)
    for a in range(3):
        for b in range(3):
            at = (a * 3 + b) * CH
            sums[0, at : at + CH] = from_acc(a, b).T * scale
    for side, message in pad_sides(vp, vm, hp, hm):
        strip = back[side]
        up, down = neighbours(strip)
        joined = jnp.concatenate([up, strip, down], axis=1).astype(BF16)
        term = lax.dot_general(message[0:SIDE], joined, first, preferred_element_type=F32)
        for k in range(3):
            add(0, edge_tap(side, k), term[:, k * CH : (k + 1) * CH])
    own = corner_rows(back)
    for q, message, start in pad_corners(hp, hm):
        right = jnp.where(row == 0, own[q], 0.0).astype(BF16)
        add(0, CORNER_TAP[q], lax.dot_general(message[start : start + 16], right, first, preferred_element_type=F32))

    gather(hidden, up_copies)
    for a in range(3):
        for b in range(3):
            at = (a * 3 + b) * CH
            sums[1, at : at + CH] = from_acc(2 - a, 2 - b) * scale
    for side, offset in ((N, width), (E, -1), (S, -width), (W, 1)):
        code = lax.rem(code_at(edge, block(offset), side), 4)
        term = lax.dot_general(fore[code].astype(BF16), pieces[side], first, preferred_element_type=F32)
        for k in range(3):
            add(1, edge_tap(side, k), term[:, k * CH : (k + 1) * CH])
    own = corner_rows(fore)
    for q, offset in ((NW, width + 1), (NE, width - 1), (SE, -width - 1), (SW, -width + 1)):
        code = code_at(corner, block(offset), q)
        cell = jnp.where(code == 0, own[0], jnp.where(code == 1, own[1], jnp.where(code == 2, own[2], own[3])))
        left = jnp.where(row == 1, cell, 0.0).astype(BF16)
        add(1, CORNER_TAP[q], lax.dot_general(left, corners[q], first, preferred_element_type=F32))

    high = (me[0] // 2) % 2
    keep[...] = sums[high]
    send[...] = sums[1 - high]


def weights_kernel(token, kernel_one, kernel_two, in_one, fwd_two):
    turned_weights(kernel_one, in_one)
    plain_weights(kernel_two, fwd_two)


def outputs_kernel(hidden, vp, vm, hp, hm, fwd_two, outputs, copies, west, east):
    halo_copies(copies, hidden, west, east, vp, vm, hp, hm)
    conv_all(copies, fwd_two, outputs)


def grads_kernel(
    count, width, me, edge, corner, vp, vm, hp, hm, grad_pre, in_one, grad_fields, copies, adds
):
    mb = 8
    returned(me[0], edge, corner, count, width, in_one, vp, vm, hp, hm, adds)
    zero_copies(copies, grad_pre)

    def rows(n, first=False, last=False):
        m = n * mb
        got = conv_pairs(copies, in_one, m, mb)
        for k in range(mb):
            for part in range(2):
                g = with_adds(
                    got[k * SIDE : (k + 1) * SIDE, part * CH : (part + 1) * CH],
                    2 * (m + k) + part, adds,
                    first and k == 0 and part == 0, last and k == mb - 1 and part == 1,
                )
                grad_fields[m + k, part] = g.astype(BF16)

    def step(n, _):
        rows(n)
        return 0

    rows(0, first=True)
    lax.fori_loop(1, HALF // mb - 1, step, 0)
    rows(HALF // mb - 1, last=True)


def finish_kernel(me, mine, other, first, second):
    high = (me[0] // FIRST) % 2

    @pl.when(high == 0)
    def _():
        first[...] = mine[...].astype(F32)
        second[...] = other[...].astype(F32)

    @pl.when(high == 1)
    def _():
        first[...] = other[...].astype(F32)
        second[...] = mine[...].astype(F32)


def struct(shape, dtype=BF16):
    return jax.ShapeDtypeStruct(shape, dtype)


BLOCK = (HALF, 2, SIDE, CH)
COPIES = (3, HALF + 1, 2, SIDE, CH)
WEIGHTS = (12 * CH, 2 * CH)


def call(body, tables, arrays, outs, scratch=(), flops=0, moved=4 << 20, space=VMEM, room=ROOM):
    return pl.pallas_call(
        body,
        out_shape=outs,
        in_specs=[SMEM] * tables + [space] * arrays,
        out_specs=tuple(VMEM for _ in outs),
        scratch_shapes=list(scratch),
        compiler_params=pltpu.CompilerParams(vmem_limit_bytes=room),
        cost_estimate=pl.CostEstimate(flops=flops, bytes_accessed=moved, transcendentals=0),
    )


def swap(x, bit):
    size = lax.axis_size(AXES)
    return lax.ppermute(x, AXES, [(i, i ^ bit) for i in range(size)])


def both_ways(ahead, behind, step):
    size = lax.axis_size(AXES)
    even = (lax.axis_index(AXES) // step) % 2 == 0

    def pairs(turn):
        return [(i, (i + (step if (i // step + turn) % 2 == 0 else -step)) % size) for i in range(size)]

    one = lax.ppermute(jnp.where(even, ahead, behind), AXES, pairs(0))
    two = lax.ppermute(jnp.where(even, behind, ahead), AXES, pairs(1))
    return jnp.where(even, two, one), jnp.where(even, one, two)


def vertical(vp, vm, width):
    return both_ways(vp, vm, width)


def horizontal(vp, vm, hp, hm):
    hp = jnp.concatenate([hp, vp[STRIPS : STRIPS + 16], vm[STRIPS : STRIPS + 16]])
    hm = jnp.concatenate([hm, vp[STRIPS + 16 : VROWS], vm[STRIPS + 16 : VROWS]])
    return both_ways(hp, hm, 1)


FIRST = 2
PLANE = (128, 64, 32, 1)
WHOLE = (4, 8, 16)


def plane_groups(size):
    mask = sum(PLANE)
    rest = [i for i in range(size) if i & mask == 0]
    members = [sum(bit for k, bit in enumerate(PLANE) if n >> k & 1) for n in range(1 << len(PLANE))]
    return [[base + member for member in members] for base in rest]


def total(keep, send, done, works):
    me = lax.axis_index(AXES).astype(jnp.int32)
    groups = plane_groups(lax.axis_size(AXES))
    steps = [0]

    def scatter(sent):
        return lax.all_to_all(sent, AXES, 0, 0, axis_index_groups=groups, tiled=True)

    def beside(sent, bit):
        move = scatter if bit is None else lambda sent: swap(sent, bit)
        work = works.get(steps[0])
        steps[0] += 1
        if work is None:
            return move(sent)
        sent, held = lax.optimization_barrier((sent, done.copy()))
        done.update(held)
        got = move(sent)
        gave = work(done)
        got, gave = lax.optimization_barrier((got, gave))
        done.update(gave)
        return got

    x = keep + beside(send, FIRST)
    parts = (len(groups[0]), x.shape[0] // len(groups[0]), CH)
    spread = beside(x.astype(BF16).reshape(parts), None)
    x = jnp.sum(spread.astype(F32), axis=0)
    for bit in WHOLE:
        x = x + beside(x, bit)
    spread = jnp.broadcast_to(x.astype(BF16)[None], parts)
    x = beside(spread, None).reshape(-1, CH)
    out = struct(x.shape, F32)
    grads = call(finish_kernel, 1, 2, (out, out))(me.reshape(1), x, beside(x, FIRST))
    return grads, done


def local(inputs, kernel_one, kernel_two, cotangent, edge_codes, corner_codes):
    count = lax.axis_size(AXES)
    width = lax.axis_size("face") // GRID_ROWS * lax.axis_size("sub")
    scale = 1.0 / math.sqrt(count * SIDE * SIDE)
    me = lax.axis_index(AXES).astype(jnp.int32).reshape(1)
    tables = (me, jnp.transpose(edge_codes, (1, 2, 0)), jnp.transpose(corner_codes, (1, 2, 0)))
    fields = inputs.reshape(BLOCK)
    upstream = cotangent.reshape(BLOCK)
    message = struct((VROWS, CH))
    own = struct((STRIPS, CH))
    weights = struct(WEIGHTS)
    block = struct(BLOCK)
    copies = struct(COPIES)
    wide = struct(BLOCK, F32)
    sides = (4, SIDE, CH)
    strips = pltpu.VMEM(sides, F32)
    column = pltpu.VMEM((SIDE, CH), F32)
    conv_flops = 2 * SIDE * SIDE * 9 * CH * CH

    vp, vm, hp, hm = call(
        lambda *refs: pack_kernel(count, width, *refs), 3, 2, (message, message, own, own),
        [
            strips, strips, pltpu.VMEM((2, 2, SIDE, CH), BF16),
            pltpu.VMEM((2, 2, HALF, 2, 16, CH), BF16), pltpu.SemaphoreType.DMA((2, 4)),
        ],
        space=ANY, room=56 << 20,
    )(*tables, fields, upstream)
    vp, vm, token = lax.optimization_barrier((vp, vm, me))
    vp, vm = vertical(vp, vm, width)
    in_two, up_copies, grad = call(back_kernel, 1, 2, (weights, copies, wide), (), conv_flops)(
        token, kernel_two, upstream
    )
    vp, vm, in_two, up_copies, grad, token = lax.optimization_barrier(
        (vp, vm, in_two, up_copies, grad, token)
    )
    hp, hm = horizontal(vp, vm, hp, hm)
    fwd_one, field_copies, pre = call(fore_kernel, 1, 2, (weights, copies, wide), (), conv_flops)(
        token, kernel_one, fields
    )
    hidden, grad_pre, vp2, vm2, hp2, hm2, fore, back, pieces, corners = call(
        lambda *refs: middle_kernel(count, width, *refs), 3, 8,
        (
            block, block, message, message, own, own, struct(sides, F32), struct(sides, F32),
            struct((4, SIDE, 3 * CH)), struct((4, 16, CH)),
        ),
        [strips, strips], conv_flops,
    )(*tables, vp, vm, hp, hm, fwd_one, in_two, pre, grad)
    hidden, grad_pre, vp2, vm2, token = lax.optimization_barrier((hidden, grad_pre, vp2, vm2, token))
    in_one, fwd_two = call(weights_kernel, 1, 2, (weights, weights))(token, kernel_one, kernel_two)
    keep, send = call(
        lambda *refs: sums_kernel(count, width, scale, *refs), 3, 12,
        (struct((9 * CH, CH), F32), struct((9 * CH, CH), F32)),
        [pltpu.VMEM((2 * CH, 12 * CH), F32), pltpu.VMEM((2, 9 * CH, CH), F32)],
        2 * conv_flops,
    )(*tables, vp, vm, hp, hm, hidden, grad_pre, field_copies, up_copies, fore, back, pieces, corners)

    def second_round(done):
        vp, vm = vertical(done["vp"], done["vm"], width)
        hp, hm = horizontal(vp, vm, hp2, hm2)
        return dict(vp=vp, vm=vm, hp=hp, hm=hm)

    def messages(done):
        return done["vp"], done["vm"], done["hp"], done["hm"]

    def make_outputs(done):
        outputs, = call(
            outputs_kernel, 0, 6, (block,), [pltpu.VMEM(COPIES, BF16), column, column], conv_flops
        )(hidden, *messages(done), fwd_two)
        return dict(outputs=outputs)

    def make_grads(done):
        grad_fields, = call(
            lambda *refs: grads_kernel(count, width, *refs), 3, 6, (block,),
            [pltpu.VMEM(COPIES, BF16), strips], conv_flops,
        )(*tables, *messages(done), grad_pre, in_one)
        return dict(grad_fields=grad_fields)

    grads, done = total(
        keep, send, dict(vp=vp2, vm=vm2),
        {1: second_round, 2: make_outputs, 3: make_grads},
    )
    shape = (1, 1, SIDE, SIDE, CH)
    taps = (3, 3, CH, CH)
    return (
        done["outputs"].reshape(shape), done["grad_fields"].reshape(shape),
        grads[0].reshape(taps), grads[1].reshape(taps),
    )


def solution(mesh):
    block = P("face", "sub", None, None, None)
    return jax.shard_map(
        local,
        mesh=mesh,
        in_specs=(block, P(), P(), block, P(), P()),
        out_specs=(block, block, P(), P()),
        check_vma=False,
    )
```

```python
import math

import jax
import jax.numpy as jnp
from jax import lax
from jax.experimental import pallas as pl
from jax.experimental.pallas import tpu as pltpu
from jax.sharding import PartitionSpec as P

AXES = ("face", "sub")
GRID_ROWS = 8
SIDE = 64
CH = 128
HALF = SIDE // 2
STRIPS = 2 * SIDE
VROWS = STRIPS + 32
BF16 = jnp.bfloat16
F32 = jnp.float32
N, E, S, W = 0, 1, 2, 3
NW, NE, SE, SW = 0, 1, 2, 3
VMEM = pl.BlockSpec(memory_space=pltpu.VMEM)
SMEM = pl.BlockSpec(memory_space=pltpu.SMEM)
ROOM = 20 << 20


def code_at(table, block, which):
    return table[block % 2, which, block // 2]


def iota(shape, dim):
    return lax.broadcasted_iota(jnp.int32, shape, dim)


def strips_from(north, south, low, high, dst):
    dst[N] = north.astype(F32)
    dst[S] = south.astype(F32)
    low = low.reshape(SIDE, 16, CH).astype(F32)
    dst[W] = jnp.sum(jnp.where(iota(low.shape, 1) == 0, low, 0.0), axis=1)
    high = high.reshape(SIDE, 16, CH).astype(F32)
    dst[E] = jnp.sum(jnp.where(iota(high.shape, 1) == 15, high, 0.0), axis=1)


def side_strips(block, dst):
    strips_from(
        block[0, 0], block[HALF - 1, 1], block[:, :, 0:16, :], block[:, :, SIDE - 16 : SIDE, :], dst
    )


def corner_rows(strips):
    north = strips[N]
    south = strips[S]
    last = SIDE - 1
    return [north[0:1], north[last : last + 1], south[last : last + 1], south[0:1]]


def turned(strip, flip):
    row = iota((SIDE, SIDE), 0)
    col = iota((SIDE, SIDE), 1)
    target = jnp.where(flip, SIDE - 1 - row, row)
    matrix = jnp.where(col == target, 1.0, 0.0).astype(BF16)
    return jnp.dot(matrix, strip.astype(BF16), preferred_element_type=F32).astype(BF16)


def corner_block(code, own, other):
    picked = jnp.where(code == 0, own[0], jnp.where(code == 1, own[1], jnp.where(code == 2, own[2], own[3])))
    row = iota((16, CH), 0)
    return (jnp.where(row == 0, picked, 0.0) + jnp.where(row == 1, other, 0.0)).astype(BF16)


def pack(me, edge, corner, count, width, fore, back, vp, vm, hp, hm):
    fore_corners = corner_rows(fore)
    back_corners = corner_rows(back)

    def block(offset):
        return lax.rem(me + offset + 2 * count, count)

    def strips(dst, offset, read_side, own_side):
        code = code_at(edge, block(offset), read_side)
        dst[0:SIDE] = turned(fore[lax.rem(code, 4)], code >= 4)
        dst[SIDE:STRIPS] = turned(back[own_side], code_at(edge, me, own_side) >= 4)

    def relayed(offset, read_corner, own_corner):
        return corner_block(
            code_at(corner, block(offset), read_corner), fore_corners, back_corners[own_corner]
        )

    strips(vp, width, N, S)
    vp[STRIPS : STRIPS + 16] = relayed(width + 1, NW, SE)
    vp[STRIPS + 16 : VROWS] = relayed(width - 1, NE, SW)
    strips(vm, -width, S, N)
    vm[STRIPS : STRIPS + 16] = relayed(-width + 1, SW, NE)
    vm[STRIPS + 16 : VROWS] = relayed(-width - 1, SE, NW)
    strips(hp, 1, W, E)
    strips(hm, -1, E, W)


def choose(even, one, two, ahead, behind):
    @pl.when(even)
    def _():
        ahead[...] = one[...]
        behind[...] = two[...]

    @pl.when(jnp.logical_not(even))
    def _():
        ahead[...] = two[...]
        behind[...] = one[...]


def even_row(me, width):
    return (me // width) % 2 == 0


def even_column(me):
    return me % 2 == 0


def put_row(dst, pair, part, row, west, east):
    col = iota((SIDE, CH), 0)
    wide = row.astype(F32)
    dst[1, pair, part] = row.astype(BF16)
    dst[0, pair, part] = jnp.where(col == 0, west, pltpu.roll(wide, 1, 0)).astype(BF16)
    dst[2, pair, part] = jnp.where(col == SIDE - 1, east, pltpu.roll(wide, SIDE - 1, 0)).astype(BF16)


def shift_copies(dst, src, west=None, east=None):
    def step(k, _):
        for part in range(2):
            i = 2 * k + part
            w = 0.0 if west is None else west[pl.ds(i, 1), :]
            e = 0.0 if east is None else east[pl.ds(i, 1), :]
            put_row(dst, k + part, 1 - part, src[k, part], w, e)
        return 0

    lax.fori_loop(0, HALF, step, 0, unroll=4)


def halo_copies(dst, src, west, east, vp, vm, hp, hm):
    west[...] = hp[0:SIDE].astype(F32)
    east[...] = hm[0:SIDE].astype(F32)
    shift_copies(dst, src, west, east)
    hp1 = hp[STRIPS : STRIPS + 16].astype(F32)
    hp2 = hp[STRIPS + 16 : VROWS].astype(F32)
    hm1 = hm[STRIPS : STRIPS + 16].astype(F32)
    hm2 = hm[STRIPS + 16 : VROWS].astype(F32)
    put_row(dst, 0, 0, vp[0:SIDE], hp1[0:1], hm1[0:1])
    put_row(dst, HALF, 1, vm[0:SIDE], hp2[0:1], hm2[0:1])


def zero_copies(dst, src):
    zero = jnp.zeros((SIDE, CH), BF16)
    for b in range(3):
        dst[b, 0, 0] = zero
        dst[b, HALF, 1] = zero
    shift_copies(dst, src)


def window(copies, m, mb):
    parts = [
        copies[b, pl.ds(m + a // 2, mb), a % 2].reshape(mb * SIDE, CH)
        for a in range(4)
        for b in range(3)
    ]
    return jnp.concatenate(parts, axis=1)


def conv_pairs(copies, weights, m, mb):
    return jnp.dot(window(copies, m, mb), weights[...], preferred_element_type=F32)


def edge_tap(side, k):
    return {N: (0, k), S: (2, k), W: (k, 0), E: (k, 2)}[side]


CORNER_TAP = {NW: (0, 0), NE: (0, 2), SE: (2, 2), SW: (2, 0)}


def neighbours(strip):
    row = iota((SIDE, CH), 0)
    up = jnp.where(row == SIDE - 1, 0.0, pltpu.roll(strip, SIDE - 1, 0))
    down = jnp.where(row == 0, 0.0, pltpu.roll(strip, 1, 0))
    return up, down


def tap_plain(weights, a, b):
    at = (a * 3 + b) * CH
    return weights[at : at + CH, 0:CH]


def tap_transposed(turned_weights, a, b):
    at = ((2 - a) * 3 + 2 - b) * CH
    return turned_weights[at : at + CH, 0:CH]


def returned(me, edge, corner, count, width, turned_weights, vp, vm, hp, hm, adds, pieces=None, corners=None):
    def block(offset):
        return lax.rem(me + offset + 2 * count, count)

    adds[...] = jnp.zeros_like(adds)
    row = iota((SIDE, CH), 0)
    for side, offset, message in ((N, width, vm), (E, -1, hp), (S, -width, vp), (W, 1, hm)):
        code = code_at(edge, block(offset), side)
        flip = code >= 4
        strip = message[SIDE:STRIPS].astype(F32)
        up, down = neighbours(strip)
        joined = jnp.concatenate(
            [jnp.where(flip, down, up), strip, jnp.where(flip, up, down)], axis=1
        ).astype(BF16)
        if pieces is not None:
            pieces[side] = joined
        taps = jnp.concatenate(
            [tap_transposed(turned_weights, *edge_tap(side, k)) for k in range(3)], axis=0
        )
        at = lax.rem(code, 4)
        adds[at] = adds[at] + jnp.dot(joined, taps, preferred_element_type=F32)
    for q, offset, message, start in (
        (NW, width + 1, hm, STRIPS + 16),
        (NE, width - 1, hp, STRIPS + 16),
        (SE, -width - 1, hp, STRIPS),
        (SW, -width + 1, hm, STRIPS),
    ):
        code = code_at(corner, block(offset), q)
        cells = message[start : start + 16]
        if corners is not None:
            corners[q] = cells
        given = jnp.dot(
            cells, tap_transposed(turned_weights, *CORNER_TAP[q]), preferred_element_type=F32
        )[1:2]
        first = jnp.where(row == 0, given, 0.0)
        last = jnp.where(row == SIDE - 1, given, 0.0)
        adds[N] = adds[N] + jnp.where(code == NW, first, 0.0) + jnp.where(code == NE, last, 0.0)
        adds[S] = adds[S] + jnp.where(code == SW, first, 0.0) + jnp.where(code == SE, last, 0.0)


def with_adds(rows, i, adds, first=False, last=False):
    col = iota((8, CH), 0)
    rows = jnp.concatenate(
        [
            rows[0:8] + jnp.where(col == 0, adds[W, pl.ds(i, 1), :], 0.0),
            rows[8 : SIDE - 8],
            rows[SIDE - 8 :] + jnp.where(col == 7, adds[E, pl.ds(i, 1), :], 0.0),
        ],
        axis=0,
    )
    if first:
        rows = rows + adds[N]
    if last:
        rows = rows + adds[S]
    return rows


def pad_sides(vp, vm, hp, hm):
    return ((N, vp), (S, vm), (W, hp), (E, hm))


def pad_corners(hp, hm):
    return ((NW, hp, STRIPS), (NE, hm, STRIPS), (SE, hm, STRIPS + 16), (SW, hp, STRIPS + 16))


def received(weights, vp, vm, hp, hm, adds):
    row = iota((SIDE, CH), 0)
    for side, message in pad_sides(vp, vm, hp, hm):
        strip = message[0:SIDE].astype(F32)
        up, down = neighbours(strip)
        joined = jnp.concatenate([down, strip, up], axis=1).astype(BF16)
        taps = jnp.concatenate([tap_plain(weights, *edge_tap(side, k)) for k in range(3)], axis=0)
        adds[side] = jnp.dot(joined, taps, preferred_element_type=F32)
    for q, message, start in pad_corners(hp, hm):
        cells = message[start : start + 16]
        given = jnp.dot(cells, tap_plain(weights, *CORNER_TAP[q]), preferred_element_type=F32)[0:1]
        side = N if q in (NW, NE) else S
        place = 0 if q in (NW, SW) else SIDE - 1
        adds[side] = adds[side] + jnp.where(row == place, given, 0.0)


def pack_kernel(count, width, me, edge, corner, fields, upstream, va, vb, hp, hm, here, fore, back, vp, vm):
    here[...] = upstream[...]
    side_strips(fields, fore)
    side_strips(upstream, back)
    pack(me[0], edge, corner, count, width, fore, back, vp, vm, hp, hm)
    choose(even_row(me[0], width), vp, vm, va, vb)


def relay_kernel(width, me, one, two, hp, hm, vp, vm, ha, hb):
    choose(even_row(me[0], width), two, one, vp, vm)

    def send(even, right, left):
        @pl.when(even)
        def _():
            for own, dst, start in ((hp, right, STRIPS), (hm, left, STRIPS + 16)):
                dst[0:STRIPS] = own[...]
                dst[STRIPS : STRIPS + 16] = vp[start : start + 16]
                dst[STRIPS + 16 : VROWS] = vm[start : start + 16]

    even = even_column(me[0])
    send(even, ha, hb)
    send(jnp.logical_not(even), hb, ha)


def name_kernel(me, one, two, hp, hm):
    choose(even_column(me[0]), two, one, hp, hm)


def plain_weights(source, dst):
    zero = jnp.zeros((CH, CH), BF16)
    for b in range(3):
        for a in range(3):
            at = (a * 3 + b) * CH
            dst[at : at + CH, 0:CH] = source[a, b]
            dst[at + 3 * CH : at + 4 * CH, CH : 2 * CH] = source[a, b]
        dst[(9 + b) * CH : (10 + b) * CH, 0:CH] = zero
        dst[b * CH : (b + 1) * CH, CH : 2 * CH] = zero


def turned_weights(source, dst):
    zero = jnp.zeros((CH, CH), BF16)
    for b in range(3):
        for a in range(3):
            at = (a * 3 + b) * CH
            swapped = source[2 - a, 2 - b].astype(F32).T.astype(BF16)
            dst[at : at + CH, 0:CH] = swapped
            dst[at + 3 * CH : at + 4 * CH, CH : 2 * CH] = swapped
        dst[(9 + b) * CH : (10 + b) * CH, 0:CH] = zero
        dst[b * CH : (b + 1) * CH, CH : 2 * CH] = zero


def conv_all(copies, weights, dst):
    mb = 16

    def step(n, _):
        m = n * mb
        got = conv_pairs(copies, weights, m, mb)
        for part in range(2):
            lanes = slice(part * CH, (part + 1) * CH)
            dst[pl.ds(m, mb), part] = got[:, lanes].reshape(mb, SIDE, CH).astype(dst.dtype)
        return 0

    lax.fori_loop(0, HALF // mb, step, 0)


def back_kernel(token, kernel_two, upstream, in_two, up_copies, grad):
    turned_weights(kernel_two, in_two)
    zero_copies(up_copies, upstream)
    conv_all(up_copies, in_two, grad)


def fore_kernel(token, kernel_one, fields, fwd_one, copies, pre):
    plain_weights(kernel_one, fwd_one)
    zero_copies(copies, fields)
    conv_all(copies, fwd_one, pre)


def middle_kernel(
    count, width, me, edge, corner, vp, vm, one_side, other_side, fwd_one, in_two, pre, grad,
    hidden, grad_pre, va2, vb2, hp2, hm2, fore, back, pieces, corners, hp, hm,
    grad_adds, pre_adds, vp2, vm2,
):
    choose(even_column(me[0]), other_side, one_side, hp, hm)
    returned(me[0], edge, corner, count, width, in_two, vp, vm, hp, hm, grad_adds, pieces, corners)
    received(fwd_one, vp, vm, hp, hm, pre_adds)

    def one(m, part, first=False, last=False):
        i = 2 * m + part
        p = with_adds(pre[m, part], i, pre_adds, first, last)
        g = with_adds(grad[m, part], i, grad_adds, first, last)
        s = 1.0 / (1.0 + jnp.exp(-p))
        hidden[m, part] = (p * s).astype(BF16)
        grad_pre[m, part] = (g * s * (1.0 + p * (1.0 - s))).astype(BF16)

    def step(m, _):
        one(m, 0)
        one(m, 1)
        return 0

    one(0, 0, first=True)
    one(0, 1)
    lax.fori_loop(1, HALF - 1, step, 0, unroll=2)
    one(HALF - 1, 0)
    one(HALF - 1, 1, last=True)
    side_strips(hidden, fore)
    side_strips(grad_pre, back)
    pack(me[0], edge, corner, count, width, fore, back, vp2, vm2, hp2, hm2)
    choose(even_row(me[0], width), vp2, vm2, va2, vb2)


def sums_kernel(
    count, width, scale, kept, me, edge, corner, vp, vm, hp, hm, hidden, grad_pre, field_copies, up_copies,
    fore, back, pieces, corners, sums, acc,
):
    gb = 8
    first = (((0,), (0,)), ((), ()))

    def gather(values, shifted):
        def grad_step(n, _):
            m = n * gb
            left = jnp.concatenate(
                [values[pl.ds(m, gb), part].reshape(gb * SIDE, CH) for part in range(2)], axis=1
            )
            acc[...] += lax.dot_general(left, window(shifted, m, gb), first, preferred_element_type=F32)
            return 0

        acc[...] = jnp.zeros_like(acc)
        lax.fori_loop(0, HALF // gb, grad_step, 0)

    def from_acc(a, b):
        low = (a * 3 + b) * CH
        high = low + 3 * CH
        return acc[0:CH, low : low + CH] + acc[CH : 2 * CH, high : high + CH]

    def add(tap, term):
        at = (tap[0] * 3 + tap[1]) * CH
        sums[at : at + CH] = sums[at : at + CH] + term * scale

    def block(offset):
        return lax.rem(me[0] + offset + 2 * count, count)

    row = iota((16, CH), 0)
    high = (me[0] // FIRST) % 2

    @pl.when(high == (0 if kept else 1))
    def _():
        gather(grad_pre, field_copies)
        for a in range(3):
            for b in range(3):
                at = (a * 3 + b) * CH
                sums[at : at + CH] = from_acc(a, b).T * scale
        for side, message in pad_sides(vp, vm, hp, hm):
            strip = back[side]
            up, down = neighbours(strip)
            joined = jnp.concatenate([up, strip, down], axis=1).astype(BF16)
            term = lax.dot_general(message[0:SIDE], joined, first, preferred_element_type=F32)
            for k in range(3):
                add(edge_tap(side, k), term[:, k * CH : (k + 1) * CH])
        own = corner_rows(back)
        for q, message, start in pad_corners(hp, hm):
            right = jnp.where(row == 0, own[q], 0.0).astype(BF16)
            add(CORNER_TAP[q], lax.dot_general(message[start : start + 16], right, first, preferred_element_type=F32))

    @pl.when(high == (1 if kept else 0))
    def _():
        gather(hidden, up_copies)
        for a in range(3):
            for b in range(3):
                at = (a * 3 + b) * CH
                sums[at : at + CH] = from_acc(2 - a, 2 - b) * scale
        for side, offset in ((N, width), (E, -1), (S, -width), (W, 1)):
            code = lax.rem(code_at(edge, block(offset), side), 4)
            term = lax.dot_general(fore[code].astype(BF16), pieces[side], first, preferred_element_type=F32)
            for k in range(3):
                add(edge_tap(side, k), term[:, k * CH : (k + 1) * CH])
        own = corner_rows(fore)
        for q, offset in ((NW, width + 1), (NE, width - 1), (SE, -width - 1), (SW, -width + 1)):
            code = code_at(corner, block(offset), q)
            cell = jnp.where(code == 0, own[0], jnp.where(code == 1, own[1], jnp.where(code == 2, own[2], own[3])))
            left = jnp.where(row == 1, cell, 0.0).astype(BF16)
            add(CORNER_TAP[q], lax.dot_general(left, corners[q], first, preferred_element_type=F32))


def weights_kernel(token, kernel_one, kernel_two, in_one, fwd_two):
    turned_weights(kernel_one, in_one)
    plain_weights(kernel_two, fwd_two)


def outputs_kernel(hidden, vp, vm, hp, hm, fwd_two, outputs, copies, west, east):
    halo_copies(copies, hidden, west, east, vp, vm, hp, hm)
    conv_all(copies, fwd_two, outputs)


def grads_kernel(
    count, width, me, edge, corner, vp, vm, hp, hm, grad_pre, in_one, grad_fields, copies, adds
):
    mb = 8
    returned(me[0], edge, corner, count, width, in_one, vp, vm, hp, hm, adds)
    zero_copies(copies, grad_pre)

    def rows(n, first=False, last=False):
        m = n * mb
        got = conv_pairs(copies, in_one, m, mb)
        for k in range(mb):
            for part in range(2):
                g = with_adds(
                    got[k * SIDE : (k + 1) * SIDE, part * CH : (part + 1) * CH],
                    2 * (m + k) + part, adds,
                    first and k == 0 and part == 0, last and k == mb - 1 and part == 1,
                )
                grad_fields[m + k, part] = g.astype(BF16)

    def step(n, _):
        rows(n)
        return 0

    rows(0, first=True)
    lax.fori_loop(1, HALF // mb - 1, step, 0)
    rows(HALF // mb - 1, last=True)


def finish_kernel(me, mine, other, first, second):
    high = (me[0] // FIRST) % 2

    @pl.when(high == 0)
    def _():
        first[...] = mine[...].astype(F32)
        second[...] = other[...].astype(F32)

    @pl.when(high == 1)
    def _():
        first[...] = other[...].astype(F32)
        second[...] = mine[...].astype(F32)


def struct(shape, dtype=BF16):
    return jax.ShapeDtypeStruct(shape, dtype)


BLOCK = (HALF, 2, SIDE, CH)
COPIES = (3, HALF + 1, 2, SIDE, CH)
WEIGHTS = (12 * CH, 2 * CH)


def call(body, tables, arrays, outs, scratch=(), flops=0, moved=4 << 20):
    return pl.pallas_call(
        body,
        out_shape=outs,
        in_specs=[SMEM] * tables + [VMEM] * arrays,
        out_specs=tuple(VMEM for _ in outs),
        scratch_shapes=list(scratch),
        compiler_params=pltpu.CompilerParams(vmem_limit_bytes=ROOM),
        cost_estimate=pl.CostEstimate(flops=flops, bytes_accessed=moved, transcendentals=0),
    )


def swap(x, bit):
    size = lax.axis_size(AXES)
    return lax.ppermute(x, AXES, [(i, i ^ bit) for i in range(size)])


def both_ways(one, two, step):
    size = lax.axis_size(AXES)

    def pairs(turn):
        return [(i, (i + (step if (i // step + turn) % 2 == 0 else -step)) % size) for i in range(size)]

    return lax.ppermute(one, AXES, pairs(0)), lax.ppermute(two, AXES, pairs(1))


FIRST = 2
PLANE = (128, 64, 32, 1)
WHOLE = (4, 8, 16)


def plane_groups(size):
    mask = sum(PLANE)
    rest = [i for i in range(size) if i & mask == 0]
    members = [sum(bit for k, bit in enumerate(PLANE) if n >> k & 1) for n in range(1 << len(PLANE))]
    return [[base + member for member in members] for base in rest]


def total(send, done, works):
    me = lax.axis_index(AXES).astype(jnp.int32)
    groups = plane_groups(lax.axis_size(AXES))
    steps = [0]

    def scatter(sent):
        return lax.all_to_all(sent, AXES, 0, 0, axis_index_groups=groups, tiled=True)

    def beside(sent, bit):
        move = scatter if bit is None else lambda sent: swap(sent, bit)
        work = works.get(steps[0])
        steps[0] += 1
        if work is None:
            return move(sent)
        sent, held = lax.optimization_barrier((sent, done.copy()))
        done.update(held)
        got = move(sent)
        gave = work(done)
        got, gave = lax.optimization_barrier((got, gave))
        done.update(gave)
        return got

    x = beside(send, FIRST)
    x = done["keep"] + x
    parts = (len(groups[0]), x.shape[0] // len(groups[0]), CH)
    spread = beside(x.astype(BF16).reshape(parts), None)
    x = jnp.sum(spread.astype(F32), axis=0)
    for bit in WHOLE:
        x = x + beside(x, bit)
    spread = jnp.broadcast_to(x.astype(BF16)[None], parts)
    x = beside(spread, None).reshape(-1, CH)
    out = struct(x.shape, F32)
    grads = call(finish_kernel, 1, 2, (out, out))(me.reshape(1), x, beside(x, FIRST))
    return grads, done


def local(inputs, kernel_one, kernel_two, cotangent, edge_codes, corner_codes):
    count = lax.axis_size(AXES)
    width = lax.axis_size("face") // GRID_ROWS * lax.axis_size("sub")
    scale = 1.0 / math.sqrt(count * SIDE * SIDE)
    me = lax.axis_index(AXES).astype(jnp.int32).reshape(1)
    tables = (me, jnp.transpose(edge_codes, (1, 2, 0)), jnp.transpose(corner_codes, (1, 2, 0)))
    fields = inputs.reshape(BLOCK)
    upstream = cotangent.reshape(BLOCK)
    message = struct((VROWS, CH))
    own = struct((STRIPS, CH))
    weights = struct(WEIGHTS)
    block = struct(BLOCK)
    taps = struct((3, 3, CH, CH))
    copies = struct(COPIES)
    wide = struct(BLOCK, F32)
    sides = (4, SIDE, CH)
    strips = pltpu.VMEM(sides, F32)
    vertical_pair = pltpu.VMEM((VROWS, CH), BF16)
    column = pltpu.VMEM((SIDE, CH), F32)
    conv_flops = 2 * SIDE * SIDE * 9 * CH * CH

    va, vb, hp, hm, upstream = call(
        lambda *refs: pack_kernel(count, width, *refs), 3, 2, (message, message, own, own, block),
        [strips, strips, vertical_pair, vertical_pair],
    )(*tables, fields, upstream)
    va, vb, token = lax.optimization_barrier((va, vb, me))
    va, vb = both_ways(va, vb, width)
    in_two, up_copies, grad = call(back_kernel, 1, 2, (weights, copies, wide), (), conv_flops)(
        token, kernel_two, upstream
    )
    va, vb, in_two, up_copies, grad, token = lax.optimization_barrier(
        (va, vb, in_two, up_copies, grad, token)
    )

    def relay(token, va, vb, hp, hm):
        return call(
            lambda *refs: relay_kernel(width, *refs), 1, 4, (message, message, message, message), (), 0, 1 << 18
        )(token, va, vb, hp, hm)

    vp, vm, ha, hb = relay(token, va, vb, hp, hm)
    ha, hb, token = lax.optimization_barrier((ha, hb, token))
    ha, hb = both_ways(ha, hb, 1)
    fwd_one, field_copies, pre = call(fore_kernel, 1, 2, (weights, copies, wide), (), conv_flops)(
        token, kernel_one, fields
    )
    hidden, grad_pre, va2, vb2, hp2, hm2, fore, back, pieces, corners, hp, hm = call(
        lambda *refs: middle_kernel(count, width, *refs), 3, 8,
        (
            block, block, message, message, own, own, struct(sides, F32), struct(sides, F32),
            struct((4, SIDE, 3 * CH)), struct((4, 16, CH)),
            message, message,
        ),
        [strips, strips, vertical_pair, vertical_pair], conv_flops,
    )(*tables, vp, vm, ha, hb, fwd_one, in_two, pre, grad)
    hidden, grad_pre, va2, vb2, token = lax.optimization_barrier((hidden, grad_pre, va2, vb2, token))
    in_one, fwd_two = call(weights_kernel, 1, 2, (weights, weights))(token, kernel_one, kernel_two)
    def half(kept, token):
        got, = call(
            lambda me, *refs: sums_kernel(count, width, scale, kept, me, *refs), 3, 12,
            (struct((9 * CH, CH), F32),), [pltpu.VMEM((2 * CH, 12 * CH), F32)], conv_flops,
        )(
            token, *tables[1:], vp, vm, hp, hm, hidden, grad_pre, field_copies, up_copies,
            fore, back, pieces, corners,
        )
        return got

    def keep_half(done):
        return dict(keep=half(True, done["token"]))

    def second_round(done):
        va, vb = both_ways(done["va"], done["vb"], width)
        vp, vm, ha, hb = relay(me, va, vb, hp2, hm2)
        ha, hb = both_ways(ha, hb, 1)
        hp, hm = call(name_kernel, 1, 2, (message, message), (), 0, 1 << 18)(me, ha, hb)
        return dict(vp=vp, vm=vm, hp=hp, hm=hm)

    def messages(done):
        return done["vp"], done["vm"], done["hp"], done["hm"]

    def make_outputs(done):
        outputs, = call(
            outputs_kernel, 0, 6, (block,), [pltpu.VMEM(COPIES, BF16), column, column], conv_flops
        )(hidden, *messages(done), fwd_two)
        return dict(outputs=outputs)

    def make_grads(done):
        grad_fields, = call(
            lambda *refs: grads_kernel(count, width, *refs), 3, 6, (block,),
            [pltpu.VMEM(COPIES, BF16), strips], conv_flops,
        )(*tables, *messages(done), grad_pre, in_one)
        return dict(grad_fields=grad_fields)

    grads, done = total(
        half(False, token), dict(va=va2, vb=vb2, token=token),
        {0: keep_half, 1: second_round, 2: make_outputs, 3: make_grads},
    )
    shape = (1, 1, SIDE, SIDE, CH)
    return (
        done["outputs"].reshape(shape), done["grad_fields"].reshape(shape),
        grads[0].reshape(taps.shape), grads[1].reshape(taps.shape),
    )


def solution(mesh):
    block = P("face", "sub", None, None, None)
    return jax.shard_map(
        local,
        mesh=mesh,
        in_specs=(block, P(), P(), block, P(), P()),
        out_specs=(block, block, P(), P()),
        check_vma=False,
    )
```

```python
import math

import jax
import jax.numpy as jnp
from jax import lax
from jax.experimental import pallas as pl
from jax.experimental.pallas import tpu as pltpu
from jax.sharding import PartitionSpec as P

AXES = ("face", "sub")
GRID_ROWS = 8
SIDE = 64
CH = 128
HALF = SIDE // 2
STRIPS = 2 * SIDE
VROWS = STRIPS + 32
BF16 = jnp.bfloat16
F32 = jnp.float32
N, E, S, W = 0, 1, 2, 3
NW, NE, SE, SW = 0, 1, 2, 3
VMEM = pl.BlockSpec(memory_space=pltpu.VMEM)
SMEM = pl.BlockSpec(memory_space=pltpu.SMEM)
ROOM = 20 << 20


def code_at(table, block, which):
    return table[block % 2, which, block // 2]


def iota(shape, dim):
    return lax.broadcasted_iota(jnp.int32, shape, dim)


def strips_from(north, south, low, high, dst):
    dst[N] = north.astype(F32)
    dst[S] = south.astype(F32)
    low = low.reshape(SIDE, 16, CH).astype(F32)
    dst[W] = jnp.sum(jnp.where(iota(low.shape, 1) == 0, low, 0.0), axis=1)
    high = high.reshape(SIDE, 16, CH).astype(F32)
    dst[E] = jnp.sum(jnp.where(iota(high.shape, 1) == 15, high, 0.0), axis=1)


def side_strips(block, dst):
    strips_from(
        block[0, 0], block[HALF - 1, 1], block[:, :, 0:16, :], block[:, :, SIDE - 16 : SIDE, :], dst
    )


def corner_rows(strips):
    north = strips[N]
    south = strips[S]
    last = SIDE - 1
    return [north[0:1], north[last : last + 1], south[last : last + 1], south[0:1]]


def turned(strip, flip):
    row = iota((SIDE, SIDE), 0)
    col = iota((SIDE, SIDE), 1)
    target = jnp.where(flip, SIDE - 1 - row, row)
    matrix = jnp.where(col == target, 1.0, 0.0).astype(BF16)
    return jnp.dot(matrix, strip.astype(BF16), preferred_element_type=F32).astype(BF16)


def corner_block(code, own, other):
    picked = jnp.where(code == 0, own[0], jnp.where(code == 1, own[1], jnp.where(code == 2, own[2], own[3])))
    row = iota((16, CH), 0)
    return (jnp.where(row == 0, picked, 0.0) + jnp.where(row == 1, other, 0.0)).astype(BF16)


def pack(me, edge, corner, count, width, fore, back, vp, vm, hp, hm):
    fore_corners = corner_rows(fore)
    back_corners = corner_rows(back)

    def block(offset):
        return lax.rem(me + offset + 2 * count, count)

    def strips(dst, offset, read_side, own_side):
        code = code_at(edge, block(offset), read_side)
        dst[0:SIDE] = turned(fore[lax.rem(code, 4)], code >= 4)
        dst[SIDE:STRIPS] = turned(back[own_side], code_at(edge, me, own_side) >= 4)

    def relayed(offset, read_corner, own_corner):
        return corner_block(
            code_at(corner, block(offset), read_corner), fore_corners, back_corners[own_corner]
        )

    strips(vp, width, N, S)
    vp[STRIPS : STRIPS + 16] = relayed(width + 1, NW, SE)
    vp[STRIPS + 16 : VROWS] = relayed(width - 1, NE, SW)
    strips(vm, -width, S, N)
    vm[STRIPS : STRIPS + 16] = relayed(-width + 1, SW, NE)
    vm[STRIPS + 16 : VROWS] = relayed(-width - 1, SE, NW)
    strips(hp, 1, W, E)
    strips(hm, -1, E, W)


def choose(even, one, two, ahead, behind):
    @pl.when(even)
    def _():
        ahead[...] = one[...]
        behind[...] = two[...]

    @pl.when(jnp.logical_not(even))
    def _():
        ahead[...] = two[...]
        behind[...] = one[...]


def even_row(me, width):
    return (me // width) % 2 == 0


def even_column(me):
    return me % 2 == 0


def put_row(dst, pair, part, row, west, east):
    col = iota((SIDE, CH), 0)
    wide = row.astype(F32)
    dst[1, pair, part] = row.astype(BF16)
    dst[0, pair, part] = jnp.where(col == 0, west, pltpu.roll(wide, 1, 0)).astype(BF16)
    dst[2, pair, part] = jnp.where(col == SIDE - 1, east, pltpu.roll(wide, SIDE - 1, 0)).astype(BF16)


def shift_copies(dst, src, west=None, east=None):
    def step(k, _):
        for part in range(2):
            i = 2 * k + part
            w = 0.0 if west is None else west[pl.ds(i, 1), :]
            e = 0.0 if east is None else east[pl.ds(i, 1), :]
            put_row(dst, k + part, 1 - part, src[k, part], w, e)
        return 0

    lax.fori_loop(0, HALF, step, 0, unroll=4)


def halo_copies(dst, src, west, east, vp, vm, hp, hm):
    west[...] = hp[0:SIDE].astype(F32)
    east[...] = hm[0:SIDE].astype(F32)
    shift_copies(dst, src, west, east)
    hp1 = hp[STRIPS : STRIPS + 16].astype(F32)
    hp2 = hp[STRIPS + 16 : VROWS].astype(F32)
    hm1 = hm[STRIPS : STRIPS + 16].astype(F32)
    hm2 = hm[STRIPS + 16 : VROWS].astype(F32)
    put_row(dst, 0, 0, vp[0:SIDE], hp1[0:1], hm1[0:1])
    put_row(dst, HALF, 1, vm[0:SIDE], hp2[0:1], hm2[0:1])


def zero_copies(dst, src):
    zero = jnp.zeros((SIDE, CH), BF16)
    for b in range(3):
        dst[b, 0, 0] = zero
        dst[b, HALF, 1] = zero
    shift_copies(dst, src)


def window(copies, m, mb):
    parts = [
        copies[b, pl.ds(m + a // 2, mb), a % 2].reshape(mb * SIDE, CH)
        for a in range(4)
        for b in range(3)
    ]
    return jnp.concatenate(parts, axis=1)


def conv_pairs(copies, weights, m, mb):
    return jnp.dot(window(copies, m, mb), weights[...], preferred_element_type=F32)


def edge_tap(side, k):
    return {N: (0, k), S: (2, k), W: (k, 0), E: (k, 2)}[side]


CORNER_TAP = {NW: (0, 0), NE: (0, 2), SE: (2, 2), SW: (2, 0)}


def neighbours(strip):
    row = iota((SIDE, CH), 0)
    up = jnp.where(row == SIDE - 1, 0.0, pltpu.roll(strip, SIDE - 1, 0))
    down = jnp.where(row == 0, 0.0, pltpu.roll(strip, 1, 0))
    return up, down


def tap_plain(weights, a, b):
    at = (a * 3 + b) * CH
    return weights[at : at + CH, 0:CH]


def tap_transposed(turned_weights, a, b):
    at = ((2 - a) * 3 + 2 - b) * CH
    return turned_weights[at : at + CH, 0:CH]


def returned(me, edge, corner, count, width, turned_weights, vp, vm, hp, hm, adds, pieces=None, corners=None):
    def block(offset):
        return lax.rem(me + offset + 2 * count, count)

    adds[...] = jnp.zeros_like(adds)
    row = iota((SIDE, CH), 0)
    for side, offset, message in ((N, width, vm), (E, -1, hp), (S, -width, vp), (W, 1, hm)):
        code = code_at(edge, block(offset), side)
        flip = code >= 4
        strip = message[SIDE:STRIPS].astype(F32)
        up, down = neighbours(strip)
        joined = jnp.concatenate(
            [jnp.where(flip, down, up), strip, jnp.where(flip, up, down)], axis=1
        ).astype(BF16)
        if pieces is not None:
            pieces[side] = joined
        taps = jnp.concatenate(
            [tap_transposed(turned_weights, *edge_tap(side, k)) for k in range(3)], axis=0
        )
        at = lax.rem(code, 4)
        adds[at] = adds[at] + jnp.dot(joined, taps, preferred_element_type=F32)
    for q, offset, message, start in (
        (NW, width + 1, hm, STRIPS + 16),
        (NE, width - 1, hp, STRIPS + 16),
        (SE, -width - 1, hp, STRIPS),
        (SW, -width + 1, hm, STRIPS),
    ):
        code = code_at(corner, block(offset), q)
        cells = message[start : start + 16]
        if corners is not None:
            corners[q] = cells
        given = jnp.dot(
            cells, tap_transposed(turned_weights, *CORNER_TAP[q]), preferred_element_type=F32
        )[1:2]
        first = jnp.where(row == 0, given, 0.0)
        last = jnp.where(row == SIDE - 1, given, 0.0)
        adds[N] = adds[N] + jnp.where(code == NW, first, 0.0) + jnp.where(code == NE, last, 0.0)
        adds[S] = adds[S] + jnp.where(code == SW, first, 0.0) + jnp.where(code == SE, last, 0.0)


def with_adds(rows, i, adds, first=False, last=False):
    col = iota((8, CH), 0)
    rows = jnp.concatenate(
        [
            rows[0:8] + jnp.where(col == 0, adds[W, pl.ds(i, 1), :], 0.0),
            rows[8 : SIDE - 8],
            rows[SIDE - 8 :] + jnp.where(col == 7, adds[E, pl.ds(i, 1), :], 0.0),
        ],
        axis=0,
    )
    if first:
        rows = rows + adds[N]
    if last:
        rows = rows + adds[S]
    return rows


def pad_sides(vp, vm, hp, hm):
    return ((N, vp), (S, vm), (W, hp), (E, hm))


def pad_corners(hp, hm):
    return ((NW, hp, STRIPS), (NE, hm, STRIPS), (SE, hm, STRIPS + 16), (SW, hp, STRIPS + 16))


def received(weights, vp, vm, hp, hm, adds):
    row = iota((SIDE, CH), 0)
    for side, message in pad_sides(vp, vm, hp, hm):
        strip = message[0:SIDE].astype(F32)
        up, down = neighbours(strip)
        joined = jnp.concatenate([down, strip, up], axis=1).astype(BF16)
        taps = jnp.concatenate([tap_plain(weights, *edge_tap(side, k)) for k in range(3)], axis=0)
        adds[side] = jnp.dot(joined, taps, preferred_element_type=F32)
    for q, message, start in pad_corners(hp, hm):
        cells = message[start : start + 16]
        given = jnp.dot(cells, tap_plain(weights, *CORNER_TAP[q]), preferred_element_type=F32)[0:1]
        side = N if q in (NW, NE) else S
        place = 0 if q in (NW, SW) else SIDE - 1
        adds[side] = adds[side] + jnp.where(row == place, given, 0.0)


def pack_kernel(count, width, me, edge, corner, fields, upstream, va, vb, hp, hm, here, fore, back, vp, vm):
    here[...] = upstream[...]
    side_strips(fields, fore)
    side_strips(upstream, back)
    pack(me[0], edge, corner, count, width, fore, back, vp, vm, hp, hm)
    choose(even_row(me[0], width), vp, vm, va, vb)


def relay_kernel(width, me, one, two, hp, hm, vp, vm, ha, hb):
    choose(even_row(me[0], width), two, one, vp, vm)

    def send(even, right, left):
        @pl.when(even)
        def _():
            for own, dst, start in ((hp, right, STRIPS), (hm, left, STRIPS + 16)):
                dst[0:STRIPS] = own[...]
                dst[STRIPS : STRIPS + 16] = vp[start : start + 16]
                dst[STRIPS + 16 : VROWS] = vm[start : start + 16]

    even = even_column(me[0])
    send(even, ha, hb)
    send(jnp.logical_not(even), hb, ha)


def name_kernel(me, one, two, hp, hm):
    choose(even_column(me[0]), two, one, hp, hm)


def plain_weights(source, dst):
    zero = jnp.zeros((CH, CH), BF16)
    for b in range(3):
        for a in range(3):
            at = (a * 3 + b) * CH
            dst[at : at + CH, 0:CH] = source[a, b]
            dst[at + 3 * CH : at + 4 * CH, CH : 2 * CH] = source[a, b]
        dst[(9 + b) * CH : (10 + b) * CH, 0:CH] = zero
        dst[b * CH : (b + 1) * CH, CH : 2 * CH] = zero


def turned_weights(source, dst):
    zero = jnp.zeros((CH, CH), BF16)
    for b in range(3):
        for a in range(3):
            at = (a * 3 + b) * CH
            swapped = source[2 - a, 2 - b].astype(F32).T.astype(BF16)
            dst[at : at + CH, 0:CH] = swapped
            dst[at + 3 * CH : at + 4 * CH, CH : 2 * CH] = swapped
        dst[(9 + b) * CH : (10 + b) * CH, 0:CH] = zero
        dst[b * CH : (b + 1) * CH, CH : 2 * CH] = zero


def conv_all(copies, weights, dst):
    mb = 16

    def step(n, _):
        m = n * mb
        got = conv_pairs(copies, weights, m, mb)
        for part in range(2):
            lanes = slice(part * CH, (part + 1) * CH)
            dst[pl.ds(m, mb), part] = got[:, lanes].reshape(mb, SIDE, CH).astype(dst.dtype)
        return 0

    lax.fori_loop(0, HALF // mb, step, 0)


def back_kernel(token, kernel_two, upstream, in_two, up_copies, grad):
    turned_weights(kernel_two, in_two)
    zero_copies(up_copies, upstream)
    conv_all(up_copies, in_two, grad)


def fore_kernel(token, kernel_one, fields, fwd_one, copies, pre):
    plain_weights(kernel_one, fwd_one)
    zero_copies(copies, fields)
    conv_all(copies, fwd_one, pre)


def middle_kernel(
    count, width, me, edge, corner, vp, vm, one_side, other_side, fwd_one, in_two, pre, grad,
    hidden, grad_pre, va2, vb2, hp2, hm2, fore, back, pieces, corners, hp, hm,
    grad_adds, pre_adds, vp2, vm2,
):
    choose(even_column(me[0]), other_side, one_side, hp, hm)
    returned(me[0], edge, corner, count, width, in_two, vp, vm, hp, hm, grad_adds, pieces, corners)
    received(fwd_one, vp, vm, hp, hm, pre_adds)

    def one(m, part, first=False, last=False):
        i = 2 * m + part
        p = with_adds(pre[m, part], i, pre_adds, first, last)
        g = with_adds(grad[m, part], i, grad_adds, first, last)
        s = 1.0 / (1.0 + jnp.exp(-p))
        hidden[m, part] = (p * s).astype(BF16)
        grad_pre[m, part] = (g * s * (1.0 + p * (1.0 - s))).astype(BF16)

    def step(m, _):
        one(m, 0)
        one(m, 1)
        return 0

    one(0, 0, first=True)
    one(0, 1)
    lax.fori_loop(1, HALF - 1, step, 0, unroll=2)
    one(HALF - 1, 0)
    one(HALF - 1, 1, last=True)
    side_strips(hidden, fore)
    side_strips(grad_pre, back)
    pack(me[0], edge, corner, count, width, fore, back, vp2, vm2, hp2, hm2)
    choose(even_row(me[0], width), vp2, vm2, va2, vb2)


def sums_kernel(
    count, width, scale, kept, me, edge, corner, vp, vm, hp, hm, hidden, grad_pre, field_copies, up_copies,
    fore, back, pieces, corners, sums, acc,
):
    gb = 8
    first = (((0,), (0,)), ((), ()))

    def gather(values, shifted):
        def grad_step(n, _):
            m = n * gb
            left = jnp.concatenate(
                [values[pl.ds(m, gb), part].reshape(gb * SIDE, CH) for part in range(2)], axis=1
            )
            acc[...] += lax.dot_general(left, window(shifted, m, gb), first, preferred_element_type=F32)
            return 0

        acc[...] = jnp.zeros_like(acc)
        lax.fori_loop(0, HALF // gb, grad_step, 0)

    def from_acc(a, b):
        low = (a * 3 + b) * CH
        high = low + 3 * CH
        return acc[0:CH, low : low + CH] + acc[CH : 2 * CH, high : high + CH]

    def add(tap, term):
        at = (tap[0] * 3 + tap[1]) * CH
        sums[at : at + CH] = sums[at : at + CH] + term * scale

    def block(offset):
        return lax.rem(me[0] + offset + 2 * count, count)

    row = iota((16, CH), 0)
    high = (me[0] // FIRST) % 2

    @pl.when(high == (0 if kept else 1))
    def _():
        gather(grad_pre, field_copies)
        for a in range(3):
            for b in range(3):
                at = (a * 3 + b) * CH
                sums[at : at + CH] = from_acc(a, b).T * scale
        for side, message in pad_sides(vp, vm, hp, hm):
            strip = back[side]
            up, down = neighbours(strip)
            joined = jnp.concatenate([up, strip, down], axis=1).astype(BF16)
            term = lax.dot_general(message[0:SIDE], joined, first, preferred_element_type=F32)
            for k in range(3):
                add(edge_tap(side, k), term[:, k * CH : (k + 1) * CH])
        own = corner_rows(back)
        for q, message, start in pad_corners(hp, hm):
            right = jnp.where(row == 0, own[q], 0.0).astype(BF16)
            add(CORNER_TAP[q], lax.dot_general(message[start : start + 16], right, first, preferred_element_type=F32))

    @pl.when(high == (1 if kept else 0))
    def _():
        gather(hidden, up_copies)
        for a in range(3):
            for b in range(3):
                at = (a * 3 + b) * CH
                sums[at : at + CH] = from_acc(2 - a, 2 - b) * scale
        for side, offset in ((N, width), (E, -1), (S, -width), (W, 1)):
            code = lax.rem(code_at(edge, block(offset), side), 4)
            term = lax.dot_general(fore[code].astype(BF16), pieces[side], first, preferred_element_type=F32)
            for k in range(3):
                add(edge_tap(side, k), term[:, k * CH : (k + 1) * CH])
        own = corner_rows(fore)
        for q, offset in ((NW, width + 1), (NE, width - 1), (SE, -width - 1), (SW, -width + 1)):
            code = code_at(corner, block(offset), q)
            cell = jnp.where(code == 0, own[0], jnp.where(code == 1, own[1], jnp.where(code == 2, own[2], own[3])))
            left = jnp.where(row == 1, cell, 0.0).astype(BF16)
            add(CORNER_TAP[q], lax.dot_general(left, corners[q], first, preferred_element_type=F32))


def weights_kernel(token, kernel_one, kernel_two, in_one, fwd_two):
    turned_weights(kernel_one, in_one)
    plain_weights(kernel_two, fwd_two)


def outputs_kernel(hidden, vp, vm, hp, hm, fwd_two, outputs, copies, west, east):
    halo_copies(copies, hidden, west, east, vp, vm, hp, hm)
    conv_all(copies, fwd_two, outputs)


def grads_kernel(
    count, width, me, edge, corner, vp, vm, hp, hm, grad_pre, in_one, grad_fields, copies, adds
):
    mb = 8
    returned(me[0], edge, corner, count, width, in_one, vp, vm, hp, hm, adds)
    zero_copies(copies, grad_pre)

    def rows(n, first=False, last=False):
        m = n * mb
        got = conv_pairs(copies, in_one, m, mb)
        for k in range(mb):
            for part in range(2):
                g = with_adds(
                    got[k * SIDE : (k + 1) * SIDE, part * CH : (part + 1) * CH],
                    2 * (m + k) + part, adds,
                    first and k == 0 and part == 0, last and k == mb - 1 and part == 1,
                )
                grad_fields[m + k, part] = g.astype(BF16)

    def step(n, _):
        rows(n)
        return 0

    rows(0, first=True)
    lax.fori_loop(1, HALF // mb - 1, step, 0)
    rows(HALF // mb - 1, last=True)


def fold_kernel(parts, total):
    total[...] = jnp.sum(parts[...].astype(F32), axis=0)


def finish_kernel(me, mine, other, first, second):
    high = (me[0] // FIRST) % 2

    @pl.when(high == 0)
    def _():
        first[...] = mine[...].astype(F32)
        second[...] = other[...].astype(F32)

    @pl.when(high == 1)
    def _():
        first[...] = other[...].astype(F32)
        second[...] = mine[...].astype(F32)


def struct(shape, dtype=BF16):
    return jax.ShapeDtypeStruct(shape, dtype)


BLOCK = (HALF, 2, SIDE, CH)
COPIES = (3, HALF + 1, 2, SIDE, CH)
WEIGHTS = (12 * CH, 2 * CH)


def call(body, tables, arrays, outs, scratch=(), flops=0, moved=4 << 20):
    return pl.pallas_call(
        body,
        out_shape=outs,
        in_specs=[SMEM] * tables + [VMEM] * arrays,
        out_specs=tuple(VMEM for _ in outs),
        scratch_shapes=list(scratch),
        compiler_params=pltpu.CompilerParams(vmem_limit_bytes=ROOM),
        cost_estimate=pl.CostEstimate(flops=flops, bytes_accessed=moved, transcendentals=0),
    )


def swap(x, bit):
    size = lax.axis_size(AXES)
    return lax.ppermute(x, AXES, [(i, i ^ bit) for i in range(size)])


def both_ways(one, two, step):
    size = lax.axis_size(AXES)

    def pairs(turn):
        return [(i, (i + (step if (i // step + turn) % 2 == 0 else -step)) % size) for i in range(size)]

    return lax.ppermute(one, AXES, pairs(0)), lax.ppermute(two, AXES, pairs(1))


FIRST = 2
PLANE = (128, 64, 32, 1)
WHOLE = (4, 8, 16)


def plane_groups(size):
    mask = sum(PLANE)
    rest = [i for i in range(size) if i & mask == 0]
    members = [sum(bit for k, bit in enumerate(PLANE) if n >> k & 1) for n in range(1 << len(PLANE))]
    return [[base + member for member in members] for base in rest]


def total(send, done, works):
    me = lax.axis_index(AXES).astype(jnp.int32)
    groups = plane_groups(lax.axis_size(AXES))
    steps = [0]
    free = {}

    def scatter(sent):
        return lax.all_to_all(sent, AXES, 0, 0, axis_index_groups=groups, tiled=True)

    def beside(sent, bit):
        move = scatter if bit is None else lambda sent: swap(sent, bit)
        work = works.get(steps[0])
        steps[0] += 1
        if work is None:
            return move(sent)
        sent, held = lax.optimization_barrier((sent, done.copy()))
        done.update(held)
        got = move(sent)
        gave, loose = work(done, free)
        got, gave = lax.optimization_barrier((got, gave))
        done.update(gave)
        free.update(loose)
        return got

    x = beside(send, FIRST)
    x = done["keep"] + x
    parts = (len(groups[0]), x.shape[0] // len(groups[0]), CH)
    spread = beside(x.astype(BF16).reshape(parts), None)
    x, = call(fold_kernel, 0, 1, (struct(parts[1:], F32),), (), 0, 1 << 19)(spread)
    for bit in WHOLE:
        x = x + beside(x, bit)
    spread = jnp.broadcast_to(x.astype(BF16)[None], parts)
    x = beside(spread, None).reshape(-1, CH)
    out = struct(x.shape, F32)
    grads = call(finish_kernel, 1, 2, (out, out))(me.reshape(1), x, beside(x, FIRST))
    return grads, done


def local(inputs, kernel_one, kernel_two, cotangent, edge_codes, corner_codes):
    count = lax.axis_size(AXES)
    width = lax.axis_size("face") // GRID_ROWS * lax.axis_size("sub")
    scale = 1.0 / math.sqrt(count * SIDE * SIDE)
    me = lax.axis_index(AXES).astype(jnp.int32).reshape(1)
    tables = (me, jnp.transpose(edge_codes, (1, 2, 0)), jnp.transpose(corner_codes, (1, 2, 0)))
    fields = inputs.reshape(BLOCK)
    upstream = cotangent.reshape(BLOCK)
    message = struct((VROWS, CH))
    own = struct((STRIPS, CH))
    weights = struct(WEIGHTS)
    block = struct(BLOCK)
    taps = struct((3, 3, CH, CH))
    copies = struct(COPIES)
    wide = struct(BLOCK, F32)
    sides = (4, SIDE, CH)
    strips = pltpu.VMEM(sides, F32)
    vertical_pair = pltpu.VMEM((VROWS, CH), BF16)
    column = pltpu.VMEM((SIDE, CH), F32)
    conv_flops = 2 * SIDE * SIDE * 9 * CH * CH

    va, vb, hp, hm, upstream = call(
        lambda *refs: pack_kernel(count, width, *refs), 3, 2, (message, message, own, own, block),
        [strips, strips, vertical_pair, vertical_pair],
    )(*tables, fields, upstream)
    va, vb, token = lax.optimization_barrier((va, vb, me))
    va, vb = both_ways(va, vb, width)
    in_two, up_copies, grad = call(back_kernel, 1, 2, (weights, copies, wide), (), conv_flops)(
        token, kernel_two, upstream
    )
    va, vb, in_two, up_copies, grad, token = lax.optimization_barrier(
        (va, vb, in_two, up_copies, grad, token)
    )

    def relay(token, va, vb, hp, hm):
        return call(
            lambda *refs: relay_kernel(width, *refs), 1, 4, (message, message, message, message), (), 0, 1 << 18
        )(token, va, vb, hp, hm)

    vp, vm, ha, hb = relay(token, va, vb, hp, hm)
    ha, hb, token = lax.optimization_barrier((ha, hb, token))
    ha, hb = both_ways(ha, hb, 1)
    fwd_one, field_copies, pre = call(fore_kernel, 1, 2, (weights, copies, wide), (), conv_flops)(
        token, kernel_one, fields
    )
    hidden, grad_pre, va2, vb2, hp2, hm2, fore, back, pieces, corners, hp, hm = call(
        lambda *refs: middle_kernel(count, width, *refs), 3, 8,
        (
            block, block, message, message, own, own, struct(sides, F32), struct(sides, F32),
            struct((4, SIDE, 3 * CH)), struct((4, 16, CH)),
            message, message,
        ),
        [strips, strips, vertical_pair, vertical_pair], conv_flops,
    )(*tables, vp, vm, ha, hb, fwd_one, in_two, pre, grad)
    hidden, grad_pre, va2, vb2, token = lax.optimization_barrier((hidden, grad_pre, va2, vb2, token))
    def half(kept, token):
        got, = call(
            lambda me, *refs: sums_kernel(count, width, scale, kept, me, *refs), 3, 12,
            (struct((9 * CH, CH), F32),), [pltpu.VMEM((2 * CH, 12 * CH), F32)], conv_flops,
        )(
            token, *tables[1:], vp, vm, hp, hm, hidden, grad_pre, field_copies, up_copies,
            fore, back, pieces, corners,
        )
        return got

    def first_work(done, free):
        va, vb = both_ways(done["va"], done["vb"], width)
        return dict(keep=half(True, done["token"]), va=va, vb=vb), {}

    def second_work(done, free):
        vp, vm, ha, hb = relay(done["token"], done["va"], done["vb"], hp2, hm2)
        ha, hb = both_ways(ha, hb, 1)
        return {}, dict(vp=vp, vm=vm, ha=ha, hb=hb)

    def third_work(done, free):
        hp, hm = call(name_kernel, 1, 2, (message, message), (), 0, 1 << 18)(
            done["token"], free["ha"], free["hb"]
        )
        in_one, fwd_two = call(weights_kernel, 1, 2, (weights, weights))(
            done["token"], kernel_one, kernel_two
        )
        return dict(in_one=in_one, fwd_two=fwd_two, hp=hp, hm=hm), {}

    def messages(done, free):
        return free["vp"], free["vm"], done["hp"], done["hm"]

    def make_outputs(done, free):
        outputs, = call(
            outputs_kernel, 0, 6, (block,), [pltpu.VMEM(COPIES, BF16), column, column], conv_flops
        )(hidden, *messages(done, free), done["fwd_two"])
        return dict(outputs=outputs), {}

    def make_grads(done, free):
        grad_fields, = call(
            lambda *refs: grads_kernel(count, width, *refs), 3, 6, (block,),
            [pltpu.VMEM(COPIES, BF16), strips], conv_flops,
        )(*tables, *messages(done, free), grad_pre, done["in_one"])
        return dict(grad_fields=grad_fields), {}

    grads, done = total(
        half(False, token), dict(va=va2, vb=vb2, token=token),
        {0: first_work, 1: second_work, 2: third_work, 3: make_outputs, 4: make_grads},
    )
    shape = (1, 1, SIDE, SIDE, CH)
    return (
        done["outputs"].reshape(shape), done["grad_fields"].reshape(shape),
        grads[0].reshape(taps.shape), grads[1].reshape(taps.shape),
    )


def solution(mesh):
    block = P("face", "sub", None, None, None)
    return jax.shard_map(
        local,
        mesh=mesh,
        in_specs=(block, P(), P(), block, P(), P()),
        out_specs=(block, block, P(), P()),
        check_vma=False,
    )
```

```python
import math

import jax
import jax.numpy as jnp
from jax import lax
from jax.experimental import pallas as pl
from jax.experimental.pallas import tpu as pltpu
from jax.sharding import PartitionSpec as P

AXES = ("face", "sub")
GRID_ROWS = 8
SIDE = 64
CH = 128
HALF = SIDE // 2
STRIPS = 2 * SIDE
VROWS = STRIPS + 32
BF16 = jnp.bfloat16
F32 = jnp.float32
N, E, S, W = 0, 1, 2, 3
NW, NE, SE, SW = 0, 1, 2, 3
VMEM = pl.BlockSpec(memory_space=pltpu.VMEM)
SMEM = pl.BlockSpec(memory_space=pltpu.SMEM)
ROOM = 20 << 20


def code_at(table, block, which):
    return table[block % 2, which, block // 2]


def iota(shape, dim):
    return lax.broadcasted_iota(jnp.int32, shape, dim)


def strips_from(north, south, low, high, dst):
    dst[N] = north.astype(F32)
    dst[S] = south.astype(F32)
    low = low.reshape(SIDE, 16, CH).astype(F32)
    dst[W] = jnp.sum(jnp.where(iota(low.shape, 1) == 0, low, 0.0), axis=1)
    high = high.reshape(SIDE, 16, CH).astype(F32)
    dst[E] = jnp.sum(jnp.where(iota(high.shape, 1) == 15, high, 0.0), axis=1)


def side_strips(block, dst):
    strips_from(
        block[0, 0], block[HALF - 1, 1], block[:, :, 0:16, :], block[:, :, SIDE - 16 : SIDE, :], dst
    )


def corner_rows(strips):
    north = strips[N]
    south = strips[S]
    last = SIDE - 1
    return [north[0:1], north[last : last + 1], south[last : last + 1], south[0:1]]


def turned(strip, flip):
    row = iota((SIDE, SIDE), 0)
    col = iota((SIDE, SIDE), 1)
    target = jnp.where(flip, SIDE - 1 - row, row)
    matrix = jnp.where(col == target, 1.0, 0.0).astype(BF16)
    return jnp.dot(matrix, strip.astype(BF16), preferred_element_type=F32).astype(BF16)


def corner_block(code, own, other):
    picked = jnp.where(code == 0, own[0], jnp.where(code == 1, own[1], jnp.where(code == 2, own[2], own[3])))
    row = iota((16, CH), 0)
    return (jnp.where(row == 0, picked, 0.0) + jnp.where(row == 1, other, 0.0)).astype(BF16)


def pack(me, edge, corner, count, width, fore, back, vp, vm, hp, hm):
    fore_corners = corner_rows(fore)
    back_corners = corner_rows(back)

    def block(offset):
        return lax.rem(me + offset + 2 * count, count)

    def strips(dst, offset, read_side, own_side):
        code = code_at(edge, block(offset), read_side)
        dst[0:SIDE] = turned(fore[lax.rem(code, 4)], code >= 4)
        dst[SIDE:STRIPS] = turned(back[own_side], code_at(edge, me, own_side) >= 4)

    def relayed(offset, read_corner, own_corner):
        return corner_block(
            code_at(corner, block(offset), read_corner), fore_corners, back_corners[own_corner]
        )

    strips(vp, width, N, S)
    vp[STRIPS : STRIPS + 16] = relayed(width + 1, NW, SE)
    vp[STRIPS + 16 : VROWS] = relayed(width - 1, NE, SW)
    strips(vm, -width, S, N)
    vm[STRIPS : STRIPS + 16] = relayed(-width + 1, SW, NE)
    vm[STRIPS + 16 : VROWS] = relayed(-width - 1, SE, NW)
    strips(hp, 1, W, E)
    strips(hm, -1, E, W)


def choose(even, one, two, ahead, behind):
    @pl.when(even)
    def _():
        ahead[...] = one[...]
        behind[...] = two[...]

    @pl.when(jnp.logical_not(even))
    def _():
        ahead[...] = two[...]
        behind[...] = one[...]


def even_row(me, width):
    return (me // width) % 2 == 0


def even_column(me):
    return me % 2 == 0


def put_row(dst, pair, part, row, west, east):
    col = iota((SIDE, CH), 0)
    wide = row.astype(F32)
    dst[1, pair, part] = row.astype(BF16)
    dst[0, pair, part] = jnp.where(col == 0, west, pltpu.roll(wide, 1, 0)).astype(BF16)
    dst[2, pair, part] = jnp.where(col == SIDE - 1, east, pltpu.roll(wide, SIDE - 1, 0)).astype(BF16)


def shift_copies(dst, src, west=None, east=None):
    def step(k, _):
        for part in range(2):
            i = 2 * k + part
            w = 0.0 if west is None else west[pl.ds(i, 1), :]
            e = 0.0 if east is None else east[pl.ds(i, 1), :]
            put_row(dst, k + part, 1 - part, src[k, part], w, e)
        return 0

    lax.fori_loop(0, HALF, step, 0, unroll=4)


def halo_copies(dst, src, west, east, vp, vm, hp, hm):
    west[...] = hp[0:SIDE].astype(F32)
    east[...] = hm[0:SIDE].astype(F32)
    shift_copies(dst, src, west, east)
    hp1 = hp[STRIPS : STRIPS + 16].astype(F32)
    hp2 = hp[STRIPS + 16 : VROWS].astype(F32)
    hm1 = hm[STRIPS : STRIPS + 16].astype(F32)
    hm2 = hm[STRIPS + 16 : VROWS].astype(F32)
    put_row(dst, 0, 0, vp[0:SIDE], hp1[0:1], hm1[0:1])
    put_row(dst, HALF, 1, vm[0:SIDE], hp2[0:1], hm2[0:1])


def zero_copies(dst, src):
    zero = jnp.zeros((SIDE, CH), BF16)
    for b in range(3):
        dst[b, 0, 0] = zero
        dst[b, HALF, 1] = zero
    shift_copies(dst, src)


def window(copies, m, mb):
    parts = [
        copies[b, pl.ds(m + a // 2, mb), a % 2].reshape(mb * SIDE, CH)
        for a in range(4)
        for b in range(3)
    ]
    return jnp.concatenate(parts, axis=1)


def conv_pairs(copies, weights, m, mb):
    return jnp.dot(window(copies, m, mb), weights[...], preferred_element_type=F32)


def edge_tap(side, k):
    return {N: (0, k), S: (2, k), W: (k, 0), E: (k, 2)}[side]


CORNER_TAP = {NW: (0, 0), NE: (0, 2), SE: (2, 2), SW: (2, 0)}


def neighbours(strip):
    row = iota((SIDE, CH), 0)
    up = jnp.where(row == SIDE - 1, 0.0, pltpu.roll(strip, SIDE - 1, 0))
    down = jnp.where(row == 0, 0.0, pltpu.roll(strip, 1, 0))
    return up, down


def tap_plain(weights, a, b):
    at = (a * 3 + b) * CH
    return weights[at : at + CH, 0:CH]


def tap_transposed(turned_weights, a, b):
    at = ((2 - a) * 3 + 2 - b) * CH
    return turned_weights[at : at + CH, 0:CH]


def returned(me, edge, corner, count, width, turned_weights, vp, vm, hp, hm, adds, pieces=None, corners=None):
    def block(offset):
        return lax.rem(me + offset + 2 * count, count)

    adds[...] = jnp.zeros_like(adds)
    row = iota((SIDE, CH), 0)
    for side, offset, message in ((N, width, vm), (E, -1, hp), (S, -width, vp), (W, 1, hm)):
        code = code_at(edge, block(offset), side)
        flip = code >= 4
        strip = message[SIDE:STRIPS].astype(F32)
        up, down = neighbours(strip)
        joined = jnp.concatenate(
            [jnp.where(flip, down, up), strip, jnp.where(flip, up, down)], axis=1
        ).astype(BF16)
        if pieces is not None:
            pieces[side] = joined
        taps = jnp.concatenate(
            [tap_transposed(turned_weights, *edge_tap(side, k)) for k in range(3)], axis=0
        )
        at = lax.rem(code, 4)
        adds[at] = adds[at] + jnp.dot(joined, taps, preferred_element_type=F32)
    for q, offset, message, start in (
        (NW, width + 1, hm, STRIPS + 16),
        (NE, width - 1, hp, STRIPS + 16),
        (SE, -width - 1, hp, STRIPS),
        (SW, -width + 1, hm, STRIPS),
    ):
        code = code_at(corner, block(offset), q)
        cells = message[start : start + 16]
        if corners is not None:
            corners[q] = cells
        given = jnp.dot(
            cells, tap_transposed(turned_weights, *CORNER_TAP[q]), preferred_element_type=F32
        )[1:2]
        first = jnp.where(row == 0, given, 0.0)
        last = jnp.where(row == SIDE - 1, given, 0.0)
        adds[N] = adds[N] + jnp.where(code == NW, first, 0.0) + jnp.where(code == NE, last, 0.0)
        adds[S] = adds[S] + jnp.where(code == SW, first, 0.0) + jnp.where(code == SE, last, 0.0)


def with_adds(rows, i, adds, first=False, last=False):
    col = iota((8, CH), 0)
    rows = jnp.concatenate(
        [
            rows[0:8] + jnp.where(col == 0, adds[W, pl.ds(i, 1), :], 0.0),
            rows[8 : SIDE - 8],
            rows[SIDE - 8 :] + jnp.where(col == 7, adds[E, pl.ds(i, 1), :], 0.0),
        ],
        axis=0,
    )
    if first:
        rows = rows + adds[N]
    if last:
        rows = rows + adds[S]
    return rows


def pad_sides(vp, vm, hp, hm):
    return ((N, vp), (S, vm), (W, hp), (E, hm))


def pad_corners(hp, hm):
    return ((NW, hp, STRIPS), (NE, hm, STRIPS), (SE, hm, STRIPS + 16), (SW, hp, STRIPS + 16))


def received(weights, vp, vm, hp, hm, adds):
    row = iota((SIDE, CH), 0)
    for side, message in pad_sides(vp, vm, hp, hm):
        strip = message[0:SIDE].astype(F32)
        up, down = neighbours(strip)
        joined = jnp.concatenate([down, strip, up], axis=1).astype(BF16)
        taps = jnp.concatenate([tap_plain(weights, *edge_tap(side, k)) for k in range(3)], axis=0)
        adds[side] = jnp.dot(joined, taps, preferred_element_type=F32)
    for q, message, start in pad_corners(hp, hm):
        cells = message[start : start + 16]
        given = jnp.dot(cells, tap_plain(weights, *CORNER_TAP[q]), preferred_element_type=F32)[0:1]
        side = N if q in (NW, NE) else S
        place = 0 if q in (NW, SW) else SIDE - 1
        adds[side] = adds[side] + jnp.where(row == place, given, 0.0)


def pack_kernel(count, width, me, edge, corner, fields, upstream, va, vb, hp, hm, here, fore, back, vp, vm):
    here[...] = upstream[...]
    side_strips(fields, fore)
    side_strips(upstream, back)
    pack(me[0], edge, corner, count, width, fore, back, vp, vm, hp, hm)
    choose(even_row(me[0], width), vp, vm, va, vb)


def relay_kernel(width, me, one, two, hp, hm, vp, vm, ha, hb):
    choose(even_row(me[0], width), two, one, vp, vm)

    def send(even, right, left):
        @pl.when(even)
        def _():
            for own, dst, start in ((hp, right, STRIPS), (hm, left, STRIPS + 16)):
                dst[0:STRIPS] = own[...]
                dst[STRIPS : STRIPS + 16] = vp[start : start + 16]
                dst[STRIPS + 16 : VROWS] = vm[start : start + 16]

    even = even_column(me[0])
    send(even, ha, hb)
    send(jnp.logical_not(even), hb, ha)


def name_kernel(me, one, two, hp, hm):
    choose(even_column(me[0]), two, one, hp, hm)


def plain_weights(source, dst):
    zero = jnp.zeros((CH, CH), BF16)
    for b in range(3):
        for a in range(3):
            at = (a * 3 + b) * CH
            dst[at : at + CH, 0:CH] = source[a, b]
            dst[at + 3 * CH : at + 4 * CH, CH : 2 * CH] = source[a, b]
        dst[(9 + b) * CH : (10 + b) * CH, 0:CH] = zero
        dst[b * CH : (b + 1) * CH, CH : 2 * CH] = zero


def turned_weights(source, dst):
    zero = jnp.zeros((CH, CH), BF16)
    for b in range(3):
        for a in range(3):
            at = (a * 3 + b) * CH
            swapped = source[2 - a, 2 - b].astype(F32).T.astype(BF16)
            dst[at : at + CH, 0:CH] = swapped
            dst[at + 3 * CH : at + 4 * CH, CH : 2 * CH] = swapped
        dst[(9 + b) * CH : (10 + b) * CH, 0:CH] = zero
        dst[b * CH : (b + 1) * CH, CH : 2 * CH] = zero


def conv_all(copies, weights, dst):
    mb = 16

    def step(n, _):
        m = n * mb
        got = conv_pairs(copies, weights, m, mb)
        for part in range(2):
            lanes = slice(part * CH, (part + 1) * CH)
            dst[pl.ds(m, mb), part] = got[:, lanes].reshape(mb, SIDE, CH).astype(dst.dtype)
        return 0

    lax.fori_loop(0, HALF // mb, step, 0)


def back_kernel(token, kernel_two, upstream, in_two, up_copies, grad):
    turned_weights(kernel_two, in_two)
    zero_copies(up_copies, upstream)
    conv_all(up_copies, in_two, grad)


def fore_kernel(token, kernel_one, fields, fwd_one, copies, pre):
    plain_weights(kernel_one, fwd_one)
    zero_copies(copies, fields)
    conv_all(copies, fwd_one, pre)


def middle_kernel(
    count, width, me, edge, corner, vp, vm, one_side, other_side, fwd_one, in_two, pre, grad,
    hidden, grad_pre, va2, vb2, hp2, hm2, fore, back, pieces, corners, hp, hm,
    grad_adds, pre_adds, vp2, vm2,
):
    choose(even_column(me[0]), other_side, one_side, hp, hm)
    returned(me[0], edge, corner, count, width, in_two, vp, vm, hp, hm, grad_adds, pieces, corners)
    received(fwd_one, vp, vm, hp, hm, pre_adds)

    def one(m, part, first=False, last=False):
        i = 2 * m + part
        p = with_adds(pre[m, part], i, pre_adds, first, last)
        g = with_adds(grad[m, part], i, grad_adds, first, last)
        s = 1.0 / (1.0 + jnp.exp(-p))
        hidden[m, part] = (p * s).astype(BF16)
        grad_pre[m, part] = (g * s * (1.0 + p * (1.0 - s))).astype(BF16)

    def step(m, _):
        one(m, 0)
        one(m, 1)
        return 0

    one(0, 0, first=True)
    one(0, 1)
    lax.fori_loop(1, HALF - 1, step, 0, unroll=2)
    one(HALF - 1, 0)
    one(HALF - 1, 1, last=True)
    side_strips(hidden, fore)
    side_strips(grad_pre, back)
    pack(me[0], edge, corner, count, width, fore, back, vp2, vm2, hp2, hm2)
    choose(even_row(me[0], width), vp2, vm2, va2, vb2)


def sums_kernel(
    count, width, scale, kept, me, edge, corner, vp, vm, hp, hm, hidden, grad_pre, field_copies, up_copies,
    fore, back, pieces, corners, sums, acc,
):
    gb = 8
    first = (((0,), (0,)), ((), ()))

    def gather(values, shifted):
        def grad_step(n, _):
            m = n * gb
            left = jnp.concatenate(
                [values[pl.ds(m, gb), part].reshape(gb * SIDE, CH) for part in range(2)], axis=1
            )
            acc[...] += lax.dot_general(left, window(shifted, m, gb), first, preferred_element_type=F32)
            return 0

        acc[...] = jnp.zeros_like(acc)
        lax.fori_loop(0, HALF // gb, grad_step, 0)

    def from_acc(a, b):
        low = (a * 3 + b) * CH
        high = low + 3 * CH
        return acc[0:CH, low : low + CH] + acc[CH : 2 * CH, high : high + CH]

    def add(tap, term):
        at = (tap[0] * 3 + tap[1]) * CH
        sums[at : at + CH] = sums[at : at + CH] + term * scale

    def block(offset):
        return lax.rem(me[0] + offset + 2 * count, count)

    row = iota((16, CH), 0)
    high = (me[0] // FIRST) % 2

    @pl.when(high == (0 if kept else 1))
    def _():
        gather(grad_pre, field_copies)
        for a in range(3):
            for b in range(3):
                at = (a * 3 + b) * CH
                sums[at : at + CH] = from_acc(a, b).T * scale
        for side, message in pad_sides(vp, vm, hp, hm):
            strip = back[side]
            up, down = neighbours(strip)
            joined = jnp.concatenate([up, strip, down], axis=1).astype(BF16)
            term = lax.dot_general(message[0:SIDE], joined, first, preferred_element_type=F32)
            for k in range(3):
                add(edge_tap(side, k), term[:, k * CH : (k + 1) * CH])
        own = corner_rows(back)
        for q, message, start in pad_corners(hp, hm):
            right = jnp.where(row == 0, own[q], 0.0).astype(BF16)
            add(CORNER_TAP[q], lax.dot_general(message[start : start + 16], right, first, preferred_element_type=F32))

    @pl.when(high == (1 if kept else 0))
    def _():
        gather(hidden, up_copies)
        for a in range(3):
            for b in range(3):
                at = (a * 3 + b) * CH
                sums[at : at + CH] = from_acc(2 - a, 2 - b) * scale
        for side, offset in ((N, width), (E, -1), (S, -width), (W, 1)):
            code = lax.rem(code_at(edge, block(offset), side), 4)
            term = lax.dot_general(fore[code].astype(BF16), pieces[side], first, preferred_element_type=F32)
            for k in range(3):
                add(edge_tap(side, k), term[:, k * CH : (k + 1) * CH])
        own = corner_rows(fore)
        for q, offset in ((NW, width + 1), (NE, width - 1), (SE, -width - 1), (SW, -width + 1)):
            code = code_at(corner, block(offset), q)
            cell = jnp.where(code == 0, own[0], jnp.where(code == 1, own[1], jnp.where(code == 2, own[2], own[3])))
            left = jnp.where(row == 1, cell, 0.0).astype(BF16)
            add(CORNER_TAP[q], lax.dot_general(left, corners[q], first, preferred_element_type=F32))


def weights_kernel(token, kernel_one, kernel_two, in_one, fwd_two):
    turned_weights(kernel_one, in_one)
    plain_weights(kernel_two, fwd_two)


def outputs_kernel(hidden, vp, vm, hp, hm, fwd_two, outputs, copies, west, east):
    halo_copies(copies, hidden, west, east, vp, vm, hp, hm)
    conv_all(copies, fwd_two, outputs)


def grads_kernel(
    count, width, me, edge, corner, vp, vm, hp, hm, grad_pre, in_one, grad_fields, copies, adds
):
    mb = 8
    returned(me[0], edge, corner, count, width, in_one, vp, vm, hp, hm, adds)
    zero_copies(copies, grad_pre)

    def rows(n, first=False, last=False):
        m = n * mb
        got = conv_pairs(copies, in_one, m, mb)
        for k in range(mb):
            for part in range(2):
                g = with_adds(
                    got[k * SIDE : (k + 1) * SIDE, part * CH : (part + 1) * CH],
                    2 * (m + k) + part, adds,
                    first and k == 0 and part == 0, last and k == mb - 1 and part == 1,
                )
                grad_fields[m + k, part] = g.astype(BF16)

    def step(n, _):
        rows(n)
        return 0

    rows(0, first=True)
    lax.fori_loop(1, HALF // mb - 1, step, 0)
    rows(HALF // mb - 1, last=True)


def fold_kernel(parts, copies):
    folded = jnp.sum(parts[...].astype(F32), axis=0).astype(copies.dtype)
    for k in range(copies.shape[0]):
        copies[k] = folded


def finish_kernel(me, mine, other, first, second):
    high = (me[0] // FIRST) % 2

    @pl.when(high == 0)
    def _():
        first[...] = mine[...].astype(F32)
        second[...] = other[...].astype(F32)

    @pl.when(high == 1)
    def _():
        first[...] = other[...].astype(F32)
        second[...] = mine[...].astype(F32)


def struct(shape, dtype=BF16):
    return jax.ShapeDtypeStruct(shape, dtype)


BLOCK = (HALF, 2, SIDE, CH)
COPIES = (3, HALF + 1, 2, SIDE, CH)
WEIGHTS = (12 * CH, 2 * CH)


def call(body, tables, arrays, outs, scratch=(), flops=0, moved=4 << 20):
    return pl.pallas_call(
        body,
        out_shape=outs,
        in_specs=[SMEM] * tables + [VMEM] * arrays,
        out_specs=tuple(VMEM for _ in outs),
        scratch_shapes=list(scratch),
        compiler_params=pltpu.CompilerParams(vmem_limit_bytes=ROOM),
        cost_estimate=pl.CostEstimate(flops=flops, bytes_accessed=moved, transcendentals=0),
    )


def swap(x, bit):
    size = lax.axis_size(AXES)
    return lax.ppermute(x, AXES, [(i, i ^ bit) for i in range(size)])


def both_ways(one, two, step):
    size = lax.axis_size(AXES)

    def pairs(turn):
        return [(i, (i + (step if (i // step + turn) % 2 == 0 else -step)) % size) for i in range(size)]

    return lax.ppermute(one, AXES, pairs(0)), lax.ppermute(two, AXES, pairs(1))


FIRST = 2
PLANE = (128, 64, 32, 1)
RING = (16, 8, 4)


def groups_over(bits, size):
    rest = [i for i in range(size) if i & sum(bits) == 0]
    members = [sum(bit for k, bit in enumerate(bits) if n >> k & 1) for n in range(1 << len(bits))]
    return [[base + member for member in members] for base in rest]


def total(send, done, works):
    me = lax.axis_index(AXES).astype(jnp.int32)
    plane, ring = [groups_over(bits, lax.axis_size(AXES)) for bits in (PLANE, RING)]
    steps = [0]

    def scatter(groups):
        return lambda sent: lax.all_to_all(sent, AXES, 0, 0, axis_index_groups=groups, tiled=True)

    def beside(sent, move):
        work = works.get(steps[0])
        steps[0] += 1
        if work is None:
            return move(sent)
        sent, held = lax.optimization_barrier((sent, done.copy()))
        done.update(held)
        got = move(sent)
        gave = work(done)
        got, gave = lax.optimization_barrier((got, gave))
        done.update(gave)
        return got

    def fold(x, parts, dtype):
        folded, = call(fold_kernel, 0, 1, (struct((parts,) + x.shape[1:], dtype),), (), 0, 1 << 19)(x)
        return folded

    def across(sent):
        return swap(sent, FIRST)

    x = beside(send, across)
    x = (done["keep"] + x).astype(BF16)
    parts = len(plane[0])
    x = beside(x.reshape(parts, x.shape[0] // parts, CH), scatter(plane))
    x = beside(fold(x, len(ring[0]), F32), scatter(ring))
    x = beside(fold(x, parts, BF16), scatter(plane)).reshape(-1, CH)
    out = struct(x.shape, F32)
    grads = call(finish_kernel, 1, 2, (out, out))(me.reshape(1), x, beside(x, across))
    return grads, done


def local(inputs, kernel_one, kernel_two, cotangent, edge_codes, corner_codes):
    count = lax.axis_size(AXES)
    width = lax.axis_size("face") // GRID_ROWS * lax.axis_size("sub")
    scale = 1.0 / math.sqrt(count * SIDE * SIDE)
    me = lax.axis_index(AXES).astype(jnp.int32).reshape(1)
    tables = (me, jnp.transpose(edge_codes, (1, 2, 0)), jnp.transpose(corner_codes, (1, 2, 0)))
    fields = inputs.reshape(BLOCK)
    upstream = cotangent.reshape(BLOCK)
    message = struct((VROWS, CH))
    own = struct((STRIPS, CH))
    weights = struct(WEIGHTS)
    block = struct(BLOCK)
    taps = struct((3, 3, CH, CH))
    copies = struct(COPIES)
    wide = struct(BLOCK, F32)
    sides = (4, SIDE, CH)
    strips = pltpu.VMEM(sides, F32)
    vertical_pair = pltpu.VMEM((VROWS, CH), BF16)
    column = pltpu.VMEM((SIDE, CH), F32)
    conv_flops = 2 * SIDE * SIDE * 9 * CH * CH

    va, vb, hp, hm, upstream = call(
        lambda *refs: pack_kernel(count, width, *refs), 3, 2, (message, message, own, own, block),
        [strips, strips, vertical_pair, vertical_pair],
    )(*tables, fields, upstream)
    va, vb, token = lax.optimization_barrier((va, vb, me))
    va, vb = both_ways(va, vb, width)
    in_two, up_copies, grad = call(back_kernel, 1, 2, (weights, copies, wide), (), conv_flops)(
        token, kernel_two, upstream
    )
    va, vb, in_two, up_copies, grad, token = lax.optimization_barrier(
        (va, vb, in_two, up_copies, grad, token)
    )

    def relay(token, va, vb, hp, hm):
        return call(
            lambda *refs: relay_kernel(width, *refs), 1, 4, (message, message, message, message), (), 0, 1 << 18
        )(token, va, vb, hp, hm)

    vp, vm, ha, hb = relay(token, va, vb, hp, hm)
    ha, hb, token = lax.optimization_barrier((ha, hb, token))
    ha, hb = both_ways(ha, hb, 1)
    fwd_one, field_copies, pre = call(fore_kernel, 1, 2, (weights, copies, wide), (), conv_flops)(
        token, kernel_one, fields
    )
    hidden, grad_pre, va2, vb2, hp2, hm2, fore, back, pieces, corners, hp, hm = call(
        lambda *refs: middle_kernel(count, width, *refs), 3, 8,
        (
            block, block, message, message, own, own, struct(sides, F32), struct(sides, F32),
            struct((4, SIDE, 3 * CH)), struct((4, 16, CH)),
            message, message,
        ),
        [strips, strips, vertical_pair, vertical_pair], conv_flops,
    )(*tables, vp, vm, ha, hb, fwd_one, in_two, pre, grad)
    hidden, grad_pre, va2, vb2, token = lax.optimization_barrier((hidden, grad_pre, va2, vb2, token))
    def half(kept, token):
        got, = call(
            lambda me, *refs: sums_kernel(count, width, scale, kept, me, *refs), 3, 12,
            (struct((9 * CH, CH), F32),), [pltpu.VMEM((2 * CH, 12 * CH), F32)], conv_flops,
        )(
            token, *tables[1:], vp, vm, hp, hm, hidden, grad_pre, field_copies, up_copies,
            fore, back, pieces, corners,
        )
        return got

    def first_work(done):
        va, vb = both_ways(done["va"], done["vb"], width)
        return dict(keep=half(True, done["token"]), va=va, vb=vb)

    def second_work(done):
        vp, vm, ha, hb = relay(done["token"], done["va"], done["vb"], hp2, hm2)
        ha, hb = both_ways(ha, hb, 1)
        return dict(vp=vp, vm=vm, ha=ha, hb=hb)

    def third_work(done):
        hp, hm = call(name_kernel, 1, 2, (message, message), (), 0, 1 << 18)(
            done["token"], done["ha"], done["hb"]
        )
        in_one, fwd_two = call(weights_kernel, 1, 2, (weights, weights))(
            done["token"], kernel_one, kernel_two
        )
        outputs, = call(
            outputs_kernel, 0, 6, (block,), [pltpu.VMEM(COPIES, BF16), column, column], conv_flops
        )(hidden, done["vp"], done["vm"], hp, hm, fwd_two)
        return dict(in_one=in_one, hp=hp, hm=hm, outputs=outputs)

    def fourth_work(done):
        grad_fields, = call(
            lambda *refs: grads_kernel(count, width, *refs), 3, 6, (block,),
            [pltpu.VMEM(COPIES, BF16), strips], conv_flops,
        )(*tables, done["vp"], done["vm"], done["hp"], done["hm"], grad_pre, done["in_one"])
        return dict(grad_fields=grad_fields)

    grads, done = total(
        half(False, token), dict(va=va2, vb=vb2, token=token),
        {0: first_work, 1: second_work, 2: third_work, 3: fourth_work},
    )
    shape = (1, 1, SIDE, SIDE, CH)
    return (
        done["outputs"].reshape(shape), done["grad_fields"].reshape(shape),
        grads[0].reshape(taps.shape), grads[1].reshape(taps.shape),
    )


def solution(mesh):
    block = P("face", "sub", None, None, None)
    return jax.shard_map(
        local,
        mesh=mesh,
        in_specs=(block, P(), P(), block, P(), P()),
        out_specs=(block, block, P(), P()),
        check_vma=False,
    )
```

```python
import math

import jax
import jax.numpy as jnp
from jax import lax
from jax.experimental import pallas as pl
from jax.experimental.pallas import tpu as pltpu
from jax.sharding import PartitionSpec as P

AXES = ("face", "sub")
GRID_ROWS = 8
SIDE = 64
CH = 128
HALF = SIDE // 2
STRIPS = 2 * SIDE
VROWS = STRIPS + 32
BF16 = jnp.bfloat16
F32 = jnp.float32
N, E, S, W = 0, 1, 2, 3
NW, NE, SE, SW = 0, 1, 2, 3
VMEM = pl.BlockSpec(memory_space=pltpu.VMEM)
SMEM = pl.BlockSpec(memory_space=pltpu.SMEM)
ROOM = 20 << 20


def code_at(table, block, which):
    return table[block % 2, which, block // 2]


def iota(shape, dim):
    return lax.broadcasted_iota(jnp.int32, shape, dim)


def strips_from(north, south, low, high, dst):
    dst[N] = north.astype(F32)
    dst[S] = south.astype(F32)
    low = low.reshape(SIDE, 16, CH).astype(F32)
    dst[W] = jnp.sum(jnp.where(iota(low.shape, 1) == 0, low, 0.0), axis=1)
    high = high.reshape(SIDE, 16, CH).astype(F32)
    dst[E] = jnp.sum(jnp.where(iota(high.shape, 1) == 15, high, 0.0), axis=1)


def side_strips(block, dst):
    strips_from(
        block[0, 0], block[HALF - 1, 1], block[:, :, 0:16, :], block[:, :, SIDE - 16 : SIDE, :], dst
    )


def corner_rows(strips):
    north = strips[N]
    south = strips[S]
    last = SIDE - 1
    return [north[0:1], north[last : last + 1], south[last : last + 1], south[0:1]]


def turned(strip, flip):
    row = iota((SIDE, SIDE), 0)
    col = iota((SIDE, SIDE), 1)
    target = jnp.where(flip, SIDE - 1 - row, row)
    matrix = jnp.where(col == target, 1.0, 0.0).astype(BF16)
    return jnp.dot(matrix, strip.astype(BF16), preferred_element_type=F32).astype(BF16)


def corner_block(code, own, other):
    picked = jnp.where(code == 0, own[0], jnp.where(code == 1, own[1], jnp.where(code == 2, own[2], own[3])))
    row = iota((16, CH), 0)
    return (jnp.where(row == 0, picked, 0.0) + jnp.where(row == 1, other, 0.0)).astype(BF16)


def pack(me, edge, corner, count, width, fore, back, vp, vm, hp, hm):
    fore_corners = corner_rows(fore)
    back_corners = corner_rows(back)

    def block(offset):
        return lax.rem(me + offset + 2 * count, count)

    def strips(dst, offset, read_side, own_side):
        code = code_at(edge, block(offset), read_side)
        dst[0:SIDE] = turned(fore[lax.rem(code, 4)], code >= 4)
        dst[SIDE:STRIPS] = turned(back[own_side], code_at(edge, me, own_side) >= 4)

    def relayed(offset, read_corner, own_corner):
        return corner_block(
            code_at(corner, block(offset), read_corner), fore_corners, back_corners[own_corner]
        )

    strips(vp, width, N, S)
    vp[STRIPS : STRIPS + 16] = relayed(width + 1, NW, SE)
    vp[STRIPS + 16 : VROWS] = relayed(width - 1, NE, SW)
    strips(vm, -width, S, N)
    vm[STRIPS : STRIPS + 16] = relayed(-width + 1, SW, NE)
    vm[STRIPS + 16 : VROWS] = relayed(-width - 1, SE, NW)
    strips(hp, 1, W, E)
    strips(hm, -1, E, W)


def choose(even, one, two, ahead, behind):
    @pl.when(even)
    def _():
        ahead[...] = one[...]
        behind[...] = two[...]

    @pl.when(jnp.logical_not(even))
    def _():
        ahead[...] = two[...]
        behind[...] = one[...]


def even_row(me, width):
    return (me // width) % 2 == 0


def even_column(me):
    return me % 2 == 0


def put_row(dst, pair, part, row, west, east):
    col = iota((SIDE, CH), 0)
    wide = row.astype(F32)
    dst[1, pair, part] = row.astype(BF16)
    dst[0, pair, part] = jnp.where(col == 0, west, pltpu.roll(wide, 1, 0)).astype(BF16)
    dst[2, pair, part] = jnp.where(col == SIDE - 1, east, pltpu.roll(wide, SIDE - 1, 0)).astype(BF16)


def shift_copies(dst, src, west=None, east=None):
    def step(k, _):
        for part in range(2):
            i = 2 * k + part
            w = 0.0 if west is None else west[pl.ds(i, 1), :]
            e = 0.0 if east is None else east[pl.ds(i, 1), :]
            put_row(dst, k + part, 1 - part, src[k, part], w, e)
        return 0

    lax.fori_loop(0, HALF, step, 0, unroll=4)


def halo_copies(dst, src, west, east, vp, vm, hp, hm):
    west[...] = hp[0:SIDE].astype(F32)
    east[...] = hm[0:SIDE].astype(F32)
    shift_copies(dst, src, west, east)
    hp1 = hp[STRIPS : STRIPS + 16].astype(F32)
    hp2 = hp[STRIPS + 16 : VROWS].astype(F32)
    hm1 = hm[STRIPS : STRIPS + 16].astype(F32)
    hm2 = hm[STRIPS + 16 : VROWS].astype(F32)
    put_row(dst, 0, 0, vp[0:SIDE], hp1[0:1], hm1[0:1])
    put_row(dst, HALF, 1, vm[0:SIDE], hp2[0:1], hm2[0:1])


def zero_copies(dst, src):
    zero = jnp.zeros((SIDE, CH), BF16)
    for b in range(3):
        dst[b, 0, 0] = zero
        dst[b, HALF, 1] = zero
    shift_copies(dst, src)


def window(copies, m, mb):
    parts = [
        copies[b, pl.ds(m + a // 2, mb), a % 2].reshape(mb * SIDE, CH)
        for a in range(4)
        for b in range(3)
    ]
    return jnp.concatenate(parts, axis=1)


def conv_pairs(copies, weights, m, mb):
    return jnp.dot(window(copies, m, mb), weights[...], preferred_element_type=F32)


def edge_tap(side, k):
    return {N: (0, k), S: (2, k), W: (k, 0), E: (k, 2)}[side]


CORNER_TAP = {NW: (0, 0), NE: (0, 2), SE: (2, 2), SW: (2, 0)}


def neighbours(strip):
    row = iota((SIDE, CH), 0)
    up = jnp.where(row == SIDE - 1, 0.0, pltpu.roll(strip, SIDE - 1, 0))
    down = jnp.where(row == 0, 0.0, pltpu.roll(strip, 1, 0))
    return up, down


def tap_plain(weights, a, b):
    at = (a * 3 + b) * CH
    return weights[at : at + CH, 0:CH]


def tap_transposed(turned_weights, a, b):
    at = ((2 - a) * 3 + 2 - b) * CH
    return turned_weights[at : at + CH, 0:CH]


def returned(me, edge, corner, count, width, turned_weights, vp, vm, hp, hm, adds, pieces=None, corners=None):
    def block(offset):
        return lax.rem(me + offset + 2 * count, count)

    adds[...] = jnp.zeros_like(adds)
    row = iota((SIDE, CH), 0)
    for side, offset, message in ((N, width, vm), (E, -1, hp), (S, -width, vp), (W, 1, hm)):
        code = code_at(edge, block(offset), side)
        flip = code >= 4
        strip = message[SIDE:STRIPS].astype(F32)
        up, down = neighbours(strip)
        joined = jnp.concatenate(
            [jnp.where(flip, down, up), strip, jnp.where(flip, up, down)], axis=1
        ).astype(BF16)
        if pieces is not None:
            pieces[side] = joined
        taps = jnp.concatenate(
            [tap_transposed(turned_weights, *edge_tap(side, k)) for k in range(3)], axis=0
        )
        at = lax.rem(code, 4)
        adds[at] = adds[at] + jnp.dot(joined, taps, preferred_element_type=F32)
    for q, offset, message, start in (
        (NW, width + 1, hm, STRIPS + 16),
        (NE, width - 1, hp, STRIPS + 16),
        (SE, -width - 1, hp, STRIPS),
        (SW, -width + 1, hm, STRIPS),
    ):
        code = code_at(corner, block(offset), q)
        cells = message[start : start + 16]
        if corners is not None:
            corners[q] = cells
        given = jnp.dot(
            cells, tap_transposed(turned_weights, *CORNER_TAP[q]), preferred_element_type=F32
        )[1:2]
        first = jnp.where(row == 0, given, 0.0)
        last = jnp.where(row == SIDE - 1, given, 0.0)
        adds[N] = adds[N] + jnp.where(code == NW, first, 0.0) + jnp.where(code == NE, last, 0.0)
        adds[S] = adds[S] + jnp.where(code == SW, first, 0.0) + jnp.where(code == SE, last, 0.0)


def with_adds(rows, i, adds, first=False, last=False):
    col = iota((8, CH), 0)
    rows = jnp.concatenate(
        [
            rows[0:8] + jnp.where(col == 0, adds[W, pl.ds(i, 1), :], 0.0),
            rows[8 : SIDE - 8],
            rows[SIDE - 8 :] + jnp.where(col == 7, adds[E, pl.ds(i, 1), :], 0.0),
        ],
        axis=0,
    )
    if first:
        rows = rows + adds[N]
    if last:
        rows = rows + adds[S]
    return rows


def pad_sides(vp, vm, hp, hm):
    return ((N, vp), (S, vm), (W, hp), (E, hm))


def pad_corners(hp, hm):
    return ((NW, hp, STRIPS), (NE, hm, STRIPS), (SE, hm, STRIPS + 16), (SW, hp, STRIPS + 16))


def received(weights, vp, vm, hp, hm, adds):
    row = iota((SIDE, CH), 0)
    for side, message in pad_sides(vp, vm, hp, hm):
        strip = message[0:SIDE].astype(F32)
        up, down = neighbours(strip)
        joined = jnp.concatenate([down, strip, up], axis=1).astype(BF16)
        taps = jnp.concatenate([tap_plain(weights, *edge_tap(side, k)) for k in range(3)], axis=0)
        adds[side] = jnp.dot(joined, taps, preferred_element_type=F32)
    for q, message, start in pad_corners(hp, hm):
        cells = message[start : start + 16]
        given = jnp.dot(cells, tap_plain(weights, *CORNER_TAP[q]), preferred_element_type=F32)[0:1]
        side = N if q in (NW, NE) else S
        place = 0 if q in (NW, SW) else SIDE - 1
        adds[side] = adds[side] + jnp.where(row == place, given, 0.0)


def pack_kernel(count, width, me, edge, corner, fields, upstream, va, vb, hp, hm, here, fore, back, vp, vm):
    here[...] = upstream[...]
    side_strips(fields, fore)
    side_strips(upstream, back)
    pack(me[0], edge, corner, count, width, fore, back, vp, vm, hp, hm)
    choose(even_row(me[0], width), vp, vm, va, vb)


def relay_kernel(width, me, one, two, hp, hm, vp, vm, ha, hb):
    choose(even_row(me[0], width), two, one, vp, vm)

    def send(even, right, left):
        @pl.when(even)
        def _():
            for own, dst, start in ((hp, right, STRIPS), (hm, left, STRIPS + 16)):
                dst[0:STRIPS] = own[...]
                dst[STRIPS : STRIPS + 16] = vp[start : start + 16]
                dst[STRIPS + 16 : VROWS] = vm[start : start + 16]

    even = even_column(me[0])
    send(even, ha, hb)
    send(jnp.logical_not(even), hb, ha)


def name_kernel(me, one, two, hp, hm):
    choose(even_column(me[0]), two, one, hp, hm)


def plain_weights(source, dst):
    zero = jnp.zeros((CH, CH), BF16)
    for b in range(3):
        for a in range(3):
            at = (a * 3 + b) * CH
            dst[at : at + CH, 0:CH] = source[a, b]
            dst[at + 3 * CH : at + 4 * CH, CH : 2 * CH] = source[a, b]
        dst[(9 + b) * CH : (10 + b) * CH, 0:CH] = zero
        dst[b * CH : (b + 1) * CH, CH : 2 * CH] = zero


def turned_weights(source, dst):
    zero = jnp.zeros((CH, CH), BF16)
    for b in range(3):
        for a in range(3):
            at = (a * 3 + b) * CH
            swapped = source[2 - a, 2 - b].astype(F32).T.astype(BF16)
            dst[at : at + CH, 0:CH] = swapped
            dst[at + 3 * CH : at + 4 * CH, CH : 2 * CH] = swapped
        dst[(9 + b) * CH : (10 + b) * CH, 0:CH] = zero
        dst[b * CH : (b + 1) * CH, CH : 2 * CH] = zero


def conv_all(copies, weights, dst):
    mb = 16

    def step(n, _):
        m = n * mb
        got = conv_pairs(copies, weights, m, mb)
        for part in range(2):
            lanes = slice(part * CH, (part + 1) * CH)
            dst[pl.ds(m, mb), part] = got[:, lanes].reshape(mb, SIDE, CH).astype(dst.dtype)
        return 0

    lax.fori_loop(0, HALF // mb, step, 0)


def back_kernel(token, kernel_two, upstream, in_two, up_copies, grad):
    turned_weights(kernel_two, in_two)
    zero_copies(up_copies, upstream)
    conv_all(up_copies, in_two, grad)


def fore_kernel(token, kernel_one, fields, fwd_one, copies, pre):
    plain_weights(kernel_one, fwd_one)
    zero_copies(copies, fields)
    conv_all(copies, fwd_one, pre)


def middle_kernel(
    count, width, me, edge, corner, vp, vm, one_side, other_side, fwd_one, in_two, pre, grad,
    hidden, grad_pre, va2, vb2, hp2, hm2, fore, back, pieces, corners, hp, hm,
    grad_adds, pre_adds, vp2, vm2,
):
    choose(even_column(me[0]), other_side, one_side, hp, hm)
    returned(me[0], edge, corner, count, width, in_two, vp, vm, hp, hm, grad_adds, pieces, corners)
    received(fwd_one, vp, vm, hp, hm, pre_adds)

    def one(m, part, first=False, last=False):
        i = 2 * m + part
        p = with_adds(pre[m, part], i, pre_adds, first, last)
        g = with_adds(grad[m, part], i, grad_adds, first, last)
        s = 1.0 / (1.0 + jnp.exp(-p))
        hidden[m, part] = (p * s).astype(BF16)
        grad_pre[m, part] = (g * s * (1.0 + p * (1.0 - s))).astype(BF16)

    def step(m, _):
        one(m, 0)
        one(m, 1)
        return 0

    one(0, 0, first=True)
    one(0, 1)
    lax.fori_loop(1, HALF - 1, step, 0, unroll=2)
    one(HALF - 1, 0)
    one(HALF - 1, 1, last=True)
    side_strips(hidden, fore)
    side_strips(grad_pre, back)
    pack(me[0], edge, corner, count, width, fore, back, vp2, vm2, hp2, hm2)
    choose(even_row(me[0], width), vp2, vm2, va2, vb2)


def sums_kernel(
    count, width, scale, kept, me, edge, corner, vp, vm, hp, hm, hidden, grad_pre, field_copies, up_copies,
    fore, back, pieces, corners, sums, acc,
):
    gb = 8
    first = (((0,), (0,)), ((), ()))

    def gather(values, shifted):
        def grad_step(n, _):
            m = n * gb
            left = jnp.concatenate(
                [values[pl.ds(m, gb), part].reshape(gb * SIDE, CH) for part in range(2)], axis=1
            )
            acc[...] += lax.dot_general(left, window(shifted, m, gb), first, preferred_element_type=F32)
            return 0

        acc[...] = jnp.zeros_like(acc)
        lax.fori_loop(0, HALF // gb, grad_step, 0)

    def from_acc(a, b):
        low = (a * 3 + b) * CH
        high = low + 3 * CH
        return acc[0:CH, low : low + CH] + acc[CH : 2 * CH, high : high + CH]

    def add(tap, term):
        at = (tap[0] * 3 + tap[1]) * CH
        sums[at : at + CH] = sums[at : at + CH] + term * scale

    def block(offset):
        return lax.rem(me[0] + offset + 2 * count, count)

    row = iota((16, CH), 0)
    high = (me[0] // FIRST) % 2

    @pl.when(high == (0 if kept else 1))
    def _():
        gather(grad_pre, field_copies)
        for a in range(3):
            for b in range(3):
                at = (a * 3 + b) * CH
                sums[at : at + CH] = from_acc(a, b).T * scale
        for side, message in pad_sides(vp, vm, hp, hm):
            strip = back[side]
            up, down = neighbours(strip)
            joined = jnp.concatenate([up, strip, down], axis=1).astype(BF16)
            term = lax.dot_general(message[0:SIDE], joined, first, preferred_element_type=F32)
            for k in range(3):
                add(edge_tap(side, k), term[:, k * CH : (k + 1) * CH])
        own = corner_rows(back)
        for q, message, start in pad_corners(hp, hm):
            right = jnp.where(row == 0, own[q], 0.0).astype(BF16)
            add(CORNER_TAP[q], lax.dot_general(message[start : start + 16], right, first, preferred_element_type=F32))

    @pl.when(high == (1 if kept else 0))
    def _():
        gather(hidden, up_copies)
        for a in range(3):
            for b in range(3):
                at = (a * 3 + b) * CH
                sums[at : at + CH] = from_acc(2 - a, 2 - b) * scale
        for side, offset in ((N, width), (E, -1), (S, -width), (W, 1)):
            code = lax.rem(code_at(edge, block(offset), side), 4)
            term = lax.dot_general(fore[code].astype(BF16), pieces[side], first, preferred_element_type=F32)
            for k in range(3):
                add(edge_tap(side, k), term[:, k * CH : (k + 1) * CH])
        own = corner_rows(fore)
        for q, offset in ((NW, width + 1), (NE, width - 1), (SE, -width - 1), (SW, -width + 1)):
            code = code_at(corner, block(offset), q)
            cell = jnp.where(code == 0, own[0], jnp.where(code == 1, own[1], jnp.where(code == 2, own[2], own[3])))
            left = jnp.where(row == 1, cell, 0.0).astype(BF16)
            add(CORNER_TAP[q], lax.dot_general(left, corners[q], first, preferred_element_type=F32))


def weights_kernel(token, kernel_one, kernel_two, in_one, fwd_two):
    turned_weights(kernel_one, in_one)
    plain_weights(kernel_two, fwd_two)


def outputs_kernel(hidden, vp, vm, hp, hm, fwd_two, outputs, copies, west, east):
    halo_copies(copies, hidden, west, east, vp, vm, hp, hm)
    conv_all(copies, fwd_two, outputs)


def grads_kernel(
    count, width, me, edge, corner, vp, vm, hp, hm, grad_pre, in_one, grad_fields, copies, adds
):
    mb = 8
    returned(me[0], edge, corner, count, width, in_one, vp, vm, hp, hm, adds)
    zero_copies(copies, grad_pre)

    def rows(n, first=False, last=False):
        m = n * mb
        got = conv_pairs(copies, in_one, m, mb)
        for k in range(mb):
            for part in range(2):
                g = with_adds(
                    got[k * SIDE : (k + 1) * SIDE, part * CH : (part + 1) * CH],
                    2 * (m + k) + part, adds,
                    first and k == 0 and part == 0, last and k == mb - 1 and part == 1,
                )
                grad_fields[m + k, part] = g.astype(BF16)

    def step(n, _):
        rows(n)
        return 0

    rows(0, first=True)
    lax.fori_loop(1, HALF // mb - 1, step, 0)
    rows(HALF // mb - 1, last=True)


def fold_kernel(parts, copies):
    folded = jnp.sum(parts[...].astype(F32), axis=0).astype(copies.dtype)
    for k in range(copies.shape[0]):
        copies[k] = folded


def finish_kernel(me, mine, other, first, second):
    high = (me[0] // FIRST) % 2

    @pl.when(high == 0)
    def _():
        first[...] = mine[...].astype(F32)
        second[...] = other[...].astype(F32)

    @pl.when(high == 1)
    def _():
        first[...] = other[...].astype(F32)
        second[...] = mine[...].astype(F32)


def struct(shape, dtype=BF16):
    return jax.ShapeDtypeStruct(shape, dtype)


BLOCK = (HALF, 2, SIDE, CH)
COPIES = (3, HALF + 1, 2, SIDE, CH)
WEIGHTS = (12 * CH, 2 * CH)


def call(body, tables, arrays, outs, scratch=(), flops=0, moved=4 << 20):
    return pl.pallas_call(
        body,
        out_shape=outs,
        in_specs=[SMEM] * tables + [VMEM] * arrays,
        out_specs=tuple(VMEM for _ in outs),
        scratch_shapes=list(scratch),
        compiler_params=pltpu.CompilerParams(vmem_limit_bytes=ROOM),
        cost_estimate=pl.CostEstimate(flops=flops, bytes_accessed=moved, transcendentals=0),
    )


def swap(x, bit):
    size = lax.axis_size(AXES)
    return lax.ppermute(x, AXES, [(i, i ^ bit) for i in range(size)])


def both_ways(one, two, step):
    size = lax.axis_size(AXES)

    def pairs(turn):
        return [(i, (i + (step if (i // step + turn) % 2 == 0 else -step)) % size) for i in range(size)]

    return lax.ppermute(one, AXES, pairs(0)), lax.ppermute(two, AXES, pairs(1))


FIRST = 2
PLANE = (128, 64, 32, 1)
RING = (16, 8, 4)


def groups_over(bits, size):
    rest = [i for i in range(size) if i & sum(bits) == 0]
    members = [sum(bit for k, bit in enumerate(bits) if n >> k & 1) for n in range(1 << len(bits))]
    return [[base + member for member in members] for base in rest]


def total(send, done, works):
    me = lax.axis_index(AXES).astype(jnp.int32)
    plane, ring = [groups_over(bits, lax.axis_size(AXES)) for bits in (PLANE, RING)]
    steps = [0]

    def scatter(groups):
        return lambda sent: lax.all_to_all(sent, AXES, 0, 0, axis_index_groups=groups, tiled=True)

    def beside(sent, move):
        work = works.get(steps[0])
        steps[0] += 1
        if work is None:
            return move(sent)
        sent, held = lax.optimization_barrier((sent, done.copy()))
        done.update(held)
        got = move(sent)
        gave = work(done)
        got, gave = lax.optimization_barrier((got, gave))
        done.update(gave)
        return got

    def fold(x, parts, dtype):
        folded, = call(fold_kernel, 0, 1, (struct((parts,) + x.shape[1:], dtype),), (), 0, 1 << 19)(x)
        return folded

    def across(sent):
        return swap(sent, FIRST)

    x = beside(send, across)
    x = (done["keep"] + x).astype(BF16)
    parts = len(plane[0])
    x = beside(x.reshape(parts, x.shape[0] // parts, CH), scatter(plane))
    x = beside(fold(x, len(ring[0]), F32), scatter(ring))
    x = beside(fold(x, parts, BF16), scatter(plane)).reshape(-1, CH)
    out = struct(x.shape, F32)
    grads = call(finish_kernel, 1, 2, (out, out))(me.reshape(1), x, beside(x, across))
    return grads, done


def local(inputs, kernel_one, kernel_two, cotangent, edge_codes, corner_codes):
    count = lax.axis_size(AXES)
    width = lax.axis_size("face") // GRID_ROWS * lax.axis_size("sub")
    scale = 1.0 / math.sqrt(count * SIDE * SIDE)
    me = lax.axis_index(AXES).astype(jnp.int32).reshape(1)
    tables = (me, jnp.transpose(edge_codes, (1, 2, 0)), jnp.transpose(corner_codes, (1, 2, 0)))
    fields = inputs.reshape(BLOCK)
    upstream = cotangent.reshape(BLOCK)
    message = struct((VROWS, CH))
    own = struct((STRIPS, CH))
    weights = struct(WEIGHTS)
    block = struct(BLOCK)
    taps = struct((3, 3, CH, CH))
    copies = struct(COPIES)
    wide = struct(BLOCK, F32)
    sides = (4, SIDE, CH)
    strips = pltpu.VMEM(sides, F32)
    vertical_pair = pltpu.VMEM((VROWS, CH), BF16)
    column = pltpu.VMEM((SIDE, CH), F32)
    conv_flops = 2 * SIDE * SIDE * 9 * CH * CH

    va, vb, hp, hm, upstream = call(
        lambda *refs: pack_kernel(count, width, *refs), 3, 2, (message, message, own, own, block),
        [strips, strips, vertical_pair, vertical_pair],
    )(*tables, fields, upstream)
    va, vb, token = lax.optimization_barrier((va, vb, me))
    va, vb = both_ways(va, vb, width)
    in_two, up_copies, grad = call(back_kernel, 1, 2, (weights, copies, wide), (), conv_flops)(
        token, kernel_two, upstream
    )
    va, vb, in_two, up_copies, grad, token = lax.optimization_barrier(
        (va, vb, in_two, up_copies, grad, token)
    )

    def relay(token, va, vb, hp, hm):
        return call(
            lambda *refs: relay_kernel(width, *refs), 1, 4, (message, message, message, message), (), 0, 1 << 18
        )(token, va, vb, hp, hm)

    vp, vm, ha, hb = relay(token, va, vb, hp, hm)
    ha, hb, token = lax.optimization_barrier((ha, hb, token))
    ha, hb = both_ways(ha, hb, 1)
    fwd_one, field_copies, pre = call(fore_kernel, 1, 2, (weights, copies, wide), (), conv_flops)(
        token, kernel_one, fields
    )
    hidden, grad_pre, va2, vb2, hp2, hm2, fore, back, pieces, corners, hp, hm = call(
        lambda *refs: middle_kernel(count, width, *refs), 3, 8,
        (
            block, block, message, message, own, own, struct(sides, F32), struct(sides, F32),
            struct((4, SIDE, 3 * CH)), struct((4, 16, CH)),
            message, message,
        ),
        [strips, strips, vertical_pair, vertical_pair], conv_flops,
    )(*tables, vp, vm, ha, hb, fwd_one, in_two, pre, grad)
    hidden, grad_pre, va2, vb2, token = lax.optimization_barrier((hidden, grad_pre, va2, vb2, token))
    def half(kept, token):
        got, = call(
            lambda me, *refs: sums_kernel(count, width, scale, kept, me, *refs), 3, 12,
            (struct((9 * CH, CH), F32),), [pltpu.VMEM((2 * CH, 12 * CH), F32)], conv_flops,
        )(
            token, *tables[1:], vp, vm, hp, hm, hidden, grad_pre, field_copies, up_copies,
            fore, back, pieces, corners,
        )
        return got

    def first_work(done):
        va, vb = both_ways(done["va"], done["vb"], width)
        return dict(keep=half(True, done["token"]), va=va, vb=vb)

    def second_work(done):
        vp, vm, ha, hb = relay(done["token"], done["va"], done["vb"], hp2, hm2)
        ha, hb = both_ways(ha, hb, 1)
        return dict(vp=vp, vm=vm, ha=ha, hb=hb)

    def third_work(done):
        hp, hm = call(name_kernel, 1, 2, (message, message), (), 0, 1 << 18)(
            done["token"], done["ha"], done["hb"]
        )
        in_one, fwd_two = call(weights_kernel, 1, 2, (weights, weights))(
            done["token"], kernel_one, kernel_two
        )
        outputs, = call(
            outputs_kernel, 0, 6, (block,), [pltpu.VMEM(COPIES, BF16), column, column], conv_flops
        )(hidden, done["vp"], done["vm"], hp, hm, fwd_two)
        grad_fields, = call(
            lambda *refs: grads_kernel(count, width, *refs), 3, 6, (block,),
            [pltpu.VMEM(COPIES, BF16), strips], conv_flops,
        )(*tables, done["vp"], done["vm"], hp, hm, grad_pre, in_one)
        return dict(outputs=outputs, grad_fields=grad_fields)

    grads, done = total(
        half(False, token), dict(va=va2, vb=vb2, token=token),
        {0: first_work, 1: second_work, 2: third_work},
    )
    shape = (1, 1, SIDE, SIDE, CH)
    return (
        done["outputs"].reshape(shape), done["grad_fields"].reshape(shape),
        grads[0].reshape(taps.shape), grads[1].reshape(taps.shape),
    )


def solution(mesh):
    block = P("face", "sub", None, None, None)
    return jax.shard_map(
        local,
        mesh=mesh,
        in_specs=(block, P(), P(), block, P(), P()),
        out_specs=(block, block, P(), P()),
        check_vma=False,
    )
```

```python
import math

import jax
import jax.numpy as jnp
from jax import lax
from jax.experimental import pallas as pl
from jax.experimental.pallas import tpu as pltpu
from jax.sharding import PartitionSpec as P

AXES = ("face", "sub")
GRID_ROWS = 8
SIDE = 64
CH = 128
HALF = SIDE // 2
STRIPS = 2 * SIDE
VROWS = STRIPS + 32
BF16 = jnp.bfloat16
F32 = jnp.float32
N, E, S, W = 0, 1, 2, 3
NW, NE, SE, SW = 0, 1, 2, 3
VMEM = pl.BlockSpec(memory_space=pltpu.VMEM)
SMEM = pl.BlockSpec(memory_space=pltpu.SMEM)
ROOM = 20 << 20


def code_at(table, block, which):
    return table[block % 2, which, block // 2]


def iota(shape, dim):
    return lax.broadcasted_iota(jnp.int32, shape, dim)


def strips_from(north, south, low, high, dst):
    dst[N] = north.astype(F32)
    dst[S] = south.astype(F32)
    low = low.reshape(SIDE, 16, CH).astype(F32)
    dst[W] = jnp.sum(jnp.where(iota(low.shape, 1) == 0, low, 0.0), axis=1)
    high = high.reshape(SIDE, 16, CH).astype(F32)
    dst[E] = jnp.sum(jnp.where(iota(high.shape, 1) == 15, high, 0.0), axis=1)


def side_strips(block, dst):
    strips_from(
        block[0, 0], block[HALF - 1, 1], block[:, :, 0:16, :], block[:, :, SIDE - 16 : SIDE, :], dst
    )


def corner_rows(strips):
    north = strips[N]
    south = strips[S]
    last = SIDE - 1
    return [north[0:1], north[last : last + 1], south[last : last + 1], south[0:1]]


def turned(strip, flip):
    row = iota((SIDE, SIDE), 0)
    col = iota((SIDE, SIDE), 1)
    target = jnp.where(flip, SIDE - 1 - row, row)
    matrix = jnp.where(col == target, 1.0, 0.0).astype(BF16)
    return jnp.dot(matrix, strip.astype(BF16), preferred_element_type=F32).astype(BF16)


def corner_block(code, own, other):
    picked = jnp.where(code == 0, own[0], jnp.where(code == 1, own[1], jnp.where(code == 2, own[2], own[3])))
    row = iota((16, CH), 0)
    return (jnp.where(row == 0, picked, 0.0) + jnp.where(row == 1, other, 0.0)).astype(BF16)


def pack(me, edge, corner, count, width, fore, back, vp, vm, hp, hm):
    fore_corners = corner_rows(fore)
    back_corners = corner_rows(back)

    def block(offset):
        return lax.rem(me + offset + 2 * count, count)

    def strips(dst, offset, read_side, own_side):
        code = code_at(edge, block(offset), read_side)
        dst[0:SIDE] = turned(fore[lax.rem(code, 4)], code >= 4)
        dst[SIDE:STRIPS] = turned(back[own_side], code_at(edge, me, own_side) >= 4)

    def relayed(offset, read_corner, own_corner):
        return corner_block(
            code_at(corner, block(offset), read_corner), fore_corners, back_corners[own_corner]
        )

    strips(vp, width, N, S)
    vp[STRIPS : STRIPS + 16] = relayed(width + 1, NW, SE)
    vp[STRIPS + 16 : VROWS] = relayed(width - 1, NE, SW)
    strips(vm, -width, S, N)
    vm[STRIPS : STRIPS + 16] = relayed(-width + 1, SW, NE)
    vm[STRIPS + 16 : VROWS] = relayed(-width - 1, SE, NW)
    strips(hp, 1, W, E)
    strips(hm, -1, E, W)


def choose(even, one, two, ahead, behind):
    @pl.when(even)
    def _():
        ahead[...] = one[...]
        behind[...] = two[...]

    @pl.when(jnp.logical_not(even))
    def _():
        ahead[...] = two[...]
        behind[...] = one[...]


def even_row(me, width):
    return (me // width) % 2 == 0


def even_column(me):
    return me % 2 == 0


def put_row(dst, pair, part, row, west, east):
    col = iota((SIDE, CH), 0)
    wide = row.astype(F32)
    dst[1, pair, part] = row.astype(BF16)
    dst[0, pair, part] = jnp.where(col == 0, west, pltpu.roll(wide, 1, 0)).astype(BF16)
    dst[2, pair, part] = jnp.where(col == SIDE - 1, east, pltpu.roll(wide, SIDE - 1, 0)).astype(BF16)


def shift_copies(dst, src, west=None, east=None):
    def step(k, _):
        for part in range(2):
            i = 2 * k + part
            w = 0.0 if west is None else west[pl.ds(i, 1), :]
            e = 0.0 if east is None else east[pl.ds(i, 1), :]
            put_row(dst, k + part, 1 - part, src[k, part], w, e)
        return 0

    lax.fori_loop(0, HALF, step, 0, unroll=4)


def halo_copies(dst, src, west, east, vp, vm, hp, hm):
    west[...] = hp[0:SIDE].astype(F32)
    east[...] = hm[0:SIDE].astype(F32)
    shift_copies(dst, src, west, east)
    hp1 = hp[STRIPS : STRIPS + 16].astype(F32)
    hp2 = hp[STRIPS + 16 : VROWS].astype(F32)
    hm1 = hm[STRIPS : STRIPS + 16].astype(F32)
    hm2 = hm[STRIPS + 16 : VROWS].astype(F32)
    put_row(dst, 0, 0, vp[0:SIDE], hp1[0:1], hm1[0:1])
    put_row(dst, HALF, 1, vm[0:SIDE], hp2[0:1], hm2[0:1])


def zero_copies(dst, src):
    zero = jnp.zeros((SIDE, CH), BF16)
    for b in range(3):
        dst[b, 0, 0] = zero
        dst[b, HALF, 1] = zero
    shift_copies(dst, src)


def window(copies, m, mb):
    parts = [
        copies[b, pl.ds(m + a // 2, mb), a % 2].reshape(mb * SIDE, CH)
        for a in range(4)
        for b in range(3)
    ]
    return jnp.concatenate(parts, axis=1)


def conv_pairs(copies, weights, m, mb):
    return jnp.dot(window(copies, m, mb), weights[...], preferred_element_type=F32)


def edge_tap(side, k):
    return {N: (0, k), S: (2, k), W: (k, 0), E: (k, 2)}[side]


CORNER_TAP = {NW: (0, 0), NE: (0, 2), SE: (2, 2), SW: (2, 0)}


def neighbours(strip):
    row = iota((SIDE, CH), 0)
    up = jnp.where(row == SIDE - 1, 0.0, pltpu.roll(strip, SIDE - 1, 0))
    down = jnp.where(row == 0, 0.0, pltpu.roll(strip, 1, 0))
    return up, down


def tap_plain(weights, a, b):
    at = (a * 3 + b) * CH
    return weights[at : at + CH, 0:CH]


def tap_transposed(turned_weights, a, b):
    at = ((2 - a) * 3 + 2 - b) * CH
    return turned_weights[at : at + CH, 0:CH]


def returned(me, edge, corner, count, width, turned_weights, vp, vm, hp, hm, adds, pieces=None, corners=None):
    def block(offset):
        return lax.rem(me + offset + 2 * count, count)

    adds[...] = jnp.zeros_like(adds)
    row = iota((SIDE, CH), 0)
    for side, offset, message in ((N, width, vm), (E, -1, hp), (S, -width, vp), (W, 1, hm)):
        code = code_at(edge, block(offset), side)
        flip = code >= 4
        strip = message[SIDE:STRIPS].astype(F32)
        up, down = neighbours(strip)
        joined = jnp.concatenate(
            [jnp.where(flip, down, up), strip, jnp.where(flip, up, down)], axis=1
        ).astype(BF16)
        if pieces is not None:
            pieces[side] = joined
        taps = jnp.concatenate(
            [tap_transposed(turned_weights, *edge_tap(side, k)) for k in range(3)], axis=0
        )
        at = lax.rem(code, 4)
        adds[at] = adds[at] + jnp.dot(joined, taps, preferred_element_type=F32)
    for q, offset, message, start in (
        (NW, width + 1, hm, STRIPS + 16),
        (NE, width - 1, hp, STRIPS + 16),
        (SE, -width - 1, hp, STRIPS),
        (SW, -width + 1, hm, STRIPS),
    ):
        code = code_at(corner, block(offset), q)
        cells = message[start : start + 16]
        if corners is not None:
            corners[q] = cells
        given = jnp.dot(
            cells, tap_transposed(turned_weights, *CORNER_TAP[q]), preferred_element_type=F32
        )[1:2]
        first = jnp.where(row == 0, given, 0.0)
        last = jnp.where(row == SIDE - 1, given, 0.0)
        adds[N] = adds[N] + jnp.where(code == NW, first, 0.0) + jnp.where(code == NE, last, 0.0)
        adds[S] = adds[S] + jnp.where(code == SW, first, 0.0) + jnp.where(code == SE, last, 0.0)


def with_adds(rows, i, adds, first=False, last=False):
    col = iota((8, CH), 0)
    rows = jnp.concatenate(
        [
            rows[0:8] + jnp.where(col == 0, adds[W, pl.ds(i, 1), :], 0.0),
            rows[8 : SIDE - 8],
            rows[SIDE - 8 :] + jnp.where(col == 7, adds[E, pl.ds(i, 1), :], 0.0),
        ],
        axis=0,
    )
    if first:
        rows = rows + adds[N]
    if last:
        rows = rows + adds[S]
    return rows


def pad_sides(vp, vm, hp, hm):
    return ((N, vp), (S, vm), (W, hp), (E, hm))


def pad_corners(hp, hm):
    return ((NW, hp, STRIPS), (NE, hm, STRIPS), (SE, hm, STRIPS + 16), (SW, hp, STRIPS + 16))


def received(weights, vp, vm, hp, hm, adds):
    row = iota((SIDE, CH), 0)
    for side, message in pad_sides(vp, vm, hp, hm):
        strip = message[0:SIDE].astype(F32)
        up, down = neighbours(strip)
        joined = jnp.concatenate([down, strip, up], axis=1).astype(BF16)
        taps = jnp.concatenate([tap_plain(weights, *edge_tap(side, k)) for k in range(3)], axis=0)
        adds[side] = jnp.dot(joined, taps, preferred_element_type=F32)
    for q, message, start in pad_corners(hp, hm):
        cells = message[start : start + 16]
        given = jnp.dot(cells, tap_plain(weights, *CORNER_TAP[q]), preferred_element_type=F32)[0:1]
        side = N if q in (NW, NE) else S
        place = 0 if q in (NW, SW) else SIDE - 1
        adds[side] = adds[side] + jnp.where(row == place, given, 0.0)


def pack_kernel(count, width, me, edge, corner, fields, upstream, va, vb, hp, hm, here, fore, back, vp, vm):
    here[...] = upstream[...]
    side_strips(fields, fore)
    side_strips(upstream, back)
    pack(me[0], edge, corner, count, width, fore, back, vp, vm, hp, hm)
    choose(even_row(me[0], width), vp, vm, va, vb)


def relay_kernel(width, me, one, two, hp, hm, vp, vm, ha, hb):
    choose(even_row(me[0], width), two, one, vp, vm)

    def send(even, right, left):
        @pl.when(even)
        def _():
            for own, dst, start in ((hp, right, STRIPS), (hm, left, STRIPS + 16)):
                dst[0:STRIPS] = own[...]
                dst[STRIPS : STRIPS + 16] = vp[start : start + 16]
                dst[STRIPS + 16 : VROWS] = vm[start : start + 16]

    even = even_column(me[0])
    send(even, ha, hb)
    send(jnp.logical_not(even), hb, ha)


def name_kernel(me, one, two, hp, hm):
    choose(even_column(me[0]), two, one, hp, hm)


def plain_weights(source, dst):
    zero = jnp.zeros((CH, CH), BF16)
    for b in range(3):
        for a in range(3):
            at = (a * 3 + b) * CH
            dst[at : at + CH, 0:CH] = source[a, b]
            dst[at + 3 * CH : at + 4 * CH, CH : 2 * CH] = source[a, b]
        dst[(9 + b) * CH : (10 + b) * CH, 0:CH] = zero
        dst[b * CH : (b + 1) * CH, CH : 2 * CH] = zero


def turned_weights(source, dst):
    zero = jnp.zeros((CH, CH), BF16)
    for b in range(3):
        for a in range(3):
            at = (a * 3 + b) * CH
            swapped = source[2 - a, 2 - b].astype(F32).T.astype(BF16)
            dst[at : at + CH, 0:CH] = swapped
            dst[at + 3 * CH : at + 4 * CH, CH : 2 * CH] = swapped
        dst[(9 + b) * CH : (10 + b) * CH, 0:CH] = zero
        dst[b * CH : (b + 1) * CH, CH : 2 * CH] = zero


def conv_all(copies, weights, dst):
    mb = 16

    def step(n, _):
        m = n * mb
        got = conv_pairs(copies, weights, m, mb)
        for part in range(2):
            lanes = slice(part * CH, (part + 1) * CH)
            dst[pl.ds(m, mb), part] = got[:, lanes].reshape(mb, SIDE, CH).astype(dst.dtype)
        return 0

    lax.fori_loop(0, HALF // mb, step, 0)


def back_kernel(token, kernel_two, upstream, in_two, up_copies, grad):
    turned_weights(kernel_two, in_two)
    zero_copies(up_copies, upstream)
    conv_all(up_copies, in_two, grad)


def fore_kernel(token, kernel_one, fields, fwd_one, copies, pre):
    plain_weights(kernel_one, fwd_one)
    zero_copies(copies, fields)
    conv_all(copies, fwd_one, pre)


def middle_kernel(
    count, width, me, edge, corner, vp, vm, one_side, other_side, fwd_one, in_two, pre, grad,
    hidden, grad_pre, va2, vb2, hp2, hm2, fore, back, pieces, corners, hp, hm,
    grad_adds, pre_adds, vp2, vm2,
):
    choose(even_column(me[0]), other_side, one_side, hp, hm)
    returned(me[0], edge, corner, count, width, in_two, vp, vm, hp, hm, grad_adds, pieces, corners)
    received(fwd_one, vp, vm, hp, hm, pre_adds)

    def one(m, part, first=False, last=False):
        i = 2 * m + part
        p = with_adds(pre[m, part], i, pre_adds, first, last)
        g = with_adds(grad[m, part], i, grad_adds, first, last)
        s = 1.0 / (1.0 + jnp.exp(-p))
        hidden[m, part] = (p * s).astype(BF16)
        grad_pre[m, part] = (g * s * (1.0 + p * (1.0 - s))).astype(BF16)

    def step(m, _):
        one(m, 0)
        one(m, 1)
        return 0

    one(0, 0, first=True)
    one(0, 1)
    lax.fori_loop(1, HALF - 1, step, 0, unroll=2)
    one(HALF - 1, 0)
    one(HALF - 1, 1, last=True)
    side_strips(hidden, fore)
    side_strips(grad_pre, back)
    pack(me[0], edge, corner, count, width, fore, back, vp2, vm2, hp2, hm2)
    choose(even_row(me[0], width), vp2, vm2, va2, vb2)


def sums_kernel(
    count, width, scale, kept, me, edge, corner, vp, vm, hp, hm, hidden, grad_pre, field_copies, up_copies,
    fore, back, pieces, corners, sums, acc,
):
    gb = 8
    first = (((0,), (0,)), ((), ()))

    def gather(values, shifted):
        def grad_step(n, _):
            m = n * gb
            left = jnp.concatenate(
                [values[pl.ds(m, gb), part].reshape(gb * SIDE, CH) for part in range(2)], axis=1
            )
            acc[...] += lax.dot_general(left, window(shifted, m, gb), first, preferred_element_type=F32)
            return 0

        acc[...] = jnp.zeros_like(acc)
        lax.fori_loop(0, HALF // gb, grad_step, 0)

    def from_acc(a, b):
        low = (a * 3 + b) * CH
        high = low + 3 * CH
        return acc[0:CH, low : low + CH] + acc[CH : 2 * CH, high : high + CH]

    def add(tap, term):
        at = (tap[0] * 3 + tap[1]) * CH
        sums[at : at + CH] = sums[at : at + CH] + term * scale

    def block(offset):
        return lax.rem(me[0] + offset + 2 * count, count)

    row = iota((16, CH), 0)
    high = (me[0] // FIRST) % 2

    @pl.when(high == (0 if kept else 1))
    def _():
        gather(grad_pre, field_copies)
        for a in range(3):
            for b in range(3):
                at = (a * 3 + b) * CH
                sums[at : at + CH] = from_acc(a, b).T * scale
        for side, message in pad_sides(vp, vm, hp, hm):
            strip = back[side]
            up, down = neighbours(strip)
            joined = jnp.concatenate([up, strip, down], axis=1).astype(BF16)
            term = lax.dot_general(message[0:SIDE], joined, first, preferred_element_type=F32)
            for k in range(3):
                add(edge_tap(side, k), term[:, k * CH : (k + 1) * CH])
        own = corner_rows(back)
        for q, message, start in pad_corners(hp, hm):
            right = jnp.where(row == 0, own[q], 0.0).astype(BF16)
            add(CORNER_TAP[q], lax.dot_general(message[start : start + 16], right, first, preferred_element_type=F32))

    @pl.when(high == (1 if kept else 0))
    def _():
        gather(hidden, up_copies)
        for a in range(3):
            for b in range(3):
                at = (a * 3 + b) * CH
                sums[at : at + CH] = from_acc(2 - a, 2 - b) * scale
        for side, offset in ((N, width), (E, -1), (S, -width), (W, 1)):
            code = lax.rem(code_at(edge, block(offset), side), 4)
            term = lax.dot_general(fore[code].astype(BF16), pieces[side], first, preferred_element_type=F32)
            for k in range(3):
                add(edge_tap(side, k), term[:, k * CH : (k + 1) * CH])
        own = corner_rows(fore)
        for q, offset in ((NW, width + 1), (NE, width - 1), (SE, -width - 1), (SW, -width + 1)):
            code = code_at(corner, block(offset), q)
            cell = jnp.where(code == 0, own[0], jnp.where(code == 1, own[1], jnp.where(code == 2, own[2], own[3])))
            left = jnp.where(row == 1, cell, 0.0).astype(BF16)
            add(CORNER_TAP[q], lax.dot_general(left, corners[q], first, preferred_element_type=F32))


def weights_kernel(token, kernel_one, kernel_two, in_one, fwd_two):
    turned_weights(kernel_one, in_one)
    plain_weights(kernel_two, fwd_two)


def outputs_kernel(hidden, vp, vm, hp, hm, fwd_two, outputs, copies, west, east):
    halo_copies(copies, hidden, west, east, vp, vm, hp, hm)
    conv_all(copies, fwd_two, outputs)


def grads_kernel(
    count, width, me, edge, corner, vp, vm, hp, hm, grad_pre, in_one, grad_fields, copies, adds
):
    mb = 8
    returned(me[0], edge, corner, count, width, in_one, vp, vm, hp, hm, adds)
    zero_copies(copies, grad_pre)

    def rows(n, first=False, last=False):
        m = n * mb
        got = conv_pairs(copies, in_one, m, mb)
        for k in range(mb):
            for part in range(2):
                g = with_adds(
                    got[k * SIDE : (k + 1) * SIDE, part * CH : (part + 1) * CH],
                    2 * (m + k) + part, adds,
                    first and k == 0 and part == 0, last and k == mb - 1 and part == 1,
                )
                grad_fields[m + k, part] = g.astype(BF16)

    def step(n, _):
        rows(n)
        return 0

    rows(0, first=True)
    lax.fori_loop(1, HALF // mb - 1, step, 0)
    rows(HALF // mb - 1, last=True)


def fold_kernel(parts, copies):
    folded = jnp.sum(parts[...].astype(F32), axis=0).astype(copies.dtype)
    for k in range(copies.shape[0]):
        copies[k] = folded


def finish_kernel(me, mine, other, first, second):
    high = (me[0] // FIRST) % 2

    @pl.when(high == 0)
    def _():
        first[...] = mine[...].astype(F32)
        second[...] = other[...].astype(F32)

    @pl.when(high == 1)
    def _():
        first[...] = other[...].astype(F32)
        second[...] = mine[...].astype(F32)


def struct(shape, dtype=BF16):
    return jax.ShapeDtypeStruct(shape, dtype)


BLOCK = (HALF, 2, SIDE, CH)
COPIES = (3, HALF + 1, 2, SIDE, CH)
WEIGHTS = (12 * CH, 2 * CH)


def call(body, tables, arrays, outs, scratch=(), flops=0, moved=4 << 20):
    return pl.pallas_call(
        body,
        out_shape=outs,
        in_specs=[SMEM] * tables + [VMEM] * arrays,
        out_specs=tuple(VMEM for _ in outs),
        scratch_shapes=list(scratch),
        compiler_params=pltpu.CompilerParams(vmem_limit_bytes=ROOM),
        cost_estimate=pl.CostEstimate(flops=flops, bytes_accessed=moved, transcendentals=0),
    )


def swap(x, bit):
    size = lax.axis_size(AXES)
    return lax.ppermute(x, AXES, [(i, i ^ bit) for i in range(size)])


def both_ways(one, two, step):
    size = lax.axis_size(AXES)

    def pairs(turn):
        return [(i, (i + (step if (i // step + turn) % 2 == 0 else -step)) % size) for i in range(size)]

    return lax.ppermute(one, AXES, pairs(0)), lax.ppermute(two, AXES, pairs(1))


FIRST = 2
PLANE = (128, 64, 32, 1)
RING = (16, 8, 4)


def groups_over(bits, size):
    rest = [i for i in range(size) if i & sum(bits) == 0]
    members = [sum(bit for k, bit in enumerate(bits) if n >> k & 1) for n in range(1 << len(bits))]
    return [[base + member for member in members] for base in rest]


def total(send, done, works):
    me = lax.axis_index(AXES).astype(jnp.int32)
    plane, ring = [groups_over(bits, lax.axis_size(AXES)) for bits in (PLANE, RING)]
    steps = [0]

    def scatter(groups):
        return lambda sent: lax.all_to_all(sent, AXES, 0, 0, axis_index_groups=groups, tiled=True)

    def beside(sent, move):
        work = works.get(steps[0])
        steps[0] += 1
        if work is None:
            return move(sent)
        sent, held = lax.optimization_barrier((sent, done.copy()))
        done.update(held)
        got = move(sent)
        gave = work(done)
        got, gave = lax.optimization_barrier((got, gave))
        done.update(gave)
        return got

    def fold(x, parts, dtype):
        folded, = call(fold_kernel, 0, 1, (struct((parts,) + x.shape[1:], dtype),), (), 0, 1 << 19)(x)
        return folded

    def across(sent):
        return swap(sent, FIRST)

    x = beside(send, across)
    x = (done["keep"] + x).astype(BF16)
    parts = len(plane[0])
    x = beside(x.reshape(parts, x.shape[0] // parts, CH), scatter(plane))
    x = beside(fold(x, len(ring[0]), BF16), scatter(ring))
    x = beside(fold(x, parts, BF16), scatter(plane)).reshape(-1, CH)
    out = struct(x.shape, F32)
    grads = call(finish_kernel, 1, 2, (out, out))(me.reshape(1), x, beside(x, across))
    return grads, done


def local(inputs, kernel_one, kernel_two, cotangent, edge_codes, corner_codes):
    count = lax.axis_size(AXES)
    width = lax.axis_size("face") // GRID_ROWS * lax.axis_size("sub")
    scale = 1.0 / math.sqrt(count * SIDE * SIDE)
    me = lax.axis_index(AXES).astype(jnp.int32).reshape(1)
    tables = (me, jnp.transpose(edge_codes, (1, 2, 0)), jnp.transpose(corner_codes, (1, 2, 0)))
    fields = inputs.reshape(BLOCK)
    upstream = cotangent.reshape(BLOCK)
    message = struct((VROWS, CH))
    own = struct((STRIPS, CH))
    weights = struct(WEIGHTS)
    block = struct(BLOCK)
    taps = struct((3, 3, CH, CH))
    copies = struct(COPIES)
    wide = struct(BLOCK, F32)
    sides = (4, SIDE, CH)
    strips = pltpu.VMEM(sides, F32)
    vertical_pair = pltpu.VMEM((VROWS, CH), BF16)
    column = pltpu.VMEM((SIDE, CH), F32)
    conv_flops = 2 * SIDE * SIDE * 9 * CH * CH

    va, vb, hp, hm, upstream = call(
        lambda *refs: pack_kernel(count, width, *refs), 3, 2, (message, message, own, own, block),
        [strips, strips, vertical_pair, vertical_pair],
    )(*tables, fields, upstream)
    va, vb, token = lax.optimization_barrier((va, vb, me))
    va, vb = both_ways(va, vb, width)
    in_two, up_copies, grad = call(back_kernel, 1, 2, (weights, copies, wide), (), conv_flops)(
        token, kernel_two, upstream
    )
    va, vb, in_two, up_copies, grad, token = lax.optimization_barrier(
        (va, vb, in_two, up_copies, grad, token)
    )

    def relay(token, va, vb, hp, hm):
        return call(
            lambda *refs: relay_kernel(width, *refs), 1, 4, (message, message, message, message), (), 0, 1 << 18
        )(token, va, vb, hp, hm)

    vp, vm, ha, hb = relay(token, va, vb, hp, hm)
    ha, hb, token = lax.optimization_barrier((ha, hb, token))
    ha, hb = both_ways(ha, hb, 1)
    fwd_one, field_copies, pre = call(fore_kernel, 1, 2, (weights, copies, wide), (), conv_flops)(
        token, kernel_one, fields
    )
    hidden, grad_pre, va2, vb2, hp2, hm2, fore, back, pieces, corners, hp, hm = call(
        lambda *refs: middle_kernel(count, width, *refs), 3, 8,
        (
            block, block, message, message, own, own, struct(sides, F32), struct(sides, F32),
            struct((4, SIDE, 3 * CH)), struct((4, 16, CH)),
            message, message,
        ),
        [strips, strips, vertical_pair, vertical_pair], conv_flops,
    )(*tables, vp, vm, ha, hb, fwd_one, in_two, pre, grad)
    hidden, grad_pre, va2, vb2, token = lax.optimization_barrier((hidden, grad_pre, va2, vb2, token))
    def half(kept, token):
        got, = call(
            lambda me, *refs: sums_kernel(count, width, scale, kept, me, *refs), 3, 12,
            (struct((9 * CH, CH), F32),), [pltpu.VMEM((2 * CH, 12 * CH), F32)], conv_flops,
        )(
            token, *tables[1:], vp, vm, hp, hm, hidden, grad_pre, field_copies, up_copies,
            fore, back, pieces, corners,
        )
        return got

    def first_work(done):
        va, vb = both_ways(done["va"], done["vb"], width)
        return dict(keep=half(True, done["token"]), va=va, vb=vb)

    def second_work(done):
        vp, vm, ha, hb = relay(done["token"], done["va"], done["vb"], hp2, hm2)
        ha, hb = both_ways(ha, hb, 1)
        return dict(vp=vp, vm=vm, ha=ha, hb=hb)

    def third_work(done):
        hp, hm = call(name_kernel, 1, 2, (message, message), (), 0, 1 << 18)(
            done["token"], done["ha"], done["hb"]
        )
        in_one, fwd_two = call(weights_kernel, 1, 2, (weights, weights))(
            done["token"], kernel_one, kernel_two
        )
        outputs, = call(
            outputs_kernel, 0, 6, (block,), [pltpu.VMEM(COPIES, BF16), column, column], conv_flops
        )(hidden, done["vp"], done["vm"], hp, hm, fwd_two)
        grad_fields, = call(
            lambda *refs: grads_kernel(count, width, *refs), 3, 6, (block,),
            [pltpu.VMEM(COPIES, BF16), strips], conv_flops,
        )(*tables, done["vp"], done["vm"], hp, hm, grad_pre, in_one)
        return dict(outputs=outputs, grad_fields=grad_fields)

    grads, done = total(
        half(False, token), dict(va=va2, vb=vb2, token=token),
        {0: first_work, 1: second_work, 2: third_work},
    )
    shape = (1, 1, SIDE, SIDE, CH)
    return (
        done["outputs"].reshape(shape), done["grad_fields"].reshape(shape),
        grads[0].reshape(taps.shape), grads[1].reshape(taps.shape),
    )


def solution(mesh):
    block = P("face", "sub", None, None, None)
    return jax.shard_map(
        local,
        mesh=mesh,
        in_specs=(block, P(), P(), block, P(), P()),
        out_specs=(block, block, P(), P()),
        check_vma=False,
    )
```

```python
import math

import jax
import jax.numpy as jnp
from jax import lax
from jax.experimental import pallas as pl
from jax.experimental.pallas import tpu as pltpu
from jax.sharding import PartitionSpec as P

AXES = ("face", "sub")
GRID_ROWS = 8
SIDE = 64
CH = 128
HALF = SIDE // 2
STRIPS = 2 * SIDE
VROWS = STRIPS + 32
BF16 = jnp.bfloat16
F32 = jnp.float32
N, E, S, W = 0, 1, 2, 3
NW, NE, SE, SW = 0, 1, 2, 3
VMEM = pl.BlockSpec(memory_space=pltpu.VMEM)
SMEM = pl.BlockSpec(memory_space=pltpu.SMEM)
ROOM = 20 << 20


def code_at(table, block, which):
    return table[block % 2, which, block // 2]


def iota(shape, dim):
    return lax.broadcasted_iota(jnp.int32, shape, dim)


def strips_from(north, south, low, high, dst):
    dst[N] = north.astype(F32)
    dst[S] = south.astype(F32)
    low = low.reshape(SIDE, 16, CH).astype(F32)
    dst[W] = jnp.sum(jnp.where(iota(low.shape, 1) == 0, low, 0.0), axis=1)
    high = high.reshape(SIDE, 16, CH).astype(F32)
    dst[E] = jnp.sum(jnp.where(iota(high.shape, 1) == 15, high, 0.0), axis=1)


def side_strips(block, dst):
    strips_from(
        block[0, 0], block[HALF - 1, 1], block[:, :, 0:16, :], block[:, :, SIDE - 16 : SIDE, :], dst
    )


def corner_rows(strips):
    north = strips[N]
    south = strips[S]
    last = SIDE - 1
    return [north[0:1], north[last : last + 1], south[last : last + 1], south[0:1]]


def turned(strip, flip):
    row = iota((SIDE, SIDE), 0)
    col = iota((SIDE, SIDE), 1)
    target = jnp.where(flip, SIDE - 1 - row, row)
    matrix = jnp.where(col == target, 1.0, 0.0).astype(BF16)
    return jnp.dot(matrix, strip.astype(BF16), preferred_element_type=F32).astype(BF16)


def corner_block(code, own, other):
    picked = jnp.where(code == 0, own[0], jnp.where(code == 1, own[1], jnp.where(code == 2, own[2], own[3])))
    row = iota((16, CH), 0)
    return (jnp.where(row == 0, picked, 0.0) + jnp.where(row == 1, other, 0.0)).astype(BF16)


def pack(me, edge, corner, count, width, fore, back, vp, vm, hp, hm):
    fore_corners = corner_rows(fore)
    back_corners = corner_rows(back)

    def block(offset):
        return lax.rem(me + offset + 2 * count, count)

    def strips(dst, offset, read_side, own_side):
        code = code_at(edge, block(offset), read_side)
        dst[0:SIDE] = turned(fore[lax.rem(code, 4)], code >= 4)
        dst[SIDE:STRIPS] = turned(back[own_side], code_at(edge, me, own_side) >= 4)

    def relayed(offset, read_corner, own_corner):
        return corner_block(
            code_at(corner, block(offset), read_corner), fore_corners, back_corners[own_corner]
        )

    strips(vp, width, N, S)
    vp[STRIPS : STRIPS + 16] = relayed(width + 1, NW, SE)
    vp[STRIPS + 16 : VROWS] = relayed(width - 1, NE, SW)
    strips(vm, -width, S, N)
    vm[STRIPS : STRIPS + 16] = relayed(-width + 1, SW, NE)
    vm[STRIPS + 16 : VROWS] = relayed(-width - 1, SE, NW)
    strips(hp, 1, W, E)
    strips(hm, -1, E, W)


def choose(even, one, two, ahead, behind):
    @pl.when(even)
    def _():
        ahead[...] = one[...]
        behind[...] = two[...]

    @pl.when(jnp.logical_not(even))
    def _():
        ahead[...] = two[...]
        behind[...] = one[...]


def even_row(me, width):
    return (me // width) % 2 == 0


def even_column(me):
    return me % 2 == 0


def put_row(dst, pair, part, row, west, east):
    col = iota((SIDE, CH), 0)
    wide = row.astype(F32)
    dst[1, pair, part] = row.astype(BF16)
    dst[0, pair, part] = jnp.where(col == 0, west, pltpu.roll(wide, 1, 0)).astype(BF16)
    dst[2, pair, part] = jnp.where(col == SIDE - 1, east, pltpu.roll(wide, SIDE - 1, 0)).astype(BF16)


def shift_copies(dst, src, west=None, east=None):
    def step(k, _):
        for part in range(2):
            i = 2 * k + part
            w = 0.0 if west is None else west[pl.ds(i, 1), :]
            e = 0.0 if east is None else east[pl.ds(i, 1), :]
            put_row(dst, k + part, 1 - part, src[k, part], w, e)
        return 0

    lax.fori_loop(0, HALF, step, 0, unroll=4)


def halo_copies(dst, src, west, east, vp, vm, hp, hm):
    west[...] = hp[0:SIDE].astype(F32)
    east[...] = hm[0:SIDE].astype(F32)
    shift_copies(dst, src, west, east)
    hp1 = hp[STRIPS : STRIPS + 16].astype(F32)
    hp2 = hp[STRIPS + 16 : VROWS].astype(F32)
    hm1 = hm[STRIPS : STRIPS + 16].astype(F32)
    hm2 = hm[STRIPS + 16 : VROWS].astype(F32)
    put_row(dst, 0, 0, vp[0:SIDE], hp1[0:1], hm1[0:1])
    put_row(dst, HALF, 1, vm[0:SIDE], hp2[0:1], hm2[0:1])


def zero_copies(dst, src):
    zero = jnp.zeros((SIDE, CH), BF16)
    for b in range(3):
        dst[b, 0, 0] = zero
        dst[b, HALF, 1] = zero
    shift_copies(dst, src)


def window(copies, m, mb):
    parts = [
        copies[b, pl.ds(m + a // 2, mb), a % 2].reshape(mb * SIDE, CH)
        for a in range(4)
        for b in range(3)
    ]
    return jnp.concatenate(parts, axis=1)


def conv_pairs(copies, weights, m, mb):
    return jnp.dot(window(copies, m, mb), weights[...], preferred_element_type=F32)


def edge_tap(side, k):
    return {N: (0, k), S: (2, k), W: (k, 0), E: (k, 2)}[side]


CORNER_TAP = {NW: (0, 0), NE: (0, 2), SE: (2, 2), SW: (2, 0)}


def neighbours(strip):
    row = iota((SIDE, CH), 0)
    up = jnp.where(row == SIDE - 1, 0.0, pltpu.roll(strip, SIDE - 1, 0))
    down = jnp.where(row == 0, 0.0, pltpu.roll(strip, 1, 0))
    return up, down


def tap_plain(weights, a, b):
    at = (a * 3 + b) * CH
    return weights[at : at + CH, 0:CH]


def tap_transposed(turned_weights, a, b):
    at = ((2 - a) * 3 + 2 - b) * CH
    return turned_weights[at : at + CH, 0:CH]


def returned(me, edge, corner, count, width, turned_weights, vp, vm, hp, hm, adds, pieces=None, corners=None):
    def block(offset):
        return lax.rem(me + offset + 2 * count, count)

    adds[...] = jnp.zeros_like(adds)
    row = iota((SIDE, CH), 0)
    for side, offset, message in ((N, width, vm), (E, -1, hp), (S, -width, vp), (W, 1, hm)):
        code = code_at(edge, block(offset), side)
        flip = code >= 4
        strip = message[SIDE:STRIPS].astype(F32)
        up, down = neighbours(strip)
        joined = jnp.concatenate(
            [jnp.where(flip, down, up), strip, jnp.where(flip, up, down)], axis=1
        ).astype(BF16)
        if pieces is not None:
            pieces[side] = joined
        taps = jnp.concatenate(
            [tap_transposed(turned_weights, *edge_tap(side, k)) for k in range(3)], axis=0
        )
        at = lax.rem(code, 4)
        adds[at] = adds[at] + jnp.dot(joined, taps, preferred_element_type=F32)
    for q, offset, message, start in (
        (NW, width + 1, hm, STRIPS + 16),
        (NE, width - 1, hp, STRIPS + 16),
        (SE, -width - 1, hp, STRIPS),
        (SW, -width + 1, hm, STRIPS),
    ):
        code = code_at(corner, block(offset), q)
        cells = message[start : start + 16]
        if corners is not None:
            corners[q] = cells
        given = jnp.dot(
            cells, tap_transposed(turned_weights, *CORNER_TAP[q]), preferred_element_type=F32
        )[1:2]
        first = jnp.where(row == 0, given, 0.0)
        last = jnp.where(row == SIDE - 1, given, 0.0)
        adds[N] = adds[N] + jnp.where(code == NW, first, 0.0) + jnp.where(code == NE, last, 0.0)
        adds[S] = adds[S] + jnp.where(code == SW, first, 0.0) + jnp.where(code == SE, last, 0.0)


def with_adds(rows, i, adds, first=False, last=False):
    col = iota((8, CH), 0)
    rows = jnp.concatenate(
        [
            rows[0:8] + jnp.where(col == 0, adds[W, pl.ds(i, 1), :], 0.0),
            rows[8 : SIDE - 8],
            rows[SIDE - 8 :] + jnp.where(col == 7, adds[E, pl.ds(i, 1), :], 0.0),
        ],
        axis=0,
    )
    if first:
        rows = rows + adds[N]
    if last:
        rows = rows + adds[S]
    return rows


def pad_sides(vp, vm, hp, hm):
    return ((N, vp), (S, vm), (W, hp), (E, hm))


def pad_corners(hp, hm):
    return ((NW, hp, STRIPS), (NE, hm, STRIPS), (SE, hm, STRIPS + 16), (SW, hp, STRIPS + 16))


def received(weights, vp, vm, hp, hm, adds):
    row = iota((SIDE, CH), 0)
    for side, message in pad_sides(vp, vm, hp, hm):
        strip = message[0:SIDE].astype(F32)
        up, down = neighbours(strip)
        joined = jnp.concatenate([down, strip, up], axis=1).astype(BF16)
        taps = jnp.concatenate([tap_plain(weights, *edge_tap(side, k)) for k in range(3)], axis=0)
        adds[side] = jnp.dot(joined, taps, preferred_element_type=F32)
    for q, message, start in pad_corners(hp, hm):
        cells = message[start : start + 16]
        given = jnp.dot(cells, tap_plain(weights, *CORNER_TAP[q]), preferred_element_type=F32)[0:1]
        side = N if q in (NW, NE) else S
        place = 0 if q in (NW, SW) else SIDE - 1
        adds[side] = adds[side] + jnp.where(row == place, given, 0.0)


def pack_kernel(count, width, me, edge, corner, fields, upstream, va, vb, hp, hm, here, fore, back, vp, vm):
    here[...] = upstream[...]
    side_strips(fields, fore)
    side_strips(upstream, back)
    pack(me[0], edge, corner, count, width, fore, back, vp, vm, hp, hm)
    choose(even_row(me[0], width), vp, vm, va, vb)


def relay_kernel(width, me, one, two, hp, hm, vp, vm, ha, hb):
    choose(even_row(me[0], width), two, one, vp, vm)

    def send(even, right, left):
        @pl.when(even)
        def _():
            for own, dst, start in ((hp, right, STRIPS), (hm, left, STRIPS + 16)):
                dst[0:STRIPS] = own[...]
                dst[STRIPS : STRIPS + 16] = vp[start : start + 16]
                dst[STRIPS + 16 : VROWS] = vm[start : start + 16]

    even = even_column(me[0])
    send(even, ha, hb)
    send(jnp.logical_not(even), hb, ha)


def name_kernel(me, one, two, hp, hm):
    choose(even_column(me[0]), two, one, hp, hm)


def plain_weights(source, dst):
    zero = jnp.zeros((CH, CH), BF16)
    for b in range(3):
        for a in range(3):
            at = (a * 3 + b) * CH
            dst[at : at + CH, 0:CH] = source[a, b]
            dst[at + 3 * CH : at + 4 * CH, CH : 2 * CH] = source[a, b]
        dst[(9 + b) * CH : (10 + b) * CH, 0:CH] = zero
        dst[b * CH : (b + 1) * CH, CH : 2 * CH] = zero


def turned_weights(source, dst):
    zero = jnp.zeros((CH, CH), BF16)
    for b in range(3):
        for a in range(3):
            at = (a * 3 + b) * CH
            swapped = source[2 - a, 2 - b].astype(F32).T.astype(BF16)
            dst[at : at + CH, 0:CH] = swapped
            dst[at + 3 * CH : at + 4 * CH, CH : 2 * CH] = swapped
        dst[(9 + b) * CH : (10 + b) * CH, 0:CH] = zero
        dst[b * CH : (b + 1) * CH, CH : 2 * CH] = zero


def conv_all(copies, weights, dst):
    mb = 16

    def step(n, _):
        m = n * mb
        got = conv_pairs(copies, weights, m, mb)
        for part in range(2):
            lanes = slice(part * CH, (part + 1) * CH)
            dst[pl.ds(m, mb), part] = got[:, lanes].reshape(mb, SIDE, CH).astype(dst.dtype)
        return 0

    lax.fori_loop(0, HALF // mb, step, 0)


def back_kernel(token, kernel_two, upstream, in_two, up_copies, grad):
    turned_weights(kernel_two, in_two)
    zero_copies(up_copies, upstream)
    conv_all(up_copies, in_two, grad)


def fore_kernel(token, kernel_one, fields, fwd_one, copies, pre):
    plain_weights(kernel_one, fwd_one)
    zero_copies(copies, fields)
    conv_all(copies, fwd_one, pre)


def middle_kernel(
    count, width, me, edge, corner, vp, vm, one_side, other_side, fwd_one, in_two, pre, grad,
    hidden, grad_pre, va2, vb2, hp2, hm2, fore, back, pieces, corners, hp, hm,
    grad_adds, pre_adds, vp2, vm2,
):
    choose(even_column(me[0]), other_side, one_side, hp, hm)
    returned(me[0], edge, corner, count, width, in_two, vp, vm, hp, hm, grad_adds, pieces, corners)
    received(fwd_one, vp, vm, hp, hm, pre_adds)

    def one(m, part, first=False, last=False):
        i = 2 * m + part
        p = with_adds(pre[m, part], i, pre_adds, first, last)
        g = with_adds(grad[m, part], i, grad_adds, first, last)
        s = 1.0 / (1.0 + jnp.exp(-p))
        hidden[m, part] = (p * s).astype(BF16)
        grad_pre[m, part] = (g * s * (1.0 + p * (1.0 - s))).astype(BF16)

    def step(m, _):
        one(m, 0)
        one(m, 1)
        return 0

    one(0, 0, first=True)
    one(0, 1)
    lax.fori_loop(1, HALF - 1, step, 0, unroll=2)
    one(HALF - 1, 0)
    one(HALF - 1, 1, last=True)
    side_strips(hidden, fore)
    side_strips(grad_pre, back)
    pack(me[0], edge, corner, count, width, fore, back, vp2, vm2, hp2, hm2)
    choose(even_row(me[0], width), vp2, vm2, va2, vb2)


def sums_kernel(
    count, width, scale, kept, me, edge, corner, vp, vm, hp, hm, hidden, grad_pre, field_copies, up_copies,
    fore, back, pieces, corners, sums, acc,
):
    gb = 8
    first = (((0,), (0,)), ((), ()))

    def gather(values, shifted):
        def grad_step(n, _):
            m = n * gb
            left = jnp.concatenate(
                [values[pl.ds(m, gb), part].reshape(gb * SIDE, CH) for part in range(2)], axis=1
            )
            acc[...] += lax.dot_general(left, window(shifted, m, gb), first, preferred_element_type=F32)
            return 0

        acc[...] = jnp.zeros_like(acc)
        lax.fori_loop(0, HALF // gb, grad_step, 0)

    def from_acc(a, b):
        low = (a * 3 + b) * CH
        high = low + 3 * CH
        return acc[0:CH, low : low + CH] + acc[CH : 2 * CH, high : high + CH]

    def add(tap, term):
        at = (tap[0] * 3 + tap[1]) * CH
        sums[at : at + CH] = sums[at : at + CH] + term * scale

    def block(offset):
        return lax.rem(me[0] + offset + 2 * count, count)

    row = iota((16, CH), 0)
    high = (me[0] // FIRST) % 2

    @pl.when(high == (0 if kept else 1))
    def _():
        gather(grad_pre, field_copies)
        for a in range(3):
            for b in range(3):
                at = (a * 3 + b) * CH
                sums[at : at + CH] = from_acc(a, b).T * scale
        for side, message in pad_sides(vp, vm, hp, hm):
            strip = back[side]
            up, down = neighbours(strip)
            joined = jnp.concatenate([up, strip, down], axis=1).astype(BF16)
            term = lax.dot_general(message[0:SIDE], joined, first, preferred_element_type=F32)
            for k in range(3):
                add(edge_tap(side, k), term[:, k * CH : (k + 1) * CH])
        own = corner_rows(back)
        for q, message, start in pad_corners(hp, hm):
            right = jnp.where(row == 0, own[q], 0.0).astype(BF16)
            add(CORNER_TAP[q], lax.dot_general(message[start : start + 16], right, first, preferred_element_type=F32))

    @pl.when(high == (1 if kept else 0))
    def _():
        gather(hidden, up_copies)
        for a in range(3):
            for b in range(3):
                at = (a * 3 + b) * CH
                sums[at : at + CH] = from_acc(2 - a, 2 - b) * scale
        for side, offset in ((N, width), (E, -1), (S, -width), (W, 1)):
            code = lax.rem(code_at(edge, block(offset), side), 4)
            term = lax.dot_general(fore[code].astype(BF16), pieces[side], first, preferred_element_type=F32)
            for k in range(3):
                add(edge_tap(side, k), term[:, k * CH : (k + 1) * CH])
        own = corner_rows(fore)
        for q, offset in ((NW, width + 1), (NE, width - 1), (SE, -width - 1), (SW, -width + 1)):
            code = code_at(corner, block(offset), q)
            cell = jnp.where(code == 0, own[0], jnp.where(code == 1, own[1], jnp.where(code == 2, own[2], own[3])))
            left = jnp.where(row == 1, cell, 0.0).astype(BF16)
            add(CORNER_TAP[q], lax.dot_general(left, corners[q], first, preferred_element_type=F32))


def weights_kernel(token, kernel_one, kernel_two, in_one, fwd_two):
    turned_weights(kernel_one, in_one)
    plain_weights(kernel_two, fwd_two)


def outputs_kernel(hidden, vp, vm, hp, hm, fwd_two, outputs, copies, west, east):
    halo_copies(copies, hidden, west, east, vp, vm, hp, hm)
    conv_all(copies, fwd_two, outputs)


def grads_kernel(
    count, width, me, edge, corner, vp, vm, hp, hm, grad_pre, in_one, grad_fields, copies, adds
):
    mb = 8
    returned(me[0], edge, corner, count, width, in_one, vp, vm, hp, hm, adds)
    zero_copies(copies, grad_pre)

    def rows(n, first=False, last=False):
        m = n * mb
        got = conv_pairs(copies, in_one, m, mb)
        for k in range(mb):
            for part in range(2):
                g = with_adds(
                    got[k * SIDE : (k + 1) * SIDE, part * CH : (part + 1) * CH],
                    2 * (m + k) + part, adds,
                    first and k == 0 and part == 0, last and k == mb - 1 and part == 1,
                )
                grad_fields[m + k, part] = g.astype(BF16)

    def step(n, _):
        rows(n)
        return 0

    rows(0, first=True)
    lax.fori_loop(1, HALF // mb - 1, step, 0)
    rows(HALF // mb - 1, last=True)


def fold_kernel(parts, copies):
    folded = jnp.sum(parts[...].astype(F32), axis=0).astype(copies.dtype)
    for k in range(copies.shape[0]):
        copies[k] = folded


def finish_kernel(me, mine, other, first, second):
    high = (me[0] // FIRST) % 2

    @pl.when(high == 0)
    def _():
        first[...] = mine[...].astype(F32)
        second[...] = other[...].astype(F32)

    @pl.when(high == 1)
    def _():
        first[...] = other[...].astype(F32)
        second[...] = mine[...].astype(F32)


def struct(shape, dtype=BF16):
    return jax.ShapeDtypeStruct(shape, dtype)


BLOCK = (HALF, 2, SIDE, CH)
COPIES = (3, HALF + 1, 2, SIDE, CH)
WEIGHTS = (12 * CH, 2 * CH)


def call(body, tables, arrays, outs, scratch=(), flops=0, moved=4 << 20):
    return pl.pallas_call(
        body,
        out_shape=outs,
        in_specs=[SMEM] * tables + [VMEM] * arrays,
        out_specs=tuple(VMEM for _ in outs),
        scratch_shapes=list(scratch),
        compiler_params=pltpu.CompilerParams(vmem_limit_bytes=ROOM),
        cost_estimate=pl.CostEstimate(flops=flops, bytes_accessed=moved, transcendentals=0),
    )


def swap(x, bit):
    size = lax.axis_size(AXES)
    return lax.ppermute(x, AXES, [(i, i ^ bit) for i in range(size)])


def both_ways(one, two, step):
    size = lax.axis_size(AXES)

    def pairs(turn):
        return [(i, (i + (step if (i // step + turn) % 2 == 0 else -step)) % size) for i in range(size)]

    return lax.ppermute(one, AXES, pairs(0)), lax.ppermute(two, AXES, pairs(1))


FIRST = 2
PLANE = (128, 64, 32, 1)
RING = (16, 8, 4)


def groups_over(bits, size):
    rest = [i for i in range(size) if i & sum(bits) == 0]
    members = [sum(bit for k, bit in enumerate(bits) if n >> k & 1) for n in range(1 << len(bits))]
    return [[base + member for member in members] for base in rest]


def total(send, done, works):
    me = lax.axis_index(AXES).astype(jnp.int32)
    plane, ring = [groups_over(bits, lax.axis_size(AXES)) for bits in (PLANE, RING)]
    steps = [0]

    def scatter(groups):
        return lambda sent: lax.all_to_all(sent, AXES, 0, 0, axis_index_groups=groups, tiled=True)

    def beside(sent, move):
        work = works.get(steps[0])
        steps[0] += 1
        if work is None:
            return move(sent)
        sent, held = lax.optimization_barrier((sent, done.copy()))
        done.update(held)
        got = move(sent)
        gave = work(done)
        got, gave = lax.optimization_barrier((got, gave))
        done.update(gave)
        return got

    def fold(x, parts, dtype):
        folded, = call(fold_kernel, 0, 1, (struct((parts,) + x.shape[1:], dtype),), (), 0, 1 << 19)(x)
        return folded

    def across(sent):
        return swap(sent, FIRST)

    x = beside(send, across)
    x = (done["keep"] + x).astype(BF16)
    parts = len(plane[0])
    x = beside(x.reshape(parts, x.shape[0] // parts, CH), scatter(plane))
    x = beside(fold(x, len(ring[0]), BF16), scatter(ring))
    x = beside(fold(x, parts, BF16), scatter(plane)).reshape(-1, CH)
    out = struct(x.shape, F32)
    grads = call(finish_kernel, 1, 2, (out, out))(me.reshape(1), x, beside(x, across))
    return grads, done


def local(inputs, kernel_one, kernel_two, cotangent, edge_codes, corner_codes):
    count = lax.axis_size(AXES)
    width = lax.axis_size("face") // GRID_ROWS * lax.axis_size("sub")
    scale = 1.0 / math.sqrt(count * SIDE * SIDE)
    me = lax.axis_index(AXES).astype(jnp.int32).reshape(1)
    tables = (me, jnp.transpose(edge_codes, (1, 2, 0)), jnp.transpose(corner_codes, (1, 2, 0)))
    fields = inputs.reshape(BLOCK)
    upstream = cotangent.reshape(BLOCK)
    message = struct((VROWS, CH))
    own = struct((STRIPS, CH))
    weights = struct(WEIGHTS)
    block = struct(BLOCK)
    taps = struct((3, 3, CH, CH))
    copies = struct(COPIES)
    wide = struct(BLOCK, F32)
    sides = (4, SIDE, CH)
    strips = pltpu.VMEM(sides, F32)
    vertical_pair = pltpu.VMEM((VROWS, CH), BF16)
    column = pltpu.VMEM((SIDE, CH), F32)
    conv_flops = 2 * SIDE * SIDE * 9 * CH * CH

    va, vb, hp, hm, upstream = call(
        lambda *refs: pack_kernel(count, width, *refs), 3, 2, (message, message, own, own, block),
        [strips, strips, vertical_pair, vertical_pair],
    )(*tables, fields, upstream)
    va, vb, token = lax.optimization_barrier((va, vb, me))
    va, vb = both_ways(va, vb, width)
    in_two, up_copies, grad = call(back_kernel, 1, 2, (weights, copies, wide), (), conv_flops)(
        token, kernel_two, upstream
    )
    va, vb, in_two, up_copies, grad, token = lax.optimization_barrier(
        (va, vb, in_two, up_copies, grad, token)
    )

    def relay(token, va, vb, hp, hm):
        return call(
            lambda *refs: relay_kernel(width, *refs), 1, 4, (message, message, message, message), (), 0, 1 << 18
        )(token, va, vb, hp, hm)

    vp, vm, ha, hb = relay(token, va, vb, hp, hm)
    ha, hb, token = lax.optimization_barrier((ha, hb, token))
    ha, hb = both_ways(ha, hb, 1)
    fwd_one, field_copies, pre = call(fore_kernel, 1, 2, (weights, copies, wide), (), conv_flops)(
        token, kernel_one, fields
    )
    hidden, grad_pre, va2, vb2, hp2, hm2, fore, back, pieces, corners, hp, hm = call(
        lambda *refs: middle_kernel(count, width, *refs), 3, 8,
        (
            block, block, message, message, own, own, struct(sides, F32), struct(sides, F32),
            struct((4, SIDE, 3 * CH)), struct((4, 16, CH)),
            message, message,
        ),
        [strips, strips, vertical_pair, vertical_pair], conv_flops,
    )(*tables, vp, vm, ha, hb, fwd_one, in_two, pre, grad)
    hidden, grad_pre, va2, vb2, token = lax.optimization_barrier((hidden, grad_pre, va2, vb2, token))
    def half(kept, token):
        got, = call(
            lambda me, *refs: sums_kernel(count, width, scale, kept, me, *refs), 3, 12,
            (struct((9 * CH, CH), F32),), [pltpu.VMEM((2 * CH, 12 * CH), F32)], conv_flops,
        )(
            token, *tables[1:], vp, vm, hp, hm, hidden, grad_pre, field_copies, up_copies,
            fore, back, pieces, corners,
        )
        return got

    def first_work(done):
        va, vb = both_ways(done["va"], done["vb"], width)
        return dict(keep=half(True, done["token"]), va=va, vb=vb)

    late = {}

    def second_work(done):
        vp, vm, ha, hb = relay(done["token"], done["va"], done["vb"], hp2, hm2)
        ha, hb = both_ways(ha, hb, 1)
        late.update(ha=ha, hb=hb)
        return dict(vp=vp, vm=vm)

    def third_work(done):
        hp, hm = call(name_kernel, 1, 2, (message, message), (), 0, 1 << 18)(
            done["token"], late["ha"], late["hb"]
        )
        in_one, fwd_two = call(weights_kernel, 1, 2, (weights, weights))(
            done["token"], kernel_one, kernel_two
        )
        outputs, = call(
            outputs_kernel, 0, 6, (block,), [pltpu.VMEM(COPIES, BF16), column, column], conv_flops
        )(hidden, done["vp"], done["vm"], hp, hm, fwd_two)
        grad_fields, = call(
            lambda *refs: grads_kernel(count, width, *refs), 3, 6, (block,),
            [pltpu.VMEM(COPIES, BF16), strips], conv_flops,
        )(*tables, done["vp"], done["vm"], hp, hm, grad_pre, in_one)
        return dict(outputs=outputs, grad_fields=grad_fields)

    grads, done = total(
        half(False, token), dict(va=va2, vb=vb2, token=token),
        {0: first_work, 1: second_work, 2: third_work},
    )
    shape = (1, 1, SIDE, SIDE, CH)
    return (
        done["outputs"].reshape(shape), done["grad_fields"].reshape(shape),
        grads[0].reshape(taps.shape), grads[1].reshape(taps.shape),
    )


def solution(mesh):
    block = P("face", "sub", None, None, None)
    return jax.shard_map(
        local,
        mesh=mesh,
        in_specs=(block, P(), P(), block, P(), P()),
        out_specs=(block, block, P(), P()),
        check_vma=False,
    )
```
